32 devices in a mesh: blk: 2 (over core), smp: 16 (over z, y, x).
Axes of the slice: x: 2, y: 2, z: 4, core: 2. Of those that a mesh axis runs over, the one named last changes fastest.
Arguments:
- genotypes: bfloat16 [2, 16384, 2048], P('blk', 'smp'), may hold values from -2 to 10, as said below
- sizes: int32 [2], P('blk'), may hold values from 1024 to 2048, as said below
- start: float32 [2, 2048, 256], P('blk', 'smp'), may hold values from -6 to 6
Outputs:
- basis: float32 [2, 2048, 256], P('blk', 'smp')
- scaled: float32 [2, 256, 256], P('blk')
The draws below stay inside these ranges and needn't reach their ends.
Inputs may be any that keep to these rules, and one draw needn't show every extreme that they name: `sizes`: at least one block has exactly 2048 SNPs. `genotypes`: each column is a standardized count of 0, 1 or 2 alleles; columns at or past a block's size hold values that the block does not use.
All inputs are finite; a program needn't handle non-finite values.
Results may differ from the reference program's by a relative error of at most 0.0003.
Values may be sent and summed in bfloat16 or wider, within the bound.
No kernel may reach another device: no remote copies, remote signals or barrier semaphores. Data moves between devices by JAX's collectives and lax.ppermute only.
A program may use at most 128 MiB of HBM per device.

```python
import jax
import jax.numpy as jnp
from jax import lax

CAP = 2048
K = 256
ITERS = 2
SAMPLES = 16384
NBLK = 2


def haplotype(key, freqs):
    first, second = jax.random.split(key)
    latent = jax.random.uniform(first, (NBLK, SAMPLES, CAP), jnp.float32)
    fresh = jax.random.randint(second, (NBLK, SAMPLES, CAP), 0, 10, jnp.int32) == 0
    places = lax.broadcasted_iota(jnp.int32, (NBLK, SAMPLES, CAP), 2)
    breaks = jnp.logical_or(fresh, places == 0)
    anchor = lax.cummax(jnp.where(breaks, places, jnp.int32(0)), axis=2)
    copied = jnp.take_along_axis(latent, anchor, axis=2)
    return (copied < freqs).astype(jnp.float32)


def draw_genotypes(key, part):
    first, second, third = jax.random.split(jax.random.fold_in(key, 11), 3)
    freqs = jax.random.uniform(first, (NBLK, 1, CAP), jnp.float32, 0.05, 0.5)
    dosage = haplotype(second, freqs) + haplotype(third, freqs)
    scaled = (dosage - 2.0 * freqs) / jnp.sqrt(2.0 * freqs * (1.0 - freqs))
    return scaled.astype(jnp.bfloat16)


def draw_sizes(key, part):
    first, second = jax.random.split(jax.random.fold_in(key, 7))
    counts = jax.random.randint(first, (NBLK,), CAP // 2, CAP, jnp.int32)
    chosen = jax.random.randint(second, (), 0, NBLK, jnp.int32)
    places = jnp.arange(NBLK, dtype=jnp.int32)
    return jnp.where(places == chosen, jnp.int32(CAP), counts).astype(jnp.int32)


def block_scale(own_key, dims, shards, least, largest):
    gain, own = 1.0, jax.random.fold_in(own_key, 6)
    for dim, shards_of in shards:
        draws = jnp.exp(jax.random.uniform(jax.random.fold_in(own, dim), (shards_of,), jnp.float32, least / len(shards), largest / len(shards)))
        gain = gain * jnp.repeat(draws, dims[dim] // shards_of).reshape([-1 if axis == dim else 1 for axis in range(len(dims))])
    return gain


def noise(rng, shape, spread, limit, shards=(), kind=jnp.bfloat16):
    array = jax.random.normal(rng, shape, jnp.float32) * spread
    if len(shards) > 0:
        array = block_scale(rng, shape, shards, -0.22, 0.18) * array
    return jnp.clip(array, min=-limit, max=limit).astype(kind)


def setup_inputs(seed: int = 0) -> dict:
    key_list = jax.random.split(jax.random.key(seed), 4)
    return {
        "genotypes": draw_genotypes(jax.random.fold_in(key_list[3], 71), 0),
        "sizes": draw_sizes(jax.random.fold_in(key_list[3], 71), 0),
        "start": noise(key_list[2], (NBLK, CAP, K), 1.0, 6.0, ((0, 2), (1, 16)), jnp.float32),
    }


def one_block(operands):
    dosages, count, vectors = operands
    live = (jnp.arange(CAP, dtype=jnp.int32) < count).astype(jnp.bfloat16)
    masked = dosages * live[None, :]
    gram = jnp.dot(masked.T.astype(jnp.float32), masked.astype(jnp.float32), preferred_element_type=jnp.float32) / SAMPLES
    for repeat in range(ITERS):
        image = jnp.dot(gram.astype(jnp.float32), vectors.astype(jnp.float32), precision=lax.Precision.HIGHEST, preferred_element_type=jnp.float32)
        inner = jnp.dot(image.T.astype(jnp.float32), image.astype(jnp.float32), precision=lax.Precision.HIGHEST, preferred_element_type=jnp.float32)
        lower = jnp.linalg.cholesky(inner)
        vectors = lax.linalg.triangular_solve(lower, image, left_side=False, lower=True, transpose_a=True)
    image = jnp.dot(gram.astype(jnp.float32), vectors.astype(jnp.float32), precision=lax.Precision.HIGHEST, preferred_element_type=jnp.float32)
    rayleigh = jnp.dot(vectors.T.astype(jnp.float32), image.astype(jnp.float32), precision=lax.Precision.HIGHEST, preferred_element_type=jnp.float32)
    return (vectors, rayleigh)

def reference(genotypes, sizes, start):
    vectors, rayleigh = lax.map(one_block, (genotypes, sizes, start))
    total = jnp.sum(jnp.trace(rayleigh, axis1=1, axis2=2))
    scaled = rayleigh * (NBLK * K) / total
    basis = vectors * jnp.sqrt(jnp.float32(CAP))
    return (basis, scaled)
```

```python
import functools
import math

import jax
import jax.numpy as jnp
from jax import lax
from jax.experimental import pallas as pl
from jax.experimental.pallas import tpu as pltpu
from jax.sharding import PartitionSpec as P

LANES = 128
SUBLANES = 8
VMEM_LIMIT = 48 * 1024 * 1024
HIGHEST = lax.Precision.HIGHEST


def stage_bits(groups, flip):
    count = groups.bit_length() - 1
    bits = list(range(count))
    if flip and count >= 2:
        bits[0], bits[1] = bits[1], bits[0]
    stages = [[bit] for bit in bits[:2]]
    rest = bits[2:]
    while rest:
        stages.append(rest[:2])
        rest = rest[2:]
    return stages


def offsets(bits):
    found = [0]
    for bit in bits:
        found = found + [value ^ (1 << bit) for value in found]
    return found


def relative_order(stages):
    order = [0]
    for bits in reversed(stages):
        order = [high ^ low for high in offsets(bits) for low in order]
    return order


def exchange(value, groups, offset):
    return lax.ppermute(value, "smp", [(device, device ^ offset) for device in range(groups)])


def reduce_chunks(keep, send, groups, stages):
    total = keep + exchange(send, groups, 1 << stages[0][0])
    for bits in stages[1:]:
        spans = offsets(bits)
        width = total.shape[0] // len(spans)
        arrived = [
            exchange(total[place * width : (place + 1) * width], groups, span)
            for place, span in enumerate(spans)
            if place > 0
        ]
        total = total[:width]
        for part in arrived:
            total = total + part
    return total


def gather_chunks(chunk, groups, stages):
    held = chunk
    for bits in reversed(stages[1:]):
        held = jnp.concatenate([held] + [exchange(held, groups, span) for span in offsets(bits)[1:]], axis=0)
    return held, exchange(held, groups, 1 << stages[0][0])


def split_pieces(value, pieces):
    parts = []
    rest = value
    for piece in range(pieces):
        part = rest.astype(jnp.bfloat16)
        parts.append(part)
        if piece + 1 < pieces:
            rest = rest - part.astype(jnp.float32)
    return parts


def apply_kernel(
    order, pieces, scale, place_ref, size_ref, near_ref, far_ref, rows_ref, keep_ref, send_ref, split_ref, total_ref
):
    step = pl.program_id(0)
    half, width = near_ref.shape[1:]
    me = place_ref[0]

    def columns(offset):
        return pl.ds(pl.multiple_of(jnp.bitwise_xor(me, offset) * width, width), width)

    middle = len(order) // 2

    @pl.when(step == 0)
    def _():
        for place, offset in enumerate(order):
            value = near_ref[place] if place < middle else far_ref[place - middle]
            for piece, part in enumerate(split_pieces(value, pieces)):
                split_ref[pl.ds(piece * half, half), columns(offset)] = part

    rows = rows_ref[...]
    image = lax.dot_general(
        split_ref[...], rows, (((1,), (1,)), ((), ())), preferred_element_type=jnp.float32
    )
    image = sum(image[piece * half : (piece + 1) * half] for piece in range(pieces))
    back = jnp.dot(
        jnp.concatenate(split_pieces(image, pieces), axis=0), rows, preferred_element_type=jnp.float32
    )
    back = sum(back[piece * half : (piece + 1) * half] for piece in range(pieces))

    @pl.when(step == 0)
    def _():
        total_ref[...] = back

    @pl.when(step > 0)
    def _():
        total_ref[...] += back

    @pl.when(step == pl.num_programs(0) - 1)
    def _():
        for place, offset in enumerate(order):
            first = jnp.bitwise_xor(me, offset) * width
            live = first + lax.broadcasted_iota(jnp.int32, (half, width), 1) < size_ref[0]
            value = jnp.where(live, total_ref[:, columns(offset)] * scale, 0.0)
            if place < middle:
                keep_ref[place] = value
            else:
                send_ref[place - middle] = value


def apply_samples(genotypes, size, me, near, far, order, pieces, scale):
    samples, cap = genotypes.shape
    count, half, width = near.shape
    block = min(256, samples)
    whole = pl.BlockSpec((count, half, width), lambda step: (0, 0, 0))
    scalar = pl.BlockSpec(memory_space=pltpu.SMEM)
    out = jax.ShapeDtypeStruct(near.shape, jnp.float32)
    return pl.pallas_call(
        functools.partial(apply_kernel, order, pieces, scale),
        grid=(samples // block,),
        in_specs=[scalar, scalar, whole, whole, pl.BlockSpec((block, cap), lambda step: (step, 0))],
        out_specs=[whole, whole],
        out_shape=[out, out],
        scratch_shapes=[
            pltpu.VMEM((pieces * half, cap), jnp.bfloat16),
            pltpu.VMEM((half, cap), jnp.float32),
        ],
        compiler_params=pltpu.CompilerParams(vmem_limit_bytes=VMEM_LIMIT),
        cost_estimate=pl.CostEstimate(
            flops=4 * samples * cap * half * pieces,
            bytes_accessed=2 * samples * cap + 16 * half * cap,
            transcendentals=0,
        ),
    )(me, size, near, far, genotypes)


def full_rows(place_ref, orders, pairs, target_ref):
    me = place_ref[0]
    for chain, (order, (near_ref, far_ref)) in enumerate(zip(orders, pairs)):
        half, width = near_ref.shape[1:]
        middle = len(order) // 2
        for place, offset in enumerate(order):
            first = pl.multiple_of(jnp.bitwise_xor(me, offset) * width, width)
            value = near_ref[place] if place < middle else far_ref[place - middle]
            target_ref[pl.ds(chain * half, half), pl.ds(first, width)] = value


def lane_splat(tile, lane):
    return jnp.broadcast_to(tile[:, lane : lane + 1], (SUBLANES, LANES))


def row_splat(tile, row):
    return jnp.broadcast_to(tile[row : row + 1, :], (SUBLANES, LANES))


def inverse_factor(work_ref, size, panel):
    tiles = 2 * size // LANES
    below = lax.broadcasted_iota(jnp.int32, (SUBLANES, LANES), 0)
    groups = panel // SUBLANES
    for top in range(0, size, panel):
        active = [
            tile
            for tile in range(tiles)
            if (top // LANES <= tile < size // LANES)
            or (size // LANES <= tile <= size // LANES + (top + panel - 1) // LANES)
        ]
        rows = [
            {
                tile: work_ref[top + SUBLANES * group : top + SUBLANES * (group + 1), tile * LANES : (tile + 1) * LANES]
                for tile in active
            }
            for group in range(groups)
        ]
        for block in range(groups):
            base = top + SUBLANES * block
            columns = {
                group: [lane_splat(rows[group][base // LANES], base % LANES + lane) for lane in range(SUBLANES)]
                for group in range(block, groups)
            }
            for step in range(SUBLANES):
                pivot = row_splat(columns[block][step], step)
                root = lax.rsqrt(pivot)
                root = root * (1.5 - 0.5 * pivot * root * root)
                factor = {group: columns[group][step] * root for group in range(block, groups)}
                for later in range(step + 1, SUBLANES):
                    weight = row_splat(factor[block], later)
                    for group in range(block, groups):
                        columns[group][later] = columns[group][later] - factor[group] * weight
                lower = jnp.where(below > step, factor[block], 0.0)
                for tile in active:
                    line = row_splat(rows[block][tile], step) * root
                    rows[block][tile] = jnp.where(
                        below == step, line, rows[block][tile] - lower * line
                    )
                    for group in range(block + 1, groups):
                        rows[group][tile] = rows[group][tile] - factor[group] * line
        for group in range(groups):
            for tile in active:
                work_ref[top + SUBLANES * group : top + SUBLANES * (group + 1), tile * LANES : (tile + 1) * LANES] = rows[
                    group
                ][tile]
        rest = top + panel
        if rest < size:
            first, last = active[0] * LANES, (active[-1] + 1) * LANES
            lines = work_ref[top:rest, first:last]
            weights = work_ref[top:rest, rest // LANES * LANES : size].T[rest % LANES :, :]
            work_ref[rest:, first:last] -= jnp.dot(
                weights, lines, precision=HIGHEST, preferred_element_type=jnp.float32
            )


def start_factor(work_ref, inner):
    size = inner.shape[0]
    work_ref[:, :size] = inner
    row = lax.broadcasted_iota(jnp.int32, (size, size), 0)
    column = lax.broadcasted_iota(jnp.int32, (size, size), 1)
    work_ref[:, size:] = jnp.where(row == column, 1.0, 0.0)


def finish_factor(work_ref):
    size = work_ref.shape[0]
    row = lax.broadcasted_iota(jnp.int32, (size, size), 0)
    column = lax.broadcasted_iota(jnp.int32, (size, size), 1)
    return jnp.where(row >= column, work_ref[:, size:], 0.0)


def rows_inner(value):
    return lax.dot_general(
        value, value, (((1,), (1,)), ((), ())), precision=HIGHEST, preferred_element_type=jnp.float32
    )


def factor_kernel(orders, place_ref, *refs):
    pairs = list(zip(refs[: 2 * len(orders) : 2], refs[1 : 2 * len(orders) : 2]))
    out_ref, full_ref, work_ref = refs[2 * len(orders) :]
    full_rows(place_ref, orders, pairs, full_ref)
    start_factor(work_ref, rows_inner(full_ref[...]))
    inverse_factor(work_ref, work_ref.shape[0], 32)
    out_ref[...] = finish_factor(work_ref)


def first_factor(me, pairs, orders, cap):
    size = sum(near.shape[1] for near, far in pairs)
    return pl.pallas_call(
        functools.partial(factor_kernel, orders),
        in_specs=[pl.BlockSpec(memory_space=pltpu.SMEM)]
        + [pl.BlockSpec(memory_space=pltpu.VMEM)] * (2 * len(pairs)),
        out_specs=pl.BlockSpec(memory_space=pltpu.VMEM),
        out_shape=jax.ShapeDtypeStruct((size, size), jnp.float32),
        scratch_shapes=[pltpu.VMEM((size, cap), jnp.float32), pltpu.VMEM((size, 2 * size), jnp.float32)],
        compiler_params=pltpu.CompilerParams(vmem_limit_bytes=VMEM_LIMIT),
    )(me, *[ref for pair in pairs for ref in pair])


def project_kernel(
    orders, out_orders, pieces, place_ref, *refs
):
    count = 2 * len(orders)
    pairs = list(zip(refs[:count:2], refs[1:count:2]))
    first_ref, rows_ref, image_ref, inner_ref = refs[count : count + 4]
    outs = refs[count + 4 : count + 8]
    full_ref, split_ref, cross_ref = refs[count + 8 :]
    step = pl.program_id(0)
    size = first_ref.shape[0]

    @pl.when(step == 0)
    def _():
        full_rows(place_ref, orders, pairs, full_ref)
        image = jnp.dot(
            first_ref[...], full_ref[...], precision=HIGHEST, preferred_element_type=jnp.float32
        )
        image_ref[...] = image
        inner_ref[...] = rows_inner(image)
        for piece, part in enumerate(split_pieces(image, pieces)):
            split_ref[pl.ds(piece * size, size), :] = part
        cross_ref[...] = jnp.zeros_like(cross_ref)

    sampled = lax.dot_general(
        split_ref[...], rows_ref[...], (((1,), (1,)), ((), ())), preferred_element_type=jnp.float32
    )
    sampled = sum(sampled[piece * size : (piece + 1) * size] for piece in range(pieces))
    cross_ref[...] += rows_inner(sampled)

    @pl.when(step == pl.num_programs(0) - 1)
    def _():
        me = place_ref[0]
        for chain, order in enumerate(out_orders):
            keep_ref, send_ref = outs[2 * chain : 2 * chain + 2]
            height, width = keep_ref.shape[1:]
            middle = len(order) // 2
            for place, offset in enumerate(order):
                first = pl.multiple_of(jnp.bitwise_xor(me, offset) * height, height)
                value = cross_ref[pl.ds(first, height), chain * width : (chain + 1) * width]
                if place < middle:
                    keep_ref[place] = value
                else:
                    send_ref[place - middle] = value


def project(genotypes, me, pairs, orders, out_orders, first, pieces):
    samples, cap = genotypes.shape
    size = first.shape[0]
    block = min(256, samples)
    scalar = pl.BlockSpec(memory_space=pltpu.SMEM)

    def whole(shape):
        return pl.BlockSpec(shape, lambda step: (0,) * len(shape))

    height, width = size // len(out_orders[0]), size // len(out_orders)
    part = (len(out_orders[0]) // 2, height, width)
    return pl.pallas_call(
        functools.partial(project_kernel, orders, out_orders, pieces),
        grid=(samples // block,),
        in_specs=[scalar]
        + [whole(near.shape) for near, far in pairs for _ in range(2)]
        + [whole((size, size)), pl.BlockSpec((block, cap), lambda step: (step, 0))],
        out_specs=[whole((size, cap)), whole((size, size))] + [whole(part)] * (2 * len(out_orders)),
        out_shape=[
            jax.ShapeDtypeStruct((size, cap), jnp.float32),
            jax.ShapeDtypeStruct((size, size), jnp.float32),
        ]
        + [jax.ShapeDtypeStruct(part, jnp.float32)] * (2 * len(out_orders)),
        scratch_shapes=[
            pltpu.VMEM((size, cap), jnp.float32),
            pltpu.VMEM((pieces * size, cap), jnp.bfloat16),
            pltpu.VMEM((size, size), jnp.float32),
        ],
        compiler_params=pltpu.CompilerParams(vmem_limit_bytes=VMEM_LIMIT),
    )(me, *[ref for pair in pairs for ref in pair], first, genotypes)


def second_kernel(inner_ref, out_ref, work_ref):
    start_factor(work_ref, inner_ref[...])
    inverse_factor(work_ref, work_ref.shape[0], 32)
    out_ref[...] = finish_factor(work_ref)


def second_factor(inner):
    size = inner.shape[0]
    return pl.pallas_call(
        second_kernel,
        in_specs=[pl.BlockSpec(memory_space=pltpu.VMEM)],
        out_specs=pl.BlockSpec(memory_space=pltpu.VMEM),
        out_shape=jax.ShapeDtypeStruct((size, size), jnp.float32),
        scratch_shapes=[pltpu.VMEM((size, 2 * size), jnp.float32)],
        compiler_params=pltpu.CompilerParams(vmem_limit_bytes=VMEM_LIMIT),
    )(inner)


def to_natural(pair, order, me):
    places = jnp.argsort(jnp.array(order, jnp.int32))
    mine = jnp.bitwise_xor(jnp.arange(len(order), dtype=jnp.int32), me)
    stacked = jnp.concatenate(pair, axis=0)[places][mine]
    rows = jnp.transpose(stacked, (1, 0, 2)).reshape(1, stacked.shape[1], -1)
    return tuple(jnp.split(rows, 2, axis=2))


def to_relative(pair, order, me, width):
    rows = jnp.concatenate(pair, axis=2)[0]
    chunks = jnp.transpose(rows.reshape(rows.shape[0], -1, width), (1, 0, 2))
    chunks = chunks[jnp.bitwise_xor(jnp.array(order, jnp.int32), me)]
    return tuple(jnp.split(chunks, 2, axis=0))


def stacked_rows(pair, order, me):
    places = jnp.argsort(jnp.array(order, jnp.int32))
    mine = jnp.bitwise_xor(jnp.arange(len(order), dtype=jnp.int32), me)
    stacked = jnp.concatenate(pair, axis=0)[places][mine]
    return stacked.reshape(-1, stacked.shape[2])


def cut_rows(pair, order, me, height):
    rows = jnp.concatenate(pair, axis=0).reshape(-1, height, pair[0].shape[2])
    return tuple(jnp.split(rows[jnp.bitwise_xor(jnp.array(order, jnp.int32), me)], 2, axis=0))


def body(genotypes, sizes, start):
    groups = lax.axis_size("smp")
    dosages = genotypes[0]
    samples, cap = dosages.shape
    width, size = start.shape[1:]
    half = size // 2
    scale = 1.0 / (samples * groups)
    me = lax.axis_index("smp")
    where = me.reshape(1).astype(jnp.int32)
    chains = [stage_bits(groups, flip) for flip in (False, True)]
    orders = [relative_order(stages) for stages in chains]

    first_row = me * width
    live = first_row + lax.broadcasted_iota(jnp.int32, (width, size), 0) < sizes[0]
    columns = jnp.where(live, start[0], 0.0).T
    chunks = [columns[chain * half : (chain + 1) * half][None] for chain in range(2)]

    aligned = width % LANES == 0 and (size // groups) % SUBLANES == 0
    plain = [[0, 1]] * 2

    def gather(chunk, chain):
        pair = gather_chunks(chunk, groups, chains[chain])
        return pair if aligned else to_natural(pair, orders[chain], me)

    place = where if aligned else jnp.zeros_like(where)
    laid = orders if aligned else plain

    def apply(chunk, chain):
        pair = gather(chunk, chain)
        out = apply_samples(dosages, sizes, place, *pair, laid[chain], 3, scale)
        if not aligned:
            out = to_relative(out, orders[chain], me, width)
        return pair, reduce_chunks(*out, groups, chains[chain])

    images = [apply(chunks[chain], chain)[1] for chain in range(2)]
    done = [apply(images[chain], chain) for chain in range(2)]
    first = first_factor(place, [pair for pair, _ in done], laid, cap)
    pairs = [gather(done[chain][1], chain) for chain in range(2)]
    image, inner, *cross = project(dosages, place, pairs, laid, laid, first, 3)
    crossed = []
    for chain in range(2):
        part = tuple(cross[2 * chain : 2 * chain + 2])
        if not aligned:
            part = cut_rows(part, orders[chain], me, size // groups)
        part = gather_chunks(reduce_chunks(*part, groups, chains[chain]), groups, chains[chain])
        crossed.append(stacked_rows(part, orders[chain], me))
    crossed = jnp.concatenate(crossed, axis=1)
    second = second_factor(inner)
    own = lax.dynamic_slice(image, (0, first_row), (size, width))
    basis = jnp.dot(second, own, precision=HIGHEST, preferred_element_type=jnp.float32).T * math.sqrt(cap)
    rayleigh = jnp.dot(
        jnp.dot(second, crossed, precision=HIGHEST, preferred_element_type=jnp.float32),
        second.T,
        precision=HIGHEST,
        preferred_element_type=jnp.float32,
    ) * scale
    blocks = lax.axis_size("blk")
    partial = jnp.broadcast_to(jnp.trace(rayleigh), (SUBLANES, LANES))
    total = partial
    for shift in range(1, blocks):
        total = total + lax.ppermute(partial, "blk", [(block, (block + shift) % blocks) for block in range(blocks)])
    scaled = rayleigh * (genotypes.shape[0] * blocks * size) / total[0, 0]
    return basis[None], scaled[None]


def solution(mesh):
    return jax.shard_map(
        body,
        mesh=mesh,
        in_specs=(P("blk", "smp", None), P("blk"), P("blk", "smp", None)),
        out_specs=(P("blk", "smp", None), P("blk", None, None)),
        check_vma=False,
    )
```

```python
import functools
import math

import jax
import jax.numpy as jnp
from jax import lax
from jax.experimental import pallas as pl
from jax.experimental.pallas import tpu as pltpu
from jax.sharding import PartitionSpec as P

LANES = 128
SUBLANES = 8
BLOCK = 1024
PIECES = 2
VMEM_LIMIT = 48 * 1024 * 1024
HIGHEST = lax.Precision.HIGHEST
FACTOR_COST = pl.CostEstimate(flops=12_000_000_000, bytes_accessed=4 << 20, transcendentals=0)


def stage_bits(groups, flip):
    count = groups.bit_length() - 1
    bits = list(range(count))
    if flip and count >= 2:
        bits[0], bits[1] = bits[1], bits[0]
    stages = [[bit] for bit in bits[:2]]
    rest = bits[2:]
    while rest:
        stages.append(rest[:2])
        rest = rest[2:]
    return stages


def offsets(bits):
    found = [0]
    for bit in bits:
        found = found + [value ^ (1 << bit) for value in found]
    return found


def relative_order(stages):
    order = [0]
    for bits in reversed(stages):
        order = [high ^ low for high in offsets(bits) for low in order]
    return order


def exchange(value, groups, offset):
    return lax.ppermute(value, "smp", [(device, device ^ offset) for device in range(groups)])


def reduce_chunks(pairs, groups, chains):
    totals = [
        keep + exchange(send, groups, 1 << stages[0][0]) for (keep, send), stages in zip(pairs, chains)
    ]
    for depth in range(1, len(chains[0])):
        choices = [offsets(stages[depth]) for stages in chains]
        width = totals[0].shape[0] // len(choices[0])
        kept = [total[:width] for total in totals]
        for place in range(1, len(choices[0])):
            parts = [total[place * width : (place + 1) * width] for total in totals]
            spans = [spans[place] for spans in choices]
            if len(set(spans)) == 1:
                arrived = jnp.split(exchange(jnp.concatenate(parts, axis=0), groups, spans[0]), len(parts), axis=0)
            else:
                arrived = [exchange(part, groups, span) for part, span in zip(parts, spans)]
            kept = [total + part for total, part in zip(kept, arrived)]
        totals = kept
    return jnp.concatenate(totals, axis=0)


def gather_chunks(chunks, groups, chains):
    held = jnp.split(chunks, len(chains), axis=0)
    for depth in reversed(range(1, len(chains[0]))):
        choices = [offsets(stages[depth]) for stages in chains]
        if all(spans == choices[0] for spans in choices):
            whole = jnp.concatenate(held, axis=0) if depth + 1 < len(chains[0]) else chunks
            arrived = [jnp.split(exchange(whole, groups, span), len(chains), axis=0) for span in choices[0][1:]]
            held = [jnp.concatenate([own] + [part[chain] for part in arrived], axis=0) for chain, own in enumerate(held)]
        else:
            held = [
                jnp.concatenate([own] + [exchange(own, groups, span) for span in spans[1:]], axis=0)
                for own, spans in zip(held, choices)
            ]
    return [(own, exchange(own, groups, 1 << stages[0][0])) for own, stages in zip(held, chains)]


def pair_sum(parts):
    while len(parts) > 1:
        parts = [left + right for left, right in zip(parts[::2], parts[1::2])]
    return parts[0]


def sum_quarters(quarters, groups):
    count = groups.bit_length() - 1
    stages = [list(range(count))[place : place + 2] for place in range(0, count, 2)]
    spans = offsets(stages[0])
    total = pair_sum([quarters[0]] + [exchange(part, groups, span) for part, span in zip(quarters[1:], spans[1:])])
    for bits in stages[1:]:
        total = pair_sum([total] + [exchange(total, groups, span) for span in offsets(bits)[1:]])
    return [total] + [exchange(total, groups, span) for span in spans[1:]]


def split_pieces(value, pieces):
    parts = []
    rest = value
    for piece in range(pieces):
        part = rest.astype(jnp.bfloat16)
        parts.append(part)
        if piece + 1 < pieces:
            rest = rest - part.astype(jnp.float32)
    return parts


def apply_kernel(
    order, pieces, scale, place_ref, size_ref, near_ref, far_ref, rows_ref, keep_ref, send_ref, split_ref, total_ref
):
    step = pl.program_id(0)
    half, width = near_ref.shape[1:]
    me = place_ref[0]

    def columns(offset):
        return pl.ds(pl.multiple_of(jnp.bitwise_xor(me, offset) * width, width), width)

    middle = len(order) // 2

    @pl.when(step == 0)
    def _():
        for place, offset in enumerate(order):
            value = near_ref[place] if place < middle else far_ref[place - middle]
            for piece, part in enumerate(split_pieces(value, pieces)):
                split_ref[pl.ds(piece * half, half), columns(offset)] = part

    rows = rows_ref[...]
    image = lax.dot_general(
        split_ref[...], rows, (((1,), (1,)), ((), ())), preferred_element_type=jnp.float32
    )
    image = sum(image[piece * half : (piece + 1) * half] for piece in range(pieces))
    back = jnp.dot(
        jnp.concatenate(split_pieces(image, pieces), axis=0), rows, preferred_element_type=jnp.float32
    )
    back = sum(back[piece * half : (piece + 1) * half] for piece in range(pieces))

    @pl.when(step == 0)
    def _():
        total_ref[...] = back

    @pl.when(step > 0)
    def _():
        total_ref[...] += back

    @pl.when(step == pl.num_programs(0) - 1)
    def _():
        for place, offset in enumerate(order):
            first = jnp.bitwise_xor(me, offset) * width
            live = first + lax.broadcasted_iota(jnp.int32, (half, width), 1) < size_ref[0]
            value = jnp.where(live, total_ref[:, columns(offset)] * scale, 0.0)
            if place < middle:
                keep_ref[place] = value
            else:
                send_ref[place - middle] = value


def apply_samples(genotypes, size, me, near, far, order, pieces, scale):
    samples, cap = genotypes.shape
    count, half, width = near.shape
    block = min(BLOCK, samples)
    whole = pl.BlockSpec((count, half, width), lambda step: (0, 0, 0))
    scalar = pl.BlockSpec(memory_space=pltpu.SMEM)
    out = jax.ShapeDtypeStruct(near.shape, jnp.float32)
    return pl.pallas_call(
        functools.partial(apply_kernel, order, pieces, scale),
        grid=(samples // block,),
        in_specs=[scalar, scalar, whole, whole, pl.BlockSpec((block, cap), lambda step: (step, 0))],
        out_specs=[whole, whole],
        out_shape=[out, out],
        scratch_shapes=[
            pltpu.VMEM((pieces * half, cap), jnp.bfloat16),
            pltpu.VMEM((half, cap), jnp.float32),
        ],
        compiler_params=pltpu.CompilerParams(vmem_limit_bytes=VMEM_LIMIT),
        cost_estimate=pl.CostEstimate(
            flops=4 * samples * cap * half * pieces,
            bytes_accessed=2 * samples * cap + 16 * half * cap,
            transcendentals=0,
        ),
    )(me, size, near, far, genotypes)


def full_rows(place_ref, orders, pairs, target_ref):
    me = place_ref[0]
    for chain, (order, (near_ref, far_ref)) in enumerate(zip(orders, pairs)):
        half, width = near_ref.shape[1:]
        middle = len(order) // 2
        for place, offset in enumerate(order):
            first = pl.multiple_of(jnp.bitwise_xor(me, offset) * width, width)
            value = near_ref[place] if place < middle else far_ref[place - middle]
            target_ref[pl.ds(chain * half, half), pl.ds(first, width)] = value


def lane_splat(tile, lane):
    return jnp.broadcast_to(tile[:, lane : lane + 1], (SUBLANES, LANES))


def row_splat(tile, row):
    return jnp.broadcast_to(tile[row : row + 1, :], (SUBLANES, LANES))


def inverse_factor(work_ref, size, panel):
    tiles = 2 * size // LANES
    below = lax.broadcasted_iota(jnp.int32, (SUBLANES, LANES), 0)
    groups = panel // SUBLANES
    for top in range(0, size, panel):
        active = [
            tile
            for tile in range(tiles)
            if (top // LANES <= tile < size // LANES)
            or (size // LANES <= tile <= size // LANES + (top + panel - 1) // LANES)
        ]
        rows = [
            {
                tile: work_ref[top + SUBLANES * group : top + SUBLANES * (group + 1), tile * LANES : (tile + 1) * LANES]
                for tile in active
            }
            for group in range(groups)
        ]
        for block in range(groups):
            base = top + SUBLANES * block
            columns = {
                group: [lane_splat(rows[group][base // LANES], base % LANES + lane) for lane in range(SUBLANES)]
                for group in range(block, groups)
            }
            for step in range(SUBLANES):
                pivot = row_splat(columns[block][step], step)
                root = lax.rsqrt(pivot)
                root = root * (1.5 - 0.5 * pivot * root * root)
                factor = {group: columns[group][step] * root for group in range(block, groups)}
                for later in range(step + 1, SUBLANES):
                    weight = row_splat(factor[block], later)
                    for group in range(block, groups):
                        columns[group][later] = columns[group][later] - factor[group] * weight
                lower = jnp.where(below > step, factor[block], 0.0)
                for tile in active:
                    line = row_splat(rows[block][tile], step) * root
                    rows[block][tile] = jnp.where(
                        below == step, line, rows[block][tile] - lower * line
                    )
                    for group in range(block + 1, groups):
                        rows[group][tile] = rows[group][tile] - factor[group] * line
        for group in range(groups):
            for tile in active:
                work_ref[top + SUBLANES * group : top + SUBLANES * (group + 1), tile * LANES : (tile + 1) * LANES] = rows[
                    group
                ][tile]
        rest = top + panel
        if rest < size:
            first, last = active[0] * LANES, (active[-1] + 1) * LANES
            lines = work_ref[top:rest, first:last]
            weights = work_ref[top:rest, rest // LANES * LANES : size].T[rest % LANES :, :]
            work_ref[rest:, first:last] -= jnp.dot(
                weights, lines, precision=HIGHEST, preferred_element_type=jnp.float32
            )


def start_factor(work_ref, inner):
    size = inner.shape[0]
    work_ref[:, :size] = inner
    row = lax.broadcasted_iota(jnp.int32, (size, size), 0)
    column = lax.broadcasted_iota(jnp.int32, (size, size), 1)
    work_ref[:, size:] = jnp.where(row == column, 1.0, 0.0)


def finish_factor(work_ref):
    size = work_ref.shape[0]
    row = lax.broadcasted_iota(jnp.int32, (size, size), 0)
    column = lax.broadcasted_iota(jnp.int32, (size, size), 1)
    return jnp.where(row >= column, work_ref[:, size:], 0.0)


def rows_inner(value):
    return lax.dot_general(
        value, value, (((1,), (1,)), ((), ())), precision=HIGHEST, preferred_element_type=jnp.float32
    )


def factor_kernel(orders, place_ref, *refs):
    pairs = list(zip(refs[: 2 * len(orders) : 2], refs[1 : 2 * len(orders) : 2]))
    out_ref, full_ref, work_ref = refs[2 * len(orders) :]
    full_rows(place_ref, orders, pairs, full_ref)
    start_factor(work_ref, rows_inner(full_ref[...]))
    inverse_factor(work_ref, work_ref.shape[0], 32)
    out_ref[...] = finish_factor(work_ref)


def first_factor(me, pairs, orders, cap):
    size = sum(near.shape[1] for near, far in pairs)
    return pl.pallas_call(
        functools.partial(factor_kernel, orders),
        in_specs=[pl.BlockSpec(memory_space=pltpu.SMEM)]
        + [pl.BlockSpec(memory_space=pltpu.VMEM)] * (2 * len(pairs)),
        out_specs=pl.BlockSpec(memory_space=pltpu.VMEM),
        out_shape=jax.ShapeDtypeStruct((size, size), jnp.float32),
        scratch_shapes=[pltpu.VMEM((size, cap), jnp.float32), pltpu.VMEM((size, 2 * size), jnp.float32)],
        compiler_params=pltpu.CompilerParams(vmem_limit_bytes=VMEM_LIMIT),
        cost_estimate=FACTOR_COST,
    )(me, *[ref for pair in pairs for ref in pair])


def fold_symmetric(value, folded_ref, height):
    half = value.shape[0] // 2
    row = lax.broadcasted_iota(jnp.int32, (half, half), 0)
    column = lax.broadcasted_iota(jnp.int32, (half, half), 1)
    corner = value[half:, half:]
    both = jnp.where(row >= column, value[:half, :half], corner)
    diagonal = jnp.sum(jnp.where(row == column, corner, 0.0), axis=0, keepdims=True)
    quarter = half // 2
    for place in range(4):
        source = value[half:, :half] if place < 2 else both
        folded_ref[place, :quarter] = source[place % 2 * quarter : (place % 2 + 1) * quarter]
        folded_ref[place, quarter:] = jnp.broadcast_to(diagonal, (SUBLANES, half))


def unfold_symmetric(parts):
    quarter = parts[0].shape[0] - SUBLANES
    half = 2 * quarter
    row = lax.broadcasted_iota(jnp.int32, (half, half), 0)
    column = lax.broadcasted_iota(jnp.int32, (half, half), 1)
    left = jnp.concatenate([parts[0][:quarter], parts[1][:quarter]], axis=0)
    both = jnp.concatenate([parts[2][:quarter], parts[3][:quarter]], axis=0)
    turned = both.T
    corner = jnp.where(row == column, parts[3][quarter : quarter + 1], jnp.where(row < column, both, turned))
    upper = jnp.concatenate([jnp.where(row >= column, both, turned), left.T], axis=1)
    return jnp.concatenate([upper, jnp.concatenate([left, corner], axis=1)], axis=0)


def project_kernel(orders, pieces, aligned, quarter_ref, place_ref, *refs):
    count = 2 * len(orders)
    pairs = list(zip(refs[:count:2], refs[1:count:2]))
    first_ref, rows_ref, image_ref, inner_ref = refs[count : count + 4]
    outs = refs[count + 4 : count + 8]
    full_ref, split_ref, cross_ref, folded_ref = refs[count + 8 :]
    step = pl.program_id(0)
    size = first_ref.shape[0]

    @pl.when(step == 0)
    def _():
        full_rows(place_ref, orders, pairs, full_ref)
        image = jnp.dot(
            first_ref[...], full_ref[...], precision=HIGHEST, preferred_element_type=jnp.float32
        )
        inner_ref[...] = rows_inner(image)
        full_ref[...] = image
        if aligned:
            width = image_ref.shape[1]
            image_ref[...] = full_ref[:, pl.ds(pl.multiple_of(place_ref[0] * width, width), width)]
        else:
            image_ref[...] = image
        for piece, part in enumerate(split_pieces(image, pieces)):
            split_ref[pl.ds(piece * size, size), :] = part
        cross_ref[...] = jnp.zeros_like(cross_ref)

    sampled = lax.dot_general(
        split_ref[...], rows_ref[...], (((1,), (1,)), ((), ())), preferred_element_type=jnp.float32
    )
    sampled = sum(sampled[piece * size : (piece + 1) * size] for piece in range(pieces))
    cross_ref[...] += rows_inner(sampled)

    @pl.when(step == pl.num_programs(0) - 1)
    def _():
        fold_symmetric(cross_ref[...], folded_ref, size)
        for offset in range(4):
            outs[offset][...] = folded_ref[jnp.bitwise_xor(quarter_ref[0], offset)]


def project(genotypes, quarter, place, pairs, orders, first, pieces, aligned, width):
    samples, cap = genotypes.shape
    size = first.shape[0]
    block = min(BLOCK, samples)
    scalar = pl.BlockSpec(memory_space=pltpu.SMEM)

    def whole(shape):
        return pl.BlockSpec(shape, lambda step: (0,) * len(shape))

    own = (size, width if aligned else cap)
    part = (size // 4 + SUBLANES, size // 2)
    outs = [own, (size, size)] + [part] * 4
    return pl.pallas_call(
        functools.partial(project_kernel, orders, pieces, aligned),
        grid=(samples // block,),
        in_specs=[scalar, scalar]
        + [whole(near.shape) for near, far in pairs for _ in range(2)]
        + [whole((size, size)), pl.BlockSpec((block, cap), lambda step: (step, 0))],
        out_specs=[whole(shape) for shape in outs],
        out_shape=[jax.ShapeDtypeStruct(shape, jnp.float32) for shape in outs],
        scratch_shapes=[
            pltpu.VMEM((size, cap), jnp.float32),
            pltpu.VMEM((pieces * size, cap), jnp.bfloat16),
            pltpu.VMEM((size, size), jnp.float32),
            pltpu.VMEM((4,) + part, jnp.float32),
        ],
        compiler_params=pltpu.CompilerParams(vmem_limit_bytes=VMEM_LIMIT),
        cost_estimate=FACTOR_COST,
    )(quarter, place, *[ref for pair in pairs for ref in pair], first, genotypes)


def second_kernel(gain, inner_ref, own_ref, out_ref, basis_ref, work_ref):
    start_factor(work_ref, inner_ref[...])
    inverse_factor(work_ref, work_ref.shape[0], 32)
    factor = finish_factor(work_ref)
    out_ref[...] = factor
    own = jnp.dot(factor, own_ref[...], precision=HIGHEST, preferred_element_type=jnp.float32)
    basis_ref[...] = own.T * gain


def second_factor(inner, own, gain):
    size, width = own.shape
    return pl.pallas_call(
        functools.partial(second_kernel, gain),
        in_specs=[pl.BlockSpec(memory_space=pltpu.VMEM)] * 2,
        out_specs=[pl.BlockSpec(memory_space=pltpu.VMEM)] * 2,
        out_shape=[
            jax.ShapeDtypeStruct((size, size), jnp.float32),
            jax.ShapeDtypeStruct((width, size), jnp.float32),
        ],
        scratch_shapes=[pltpu.VMEM((size, 2 * size), jnp.float32)],
        compiler_params=pltpu.CompilerParams(vmem_limit_bytes=VMEM_LIMIT),
        cost_estimate=FACTOR_COST,
    )(inner, own)


def finish_kernel(scale, quarter_ref, factor_ref, *refs):
    parts, (out_ref, trace_ref, folded_ref) = refs[:4], refs[4:]
    for offset in range(4):
        folded_ref[jnp.bitwise_xor(quarter_ref[0], offset)] = parts[offset][...]
    cross = unfold_symmetric([folded_ref[place] for place in range(4)])
    factor = factor_ref[...]
    half = jnp.dot(factor, cross, precision=HIGHEST, preferred_element_type=jnp.float32)
    result = scale * lax.dot_general(
        half, factor, (((1,), (1,)), ((), ())), precision=HIGHEST, preferred_element_type=jnp.float32
    )
    out_ref[...] = result
    row = lax.broadcasted_iota(jnp.int32, result.shape, 0)
    column = lax.broadcasted_iota(jnp.int32, result.shape, 1)
    trace_ref[...] = jnp.broadcast_to(jnp.sum(jnp.where(row == column, result, 0.0)), trace_ref.shape)


def finish(quarter, factor, parts, scale):
    vmem = pl.BlockSpec(memory_space=pltpu.VMEM)
    return pl.pallas_call(
        functools.partial(finish_kernel, scale),
        in_specs=[pl.BlockSpec(memory_space=pltpu.SMEM)] + [vmem] * 5,
        out_specs=[vmem] * 2,
        out_shape=[
            jax.ShapeDtypeStruct(factor.shape, jnp.float32),
            jax.ShapeDtypeStruct((SUBLANES, LANES), jnp.float32),
        ],
        scratch_shapes=[pltpu.VMEM((4,) + parts[0].shape, jnp.float32)],
        compiler_params=pltpu.CompilerParams(vmem_limit_bytes=VMEM_LIMIT),
    )(quarter, factor, *parts)


def to_natural(pair, order, me):
    places = jnp.argsort(jnp.array(order, jnp.int32))
    mine = jnp.bitwise_xor(jnp.arange(len(order), dtype=jnp.int32), me)
    stacked = jnp.concatenate(pair, axis=0)[places][mine]
    rows = jnp.transpose(stacked, (1, 0, 2)).reshape(1, stacked.shape[1], -1)
    return tuple(jnp.split(rows, 2, axis=2))


def to_relative(pair, order, me, width):
    rows = jnp.concatenate(pair, axis=2)[0]
    chunks = jnp.transpose(rows.reshape(rows.shape[0], -1, width), (1, 0, 2))
    chunks = chunks[jnp.bitwise_xor(jnp.array(order, jnp.int32), me)]
    return tuple(jnp.split(chunks, 2, axis=0))


def body(genotypes, sizes, start):
    groups = lax.axis_size("smp")
    dosages = genotypes[0]
    samples, cap = dosages.shape
    width, size = start.shape[1:]
    half = size // 2
    scale = 1.0 / (samples * groups)
    me = lax.axis_index("smp")
    where = me.reshape(1).astype(jnp.int32)
    chains = [stage_bits(groups, flip) for flip in (False, True)]
    orders = [relative_order(stages) for stages in chains]

    first_row = me * width
    live = first_row + lax.broadcasted_iota(jnp.int32, (width, size), 0) < sizes[0]
    columns = jnp.where(live, start[0], 0.0).T
    chunks = columns.reshape(2, half, width)
    aligned = width % LANES == 0
    place = where if aligned else jnp.zeros_like(where)
    laid = orders if aligned else [[0, 1]] * 2

    def gather(chunks):
        pairs = gather_chunks(chunks, groups, chains)
        if aligned:
            return pairs
        return [to_natural(pair, order, me) for pair, order in zip(pairs, orders)]

    def apply(pairs):
        outs = [
            apply_samples(dosages, sizes, place, *pair, order, PIECES, scale) for pair, order in zip(pairs, laid)
        ]
        if not aligned:
            outs = [to_relative(out, order, me, width) for out, order in zip(outs, orders)]
        return reduce_chunks(outs, groups, chains)

    pairs = gather(apply(gather(chunks)))
    first = first_factor(place, pairs, laid, cap)
    pairs = gather(apply(pairs))
    quarter = jnp.bitwise_and(where, 3)
    own, inner, *quarters = project(dosages, quarter, place, pairs, laid, first, PIECES, aligned, width)
    if not aligned:
        own = lax.dynamic_slice(own, (0, first_row), (size, width))
    quarters = sum_quarters(quarters, groups)
    second, basis = second_factor(inner, own, math.sqrt(cap))
    rayleigh, trace = finish(quarter, second, quarters, scale)
    blocks = lax.axis_size("blk")
    total = trace
    for shift in range(1, blocks):
        total = total + lax.ppermute(trace, "blk", [(block, (block + shift) % blocks) for block in range(blocks)])
    scaled = rayleigh * (genotypes.shape[0] * blocks * size / total[0, 0])
    return basis[None], scaled[None]


def solution(mesh):
    return jax.shard_map(
        body,
        mesh=mesh,
        in_specs=(P("blk", "smp", None), P("blk"), P("blk", "smp", None)),
        out_specs=(P("blk", "smp", None), P("blk", None, None)),
        check_vma=False,
    )
```

```python
import functools
import math

import jax
import jax.numpy as jnp
from jax import lax
from jax.experimental import pallas as pl
from jax.experimental.pallas import tpu as pltpu
from jax.sharding import PartitionSpec as P

LANES = 128
SUBLANES = 8
BLOCK = 1024
PANEL = 32
PIECES = 2
CODES = 128
STEPS = 65535.0
LEAST = 2.0**-90
VMEM_LIMIT = 48 * 1024 * 1024
HIGHEST = lax.Precision.HIGHEST
FACTOR_COST = pl.CostEstimate(flops=12_000_000_000, bytes_accessed=4 << 20, transcendentals=0)


def stage_bits(groups):
    count = groups.bit_length() - 1
    return [list(range(count))[place : place + 2] for place in range(0, count, 2)]


def offsets(bits):
    found = [0]
    for bit in bits:
        found = found + [value ^ (1 << bit) for value in found]
    return found


def relative_order(stages):
    order = [0]
    for bits in reversed(stages):
        order = [high ^ low for high in offsets(bits) for low in order]
    return order


def exchange(value, groups, offset):
    return lax.ppermute(value, "smp", [(device, device ^ offset) for device in range(groups)])


def reduce_chunks(keep, sends, groups, packed):
    stages = stage_bits(groups)
    for depth, bits in enumerate(stages):
        arrived = [exchange(send, groups, span) for send, span in zip(sends, offsets(bits)[1:])]
        parts = len(offsets(stages[depth + 1])) if depth + 1 < len(stages) else 1
        if packed:
            keep, *sends = combine(keep, arrived, parts)
        else:
            keep, *sends = jnp.split(keep + sum(arrived), parts, axis=0)
    return keep, sends[0] if packed else keep


def gather_chunks(message, groups):
    stages = stage_bits(groups)
    for bits in reversed(stages[1:]):
        message = jnp.concatenate([message] + [exchange(message, groups, span) for span in offsets(bits)[1:]], axis=0)
    return [message] + [exchange(message, groups, span) for span in offsets(stages[0])[1:]]


def pair_sum(parts):
    while len(parts) > 1:
        parts = [left + right for left, right in zip(parts[::2], parts[1::2])]
    return parts[0]


def sum_quarters(quarters, groups):
    stages = stage_bits(groups)
    spans = offsets(stages[0])
    total = pair_sum([quarters[0]] + [exchange(part, groups, span) for part, span in zip(quarters[1:], spans[1:])])
    for bits in stages[1:]:
        total = pair_sum([total] + [exchange(total, groups, span) for span in offsets(bits)[1:]])
    return [total] + [exchange(total, groups, span) for span in spans[1:]]


def row_scales(peaks):
    codes = jnp.ceil(jnp.log2(jnp.maximum(peaks, LEAST)) * CODES) + 1.0
    return codes, jnp.exp2(codes * (1.0 / CODES))


def gather_columns(columns):
    lane = lax.broadcasted_iota(jnp.int32, (LANES, LANES), 1)
    matrix = jnp.zeros((LANES, LANES), jnp.float32)
    for place, column in enumerate(columns):
        matrix = jnp.where(lane == place, column, matrix)
    return matrix


def pack_tiles(tiles):
    peaks = gather_columns([jnp.max(jnp.abs(tile), axis=1, keepdims=True) for tile in tiles])
    codes, scales = row_scales(peaks)
    factors = STEPS / scales
    lines = codes.T
    half = LANES // 2
    messages = []
    for place, tile in enumerate(tiles):
        value = jnp.round(tile * factors[:, place : place + 1]).astype(jnp.int32)
        high = jnp.right_shift(value, 1)
        low = jnp.bitwise_and(value, 1)
        words = jnp.bitwise_or(jnp.left_shift(high[:half], 16), jnp.bitwise_and(high[half:], 0xFFFF))
        code = jnp.broadcast_to(lines[place : place + 1, :], (SUBLANES, LANES)).astype(jnp.int32)
        extra = jnp.left_shift(code, 16)
        for group in range(LANES // SUBLANES):
            bits = low[group * SUBLANES : (group + 1) * SUBLANES]
            extra = jnp.bitwise_or(extra, jnp.left_shift(bits, group))
        messages.append(jnp.concatenate([words, extra], axis=0))
    return messages


def unpack_tiles(messages):
    half = LANES // 2
    lines = [jnp.right_shift(message[half : half + 1], 16).astype(jnp.float32) for message in messages]
    lines.append(jnp.zeros((LANES - len(messages), LANES), jnp.float32))
    scales = (jnp.exp2(jnp.concatenate(lines, axis=0) * (1.0 / CODES)) * (1.0 / STEPS)).T

    def tile(place):
        words, extra = messages[place][:half], messages[place][half:]
        high = jnp.concatenate([jnp.right_shift(words, 16), jnp.right_shift(jnp.left_shift(words, 16), 16)], axis=0)
        low = jnp.concatenate(
            [jnp.bitwise_and(jnp.right_shift(extra, group), 1) for group in range(LANES // SUBLANES)], axis=0
        )
        value = jnp.bitwise_or(jnp.left_shift(high, 1), low)
        return value.astype(jnp.float32) * scales[:, place : place + 1]

    return [functools.partial(tile, place) for place in range(len(messages))]


PACKED = LANES // 2 + SUBLANES


def pack_chunks(chunks):
    parts = chunks[0].shape[0] // LANES
    messages = pack_tiles([chunk[part * LANES : (part + 1) * LANES] for chunk in chunks for part in range(parts)])
    return [jnp.concatenate(messages[place * parts : (place + 1) * parts], axis=0) for place in range(len(chunks))]


def unpack_chunks(messages):
    parts = messages[0].shape[0] // PACKED
    tiles = unpack_tiles(
        [message[part * PACKED : (part + 1) * PACKED] for message in messages for part in range(parts)]
    )
    return [tiles[place * parts : (place + 1) * parts] for place in range(len(messages))]


def encode_kernel(place_ref, size_ref, start_ref, out_ref):
    width, size = start_ref.shape
    row = place_ref[0] * width + lax.broadcasted_iota(jnp.int32, (width, size), 0)
    value = jnp.where(row < size_ref[0], start_ref[...], 0.0)
    out_ref[0] = pack_chunks([value.T])[0]


def encode(place, sizes, start):
    width, size = start.shape
    scalar, vmem = pl.BlockSpec(memory_space=pltpu.SMEM), pl.BlockSpec(memory_space=pltpu.VMEM)
    return pl.pallas_call(
        encode_kernel,
        in_specs=[scalar, scalar, vmem],
        out_specs=vmem,
        out_shape=jax.ShapeDtypeStruct((1, size // LANES * PACKED, width), jnp.int32),
    )(place, sizes, start)


def combine_kernel(count, parts, keep_ref, *refs):
    arrived, own_ref, sends = refs[:count], refs[count], refs[count + 1 :]
    chunks = keep_ref.shape[0]
    tiles = unpack_chunks([part[place] for place in range(chunks) for part in arrived])
    totals = []
    for place in range(chunks):
        total = keep_ref[place]
        for source in range(count):
            total = total + jnp.concatenate([tile() for tile in tiles[place * count + source]], axis=0)
        totals.append(total)
    width = chunks // parts
    for place in range(width):
        own_ref[place] = totals[place]
    first = 0 if parts == 1 else width
    for place, message in enumerate(pack_chunks(totals[first:])):
        sends[place // width][place % width] = message


def combine(keep, arrived, parts):
    chunks, rows, lanes = keep.shape
    width = chunks // parts
    vmem = pl.BlockSpec(memory_space=pltpu.VMEM)
    outs = [jax.ShapeDtypeStruct((width, rows, lanes), jnp.float32)]
    outs += [jax.ShapeDtypeStruct((width, rows // LANES * PACKED, lanes), jnp.int32)] * max(parts - 1, 1)
    return pl.pallas_call(
        functools.partial(combine_kernel, len(arrived), parts),
        in_specs=[vmem] * (1 + len(arrived)),
        out_specs=[vmem] * len(outs),
        out_shape=outs,
        compiler_params=pltpu.CompilerParams(vmem_limit_bytes=VMEM_LIMIT),
    )(keep, *arrived)


def split_pieces(value, pieces):
    parts = []
    rest = value
    for piece in range(pieces):
        part = rest.astype(jnp.bfloat16)
        parts.append(part)
        if piece + 1 < pieces:
            rest = rest - part.astype(jnp.float32)
    return parts


def load_all(order, place_ref, refs, full_ref):
    if len(refs) == 1:
        full_ref[...] = refs[0][...]
        return
    width = refs[0].shape[2]
    each = refs[0].shape[0]
    tiles = unpack_chunks([ref[place] for ref in refs for place in range(each)])
    for offset, chunk in zip(order, tiles):
        first = pl.multiple_of(jnp.bitwise_xor(place_ref[0], offset) * width, width)
        for part, tile in enumerate(chunk):
            full_ref[pl.ds(part * LANES, LANES), pl.ds(first, width)] = tile()


def apply_kernel(order, normalise, scale, sources, place_ref, size_ref, rows_ref, *refs):
    refs, outs, (full_ref, split_ref, work_ref) = refs[:sources], refs[sources:-3], refs[-3:]
    step = pl.program_id(0)
    size, cap = full_ref.shape

    @pl.when(step == 0)
    def _():
        load_all(order, place_ref, refs, full_ref)
        value = full_ref[...]
        if normalise:
            start_factor(work_ref, rows_inner(value))
            inverse_factor(work_ref, size, PANEL)
            value = jnp.dot(
                finish_factor(work_ref), value, precision=HIGHEST, preferred_element_type=jnp.float32
            )
        for piece, part in enumerate(split_pieces(value, PIECES)):
            split_ref[pl.ds(piece * size, size), :] = part

    rows = rows_ref[...]
    image = lax.dot_general(
        split_ref[...], rows, (((1,), (1,)), ((), ())), preferred_element_type=jnp.float32
    )
    image = sum(image[piece * size : (piece + 1) * size] for piece in range(PIECES)) * scale
    back = jnp.dot(
        jnp.concatenate(split_pieces(image, PIECES), axis=0), rows, preferred_element_type=jnp.float32
    )
    back = sum(back[piece * size : (piece + 1) * size] for piece in range(PIECES))

    @pl.when(step == 0)
    def _():
        full_ref[...] = back

    @pl.when(step > 0)
    def _():
        full_ref[...] += back

    @pl.when(step == pl.num_programs(0) - 1)
    def _():
        live = lax.broadcasted_iota(jnp.int32, (1, cap), 1) < size_ref[0]
        full_ref[...] = jnp.where(live, full_ref[...], 0.0)
        if len(outs) == 1:
            outs[0][...] = full_ref[...]
            return
        each, _, width = outs[0].shape
        chunks = []
        for offset in order:
            first = pl.multiple_of(jnp.bitwise_xor(place_ref[0], offset) * width, width)
            chunks.append(full_ref[:, pl.ds(first, width)])
        for place in range(each):
            outs[0][place] = chunks[place]
        for place, message in enumerate(pack_chunks(chunks[each:])):
            outs[1 + place // each][place % each] = message


def apply_samples(genotypes, sizes, place, gathered, order, normalise, scale, groups):
    samples, cap = genotypes.shape
    block = min(BLOCK, samples)
    packed = len(gathered) > 1
    if packed:
        each, rows, width = gathered[0].shape
        size = rows // PACKED * LANES
        outs = [jax.ShapeDtypeStruct((each, size, width), jnp.float32)]
        outs += [jax.ShapeDtypeStruct((each, rows, width), jnp.int32)] * (len(gathered) - 1)
    else:
        size = gathered[0].shape[0]
        outs = [jax.ShapeDtypeStruct((size, cap), jnp.float32)]
    scalar = pl.BlockSpec(memory_space=pltpu.SMEM)

    def whole(value):
        return pl.BlockSpec(value.shape, lambda step: (0,) * len(value.shape))

    return pl.pallas_call(
        functools.partial(apply_kernel, order, normalise, scale, len(gathered)),
        grid=(samples // block,),
        in_specs=[scalar, scalar, pl.BlockSpec((block, cap), lambda step: (step, 0))]
        + [whole(part) for part in gathered],
        out_specs=[whole(out) for out in outs],
        out_shape=outs,
        scratch_shapes=[
            pltpu.VMEM((size, cap), jnp.float32),
            pltpu.VMEM((PIECES * size, cap), jnp.bfloat16),
            pltpu.VMEM((size, 2 * size), jnp.float32),
        ],
        compiler_params=pltpu.CompilerParams(vmem_limit_bytes=VMEM_LIMIT),
    )(place, sizes, genotypes, *gathered)


def lane_splat(tile, lane):
    return jnp.broadcast_to(tile[:, lane : lane + 1], (SUBLANES, LANES))


def row_splat(tile, row):
    return jnp.broadcast_to(tile[row : row + 1, :], (SUBLANES, LANES))


def inverse_factor(work_ref, size, panel):
    tiles = 2 * size // LANES
    below = lax.broadcasted_iota(jnp.int32, (SUBLANES, LANES), 0)
    groups = panel // SUBLANES
    for top in range(0, size, panel):
        active = [
            tile
            for tile in range(tiles)
            if (top // LANES <= tile < size // LANES)
            or (size // LANES <= tile <= size // LANES + (top + panel - 1) // LANES)
        ]
        rows = [
            {
                tile: work_ref[top + SUBLANES * group : top + SUBLANES * (group + 1), tile * LANES : (tile + 1) * LANES]
                for tile in active
            }
            for group in range(groups)
        ]
        for block in range(groups):
            base = top + SUBLANES * block
            columns = {
                group: [lane_splat(rows[group][base // LANES], base % LANES + lane) for lane in range(SUBLANES)]
                for group in range(block, groups)
            }
            for step in range(SUBLANES):
                pivot = row_splat(columns[block][step], step)
                root = lax.rsqrt(pivot)
                root = root * (1.5 - 0.5 * pivot * root * root)
                factor = {group: columns[group][step] * root for group in range(block, groups)}
                for later in range(step + 1, SUBLANES):
                    weight = row_splat(factor[block], later)
                    for group in range(block, groups):
                        columns[group][later] = columns[group][later] - factor[group] * weight
                lower = jnp.where(below > step, factor[block], 0.0)
                for tile in active:
                    line = row_splat(rows[block][tile], step) * root
                    rows[block][tile] = jnp.where(
                        below == step, line, rows[block][tile] - lower * line
                    )
                    for group in range(block + 1, groups):
                        rows[group][tile] = rows[group][tile] - factor[group] * line
        for group in range(groups):
            for tile in active:
                work_ref[top + SUBLANES * group : top + SUBLANES * (group + 1), tile * LANES : (tile + 1) * LANES] = rows[
                    group
                ][tile]
        rest = top + panel
        if rest < size:
            first, last = active[0] * LANES, (active[-1] + 1) * LANES
            lines = work_ref[top:rest, first:last]
            weights = work_ref[top:rest, rest // LANES * LANES : size].T[rest % LANES :, :]
            work_ref[rest:, first:last] -= jnp.dot(
                weights, lines, precision=HIGHEST, preferred_element_type=jnp.float32
            )


def start_factor(work_ref, inner):
    size = inner.shape[0]
    work_ref[:, :size] = inner
    row = lax.broadcasted_iota(jnp.int32, (size, size), 0)
    column = lax.broadcasted_iota(jnp.int32, (size, size), 1)
    work_ref[:, size:] = jnp.where(row == column, 1.0, 0.0)


def finish_factor(work_ref):
    size = work_ref.shape[0]
    row = lax.broadcasted_iota(jnp.int32, (size, size), 0)
    column = lax.broadcasted_iota(jnp.int32, (size, size), 1)
    return jnp.where(row >= column, work_ref[:, size:], 0.0)


def rows_inner(value):
    return lax.dot_general(
        value, value, (((1,), (1,)), ((), ())), precision=HIGHEST, preferred_element_type=jnp.float32
    )


def fold_symmetric(value, folded_ref, height):
    half = value.shape[0] // 2
    row = lax.broadcasted_iota(jnp.int32, (half, half), 0)
    column = lax.broadcasted_iota(jnp.int32, (half, half), 1)
    corner = value[half:, half:]
    both = jnp.where(row >= column, value[:half, :half], corner)
    diagonal = jnp.sum(jnp.where(row == column, corner, 0.0), axis=0, keepdims=True)
    quarter = half // 2
    for place in range(4):
        source = value[half:, :half] if place < 2 else both
        folded_ref[place, :quarter] = source[place % 2 * quarter : (place % 2 + 1) * quarter]
        folded_ref[place, quarter:] = jnp.broadcast_to(diagonal, (SUBLANES, half))


def unfold_symmetric(parts):
    quarter = parts[0].shape[0] - SUBLANES
    half = 2 * quarter
    row = lax.broadcasted_iota(jnp.int32, (half, half), 0)
    column = lax.broadcasted_iota(jnp.int32, (half, half), 1)
    left = jnp.concatenate([parts[0][:quarter], parts[1][:quarter]], axis=0)
    both = jnp.concatenate([parts[2][:quarter], parts[3][:quarter]], axis=0)
    turned = both.T
    corner = jnp.where(row == column, parts[3][quarter : quarter + 1], jnp.where(row < column, both, turned))
    upper = jnp.concatenate([jnp.where(row >= column, both, turned), left.T], axis=1)
    return jnp.concatenate([upper, jnp.concatenate([left, corner], axis=1)], axis=0)


def project_kernel(order, sources, quarter_ref, place_ref, rows_ref, *refs):
    refs, (inner_ref, *outs), (full_ref, split_ref, cross_ref, folded_ref) = refs[:sources], refs[sources:-4], refs[-4:]
    step = pl.program_id(0)
    size = full_ref.shape[0]

    @pl.when(step == 0)
    def _():
        load_all(order, place_ref, refs, full_ref)
        image = full_ref[...]
        inner_ref[...] = rows_inner(image)
        for piece, part in enumerate(split_pieces(image, PIECES)):
            split_ref[pl.ds(piece * size, size), :] = part
        cross_ref[...] = jnp.zeros_like(cross_ref)

    sampled = lax.dot_general(
        split_ref[...], rows_ref[...], (((1,), (1,)), ((), ())), preferred_element_type=jnp.float32
    )
    sampled = sum(sampled[piece * size : (piece + 1) * size] for piece in range(PIECES))
    cross_ref[...] += rows_inner(sampled)

    @pl.when(step == pl.num_programs(0) - 1)
    def _():
        fold_symmetric(cross_ref[...], folded_ref, size)
        for offset, out_ref in enumerate(outs):
            out_ref[...] = folded_ref[jnp.bitwise_xor(quarter_ref[0], offset)]


def project(genotypes, quarter, place, gathered, order, size):
    samples, cap = genotypes.shape
    block = min(BLOCK, samples)
    scalar = pl.BlockSpec(memory_space=pltpu.SMEM)

    def whole(shape):
        return pl.BlockSpec(shape, lambda step: (0,) * len(shape))

    part = (size // 4 + SUBLANES, size // 2)
    outs = [(size, size)] + [part] * 4
    return pl.pallas_call(
        functools.partial(project_kernel, order, len(gathered)),
        grid=(samples // block,),
        in_specs=[scalar, scalar, pl.BlockSpec((block, cap), lambda step: (step, 0))]
        + [whole(part.shape) for part in gathered],
        out_specs=[whole(shape) for shape in outs],
        out_shape=[jax.ShapeDtypeStruct(shape, jnp.float32) for shape in outs],
        scratch_shapes=[
            pltpu.VMEM((size, cap), jnp.float32),
            pltpu.VMEM((PIECES * size, cap), jnp.bfloat16),
            pltpu.VMEM((size, size), jnp.float32),
            pltpu.VMEM((4,) + part, jnp.float32),
        ],
        compiler_params=pltpu.CompilerParams(vmem_limit_bytes=VMEM_LIMIT),
    )(quarter, place, genotypes, *gathered)


def second_kernel(gain, inner_ref, own_ref, out_ref, basis_ref, work_ref):
    start_factor(work_ref, inner_ref[...])
    inverse_factor(work_ref, work_ref.shape[0], PANEL)
    factor = finish_factor(work_ref)
    out_ref[...] = factor
    own = jnp.dot(factor, own_ref[...], precision=HIGHEST, preferred_element_type=jnp.float32)
    basis_ref[...] = own.T * gain


def second_factor(inner, own, gain):
    size, width = own.shape
    return pl.pallas_call(
        functools.partial(second_kernel, gain),
        in_specs=[pl.BlockSpec(memory_space=pltpu.VMEM)] * 2,
        out_specs=[pl.BlockSpec(memory_space=pltpu.VMEM)] * 2,
        out_shape=[
            jax.ShapeDtypeStruct((size, size), jnp.float32),
            jax.ShapeDtypeStruct((width, size), jnp.float32),
        ],
        scratch_shapes=[pltpu.VMEM((size, 2 * size), jnp.float32)],
        compiler_params=pltpu.CompilerParams(vmem_limit_bytes=VMEM_LIMIT),
        cost_estimate=FACTOR_COST,
    )(inner, own)


def finish_kernel(scale, quarter_ref, factor_ref, *refs):
    parts, (out_ref, trace_ref, folded_ref) = refs[:4], refs[4:]
    for offset in range(4):
        folded_ref[jnp.bitwise_xor(quarter_ref[0], offset)] = parts[offset][...]
    cross = unfold_symmetric([folded_ref[place] for place in range(4)])
    factor = factor_ref[...]
    half = jnp.dot(factor, cross, precision=HIGHEST, preferred_element_type=jnp.float32)
    result = scale * lax.dot_general(
        half, factor, (((1,), (1,)), ((), ())), precision=HIGHEST, preferred_element_type=jnp.float32
    )
    out_ref[...] = result
    row = lax.broadcasted_iota(jnp.int32, result.shape, 0)
    column = lax.broadcasted_iota(jnp.int32, result.shape, 1)
    trace_ref[...] = jnp.broadcast_to(jnp.sum(jnp.where(row == column, result, 0.0)), trace_ref.shape)


def finish(quarter, factor, parts, scale):
    vmem = pl.BlockSpec(memory_space=pltpu.VMEM)
    return pl.pallas_call(
        functools.partial(finish_kernel, scale),
        in_specs=[pl.BlockSpec(memory_space=pltpu.SMEM)] + [vmem] * 5,
        out_specs=[vmem] * 2,
        out_shape=[
            jax.ShapeDtypeStruct(factor.shape, jnp.float32),
            jax.ShapeDtypeStruct((SUBLANES, LANES), jnp.float32),
        ],
        scratch_shapes=[pltpu.VMEM((4,) + parts[0].shape, jnp.float32)],
        compiler_params=pltpu.CompilerParams(vmem_limit_bytes=VMEM_LIMIT),
    )(quarter, factor, *parts)


def to_natural(gathered, order, me):
    places = jnp.argsort(jnp.array(order, jnp.int32))
    mine = jnp.bitwise_xor(jnp.arange(len(order), dtype=jnp.int32), me)
    stacked = jnp.concatenate(gathered, axis=0)[places][mine]
    return jnp.transpose(stacked, (1, 0, 2)).reshape(stacked.shape[1], -1)


def to_relative(rows, order, me, width, parts):
    chunks = jnp.transpose(rows.reshape(rows.shape[0], -1, width), (1, 0, 2))
    return jnp.split(chunks[jnp.bitwise_xor(jnp.array(order, jnp.int32), me)], parts, axis=0)


def body(genotypes, sizes, start):
    groups = lax.axis_size("smp")
    dosages = genotypes[0]
    samples, cap = dosages.shape
    width, size = start.shape[1:]
    scale = 1.0 / (samples * groups)
    me = lax.axis_index("smp")
    place = me.reshape(1).astype(jnp.int32)
    stages = stage_bits(groups)
    order = relative_order(stages)
    packed = width == LANES

    def gather(message):
        gathered = gather_chunks(message, groups)
        return gathered if packed else [to_natural(gathered, order, me)]

    def apply(message, normalise):
        outs = apply_samples(dosages, sizes, place, gather(message), order, normalise, scale, groups)
        if not packed:
            outs = to_relative(outs[0], order, me, width, len(offsets(stages[0])))
        return reduce_chunks(outs[0], outs[1:], groups, packed)

    if packed:
        message = encode(place, sizes, start[0])
    else:
        row = me * width + lax.broadcasted_iota(jnp.int32, (width, size), 0)
        message = jnp.where(row < sizes[0], start[0], 0.0).T[None]
    _, message = apply(message, False)
    own, message = apply(message, True)
    quarter = jnp.bitwise_and(place, 3)
    inner, *quarters = project(dosages, quarter, place, gather(message), order, size)
    quarters = sum_quarters(quarters, groups)
    second, basis = second_factor(inner, own[0], math.sqrt(cap))
    rayleigh, trace = finish(quarter, second, quarters, scale)
    blocks = lax.axis_size("blk")
    total = trace
    for shift in range(1, blocks):
        total = total + lax.ppermute(trace, "blk", [(block, (block + shift) % blocks) for block in range(blocks)])
    scaled = rayleigh * (genotypes.shape[0] * blocks * size / total[0, 0])
    return basis[None], scaled[None]


def solution(mesh):
    return jax.shard_map(
        body,
        mesh=mesh,
        in_specs=(P("blk", "smp", None), P("blk"), P("blk", "smp", None)),
        out_specs=(P("blk", "smp", None), P("blk", None, None)),
        check_vma=False,
    )
```

```python
import functools
import math

import jax
import jax.numpy as jnp
from jax import lax
from jax.experimental import pallas as pl
from jax.experimental.pallas import tpu as pltpu
from jax.sharding import PartitionSpec as P

LANES = 128
SUBLANES = 8
PANEL = 32
PIECES = 2
CODES = 128
STEPS = 65535.0
LEAST = 2.0**-90
VMEM_LIMIT = 40 * 1024 * 1024
HIGHEST = lax.Precision.HIGHEST
FACTOR_COST = pl.CostEstimate(flops=4_000_000_000, bytes_accessed=4 << 20, transcendentals=0)


def stage_bits(groups):
    count = groups.bit_length() - 1
    return [list(range(count))[place : place + 2] for place in range(0, count, 2)]


def offsets(bits):
    found = [0]
    for bit in bits:
        found = found + [value ^ (1 << bit) for value in found]
    return found


def relative_order(stages):
    order = [0]
    for bits in reversed(stages):
        order = [high ^ low for high in offsets(bits) for low in order]
    return order


def exchange(value, groups, offset):
    return lax.ppermute(value, "smp", [(device, device ^ offset) for device in range(groups)])


def reduce_chunks(keep, sends, groups, packed):
    stages = stage_bits(groups)
    for depth, bits in enumerate(stages):
        arrived = [exchange(send, groups, span) for send, span in zip(sends, offsets(bits)[1:])]
        parts = len(offsets(stages[depth + 1])) if depth + 1 < len(stages) else 1
        if packed:
            keep, *sends = combine(keep, arrived, parts)
        else:
            keep, *sends = jnp.split(keep + sum(arrived), parts, axis=0)
    return keep, sends[0] if packed else keep


def gather_chunks(message, groups):
    stages = stage_bits(groups)
    for bits in reversed(stages[1:]):
        message = jnp.concatenate([message] + [exchange(message, groups, span) for span in offsets(bits)[1:]], axis=0)
    return [message] + [exchange(message, groups, span) for span in offsets(stages[0])[1:]]


def pair_sum(parts):
    while len(parts) > 1:
        parts = [left + right for left, right in zip(parts[::2], parts[1::2])]
    return parts[0]


def sum_quarters(quarters, groups, beside):
    stages = stage_bits(groups)
    spans = offsets(stages[0])
    steps = list(beside)
    state = steps.pop(0)(None)
    arrived = [exchange(part, groups, span) for part, span in zip(quarters[1:], spans[1:])]
    arrived, state = lax.optimization_barrier((arrived, state))
    total = pair_sum([quarters[0]] + arrived)
    for bits in stages[1:]:
        if len(steps) > 1:
            state = steps.pop(0)(state)
        arrived = [exchange(total, groups, span) for span in offsets(bits)[1:]]
        arrived, state = lax.optimization_barrier((arrived, state))
        total = pair_sum([total] + arrived)
    for step in steps:
        state = step(state)
    return [total] + [exchange(total, groups, span) for span in spans[1:]], state


TILES = 2
FINE = 28
NIBBLES = 4
PACKED = TILES * LANES // 2 + SUBLANES


def row_scales(peaks):
    codes = jnp.ceil(jnp.log2(jnp.maximum(peaks, LEAST)) * CODES) + 1.0
    return codes, jnp.exp2(codes * (1.0 / CODES))


def gather_columns(columns):
    lane = lax.broadcasted_iota(jnp.int32, (LANES, LANES), 1)
    matrix = jnp.zeros((LANES, LANES), jnp.float32)
    for place, column in enumerate(columns):
        matrix = jnp.where(lane == place, column, matrix)
    return matrix


def pack_chunks(chunks):
    peaks = [jnp.max(jnp.abs(chunk), axis=1, keepdims=True) for chunk in chunks]
    codes, scales = row_scales(
        gather_columns([peak[tile * LANES : (tile + 1) * LANES] for peak in peaks for tile in range(TILES)])
    )
    factors = STEPS / scales
    lines = codes.T.astype(jnp.int32)
    sub = lax.broadcasted_iota(jnp.int32, (SUBLANES, LANES), 0)
    half = TILES * LANES // 2
    messages = []
    for place, chunk in enumerate(chunks):
        factor = jnp.concatenate(
            [factors[:, TILES * place + tile : TILES * place + tile + 1] for tile in range(TILES)], axis=0
        )
        scaled = chunk * factor
        fine = FINE * SUBLANES
        value = jnp.concatenate(
            [jnp.round(scaled[:fine]).astype(jnp.int32), 2 * jnp.round(0.5 * scaled[fine:]).astype(jnp.int32)], axis=0
        )
        high = jnp.clip(jnp.right_shift(value, 1), -32768, 32767)
        words = jnp.bitwise_or(jnp.left_shift(high[:half], 16), jnp.bitwise_and(high[half:], 0xFFFF))
        first = jnp.broadcast_to(lines[TILES * place : TILES * place + 1], (SUBLANES, LANES))
        second = jnp.broadcast_to(lines[TILES * place + 1 : TILES * place + 2], (SUBLANES, LANES))
        code = jnp.where(sub < NIBBLES, first, second)
        nibble = jnp.right_shift(code, NIBBLES * jnp.bitwise_and(sub, NIBBLES - 1))
        extra = jnp.left_shift(nibble, FINE)
        for group in range(FINE):
            bits = jnp.bitwise_and(value[group * SUBLANES : (group + 1) * SUBLANES], 1)
            extra = jnp.bitwise_or(extra, jnp.left_shift(bits, group))
        messages.append(jnp.concatenate([words, extra], axis=0))
    return messages


def unpack_chunks(messages):
    half = TILES * LANES // 2
    lines = []
    for message in messages:
        nibble = jnp.bitwise_and(jnp.right_shift(message[half:], FINE), 15)
        for tile in range(TILES):
            code = jnp.left_shift(nibble[tile * NIBBLES + NIBBLES - 1 : (tile + 1) * NIBBLES], 28)
            code = jnp.right_shift(code, 28 - NIBBLES * (NIBBLES - 1))
            for place in range(NIBBLES - 1):
                line = nibble[tile * NIBBLES + place : tile * NIBBLES + place + 1]
                code = jnp.bitwise_or(code, jnp.left_shift(line, NIBBLES * place))
            lines.append(code.astype(jnp.float32))
    lines.append(jnp.zeros((LANES - len(lines), LANES), jnp.float32))
    scales = (jnp.exp2(jnp.concatenate(lines, axis=0) * (1.0 / CODES)) * (1.0 / STEPS)).T

    def make(place, tile):
        words, extra = messages[place][:half], messages[place][half:]
        high = jnp.right_shift(words if tile == 0 else jnp.left_shift(words, 16), 16)
        low = [
            jnp.bitwise_and(jnp.right_shift(extra, group), 1) if group < FINE else jnp.zeros_like(extra)
            for group in range(tile * LANES // SUBLANES, (tile + 1) * LANES // SUBLANES)
        ]
        value = jnp.bitwise_or(jnp.left_shift(high, 1), jnp.concatenate(low, axis=0))
        column = TILES * place + tile
        return value.astype(jnp.float32) * scales[:, column : column + 1]

    return [
        [functools.partial(make, place, tile) for tile in range(TILES)] for place in range(len(messages))
    ]


def encode_kernel(place_ref, size_ref, start_ref, out_ref):
    width, size = start_ref.shape
    row = place_ref[0] * width + lax.broadcasted_iota(jnp.int32, (width, size), 0)
    value = jnp.where(row < size_ref[0], start_ref[...], 0.0)
    out_ref[0] = pack_chunks([value.T])[0]


def encode(place, sizes, start):
    width, size = start.shape
    scalar, vmem = pl.BlockSpec(memory_space=pltpu.SMEM), pl.BlockSpec(memory_space=pltpu.VMEM)
    return pl.pallas_call(
        encode_kernel,
        in_specs=[scalar, scalar, vmem],
        out_specs=vmem,
        out_shape=jax.ShapeDtypeStruct((1, PACKED, width), jnp.int32),
    )(place, sizes, start)


def combine_kernel(count, parts, keep_ref, *refs):
    arrived, own_ref, sends = refs[:count], refs[count], refs[count + 1 :]
    chunks = keep_ref.shape[0]
    tiles = unpack_chunks([part[place] for place in range(chunks) for part in arrived])
    totals = []
    for place in range(chunks):
        total = keep_ref[place]
        for source in range(count):
            total = total + jnp.concatenate([tile() for tile in tiles[place * count + source]], axis=0)
        totals.append(total)
    width = chunks // parts
    for place in range(width):
        own_ref[place] = totals[place]
    first = 0 if parts == 1 else width
    for place, message in enumerate(pack_chunks(totals[first:])):
        sends[place // width][place % width] = message


def combine(keep, arrived, parts):
    chunks, rows, lanes = keep.shape
    width = chunks // parts
    vmem = pl.BlockSpec(memory_space=pltpu.VMEM)
    outs = [jax.ShapeDtypeStruct((width, rows, lanes), jnp.float32)]
    outs += [jax.ShapeDtypeStruct((width, PACKED, lanes), jnp.int32)] * max(parts - 1, 1)
    return pl.pallas_call(
        functools.partial(combine_kernel, len(arrived), parts),
        in_specs=[vmem] * (1 + len(arrived)),
        out_specs=[vmem] * len(outs),
        out_shape=outs,
        compiler_params=pltpu.CompilerParams(vmem_limit_bytes=VMEM_LIMIT),
    )(keep, *arrived)


def split_pieces(value, pieces):
    parts = []
    rest = value
    for piece in range(pieces):
        part = rest.astype(jnp.bfloat16)
        parts.append(part)
        if piece + 1 < pieces:
            rest = rest - part.astype(jnp.float32)
    return parts


def load_all(order, place_ref, refs, full_ref):
    if len(refs) == 1:
        full_ref[...] = refs[0][...]
        return
    width = refs[0].shape[2]
    each = refs[0].shape[0]
    tiles = unpack_chunks([ref[place] for ref in refs for place in range(each)])
    for offset, chunk in zip(order, tiles):
        first = pl.multiple_of(jnp.bitwise_xor(place_ref[0], offset) * width, width)
        for part, tile in enumerate(chunk):
            full_ref[pl.ds(part * LANES, LANES), pl.ds(first, width)] = tile()


def apply_kernel(order, normalise, scale, sources, place_ref, size_ref, rows_ref, *refs):
    refs, outs, (full_ref, work_ref, held_ref, sem) = refs[:sources], refs[sources:-4], refs[-4:]
    size, cap = full_ref.shape
    copy = pltpu.make_async_copy(rows_ref, held_ref, sem)
    copy.start()
    load_all(order, place_ref, refs, full_ref)
    value = full_ref[...]
    if normalise:
        start_factor(work_ref, rows_inner(value))
        inverse_factor(work_ref, size, PANEL)
        value = jnp.dot(finish_factor(work_ref), value, precision=HIGHEST, preferred_element_type=jnp.float32)
    split = jnp.concatenate(split_pieces(value, PIECES), axis=0)
    copy.wait()
    image = rows_dot(split, held_ref[...])
    image = sum(image[piece * size : (piece + 1) * size] for piece in range(PIECES)) * scale
    split = jnp.concatenate(split_pieces(image, PIECES), axis=0)
    back = jnp.dot(split, held_ref[...], preferred_element_type=jnp.float32)
    back = sum(back[piece * size : (piece + 1) * size] for piece in range(PIECES))
    live = lax.broadcasted_iota(jnp.int32, (1, cap), 1) < size_ref[0]
    back = jnp.where(live, back, 0.0)
    if len(outs) == 1:
        outs[0][...] = back
        return
    full_ref[...] = back
    each, _, width = outs[0].shape
    chunks = []
    for offset in order:
        first = pl.multiple_of(jnp.bitwise_xor(place_ref[0], offset) * width, width)
        chunks.append(full_ref[:, pl.ds(first, width)])
    for place in range(each):
        outs[0][place] = chunks[place]
    for place, message in enumerate(pack_chunks(chunks[each:])):
        outs[1 + place // each][place % each] = message


def apply_samples(genotypes, sizes, place, gathered, order, normalise, scale):
    samples, cap = genotypes.shape
    if len(gathered) > 1:
        each, rows, width = gathered[0].shape
        size = TILES * LANES
        outs = [jax.ShapeDtypeStruct((each, size, width), jnp.float32)]
        outs += [jax.ShapeDtypeStruct((each, rows, width), jnp.int32)] * (len(gathered) - 1)
    else:
        size = gathered[0].shape[0]
        outs = [jax.ShapeDtypeStruct((size, cap), jnp.float32)]
    scalar, vmem = pl.BlockSpec(memory_space=pltpu.SMEM), pl.BlockSpec(memory_space=pltpu.VMEM)
    return pl.pallas_call(
        functools.partial(apply_kernel, order, normalise, scale, len(gathered)),
        in_specs=[scalar, scalar, pl.BlockSpec(memory_space=pl.ANY)] + [vmem] * len(gathered),
        out_specs=[vmem] * len(outs),
        out_shape=outs,
        scratch_shapes=[
            pltpu.VMEM((size, cap), jnp.float32),
            pltpu.VMEM((size, 2 * size), jnp.float32),
            pltpu.VMEM((samples, cap), jnp.bfloat16),
            pltpu.SemaphoreType.DMA,
        ],
        compiler_params=pltpu.CompilerParams(vmem_limit_bytes=VMEM_LIMIT),
    )(place, sizes, genotypes, *gathered)


def lane_splat(tile, lane):
    return jnp.broadcast_to(tile[:, lane : lane + 1], (SUBLANES, LANES))


def row_splat(tile, row):
    return jnp.broadcast_to(tile[row : row + 1, :], (SUBLANES, LANES))


def inverse_factor(work_ref, size, panel, first_top=0, last_top=None):
    tiles = 2 * size // LANES
    below = lax.broadcasted_iota(jnp.int32, (SUBLANES, LANES), 0)
    groups = panel // SUBLANES
    for top in range(first_top, size if last_top is None else last_top, panel):
        active = [
            tile
            for tile in range(tiles)
            if (top // LANES <= tile < size // LANES)
            or (size // LANES <= tile <= size // LANES + (top + panel - 1) // LANES)
        ]
        rows = [
            {
                tile: work_ref[top + SUBLANES * group : top + SUBLANES * (group + 1), tile * LANES : (tile + 1) * LANES]
                for tile in active
            }
            for group in range(groups)
        ]
        for block in range(groups):
            base = top + SUBLANES * block
            columns = {
                group: [lane_splat(rows[group][base // LANES], base % LANES + lane) for lane in range(SUBLANES)]
                for group in range(block, groups)
            }
            for step in range(SUBLANES):
                pivot = row_splat(columns[block][step], step)
                root = lax.rsqrt(pivot)
                factor = {group: columns[group][step] * root for group in range(block, groups)}
                for later in range(step + 1, SUBLANES):
                    weight = row_splat(factor[block], later)
                    for group in range(block, groups):
                        columns[group][later] = columns[group][later] - factor[group] * weight
                lower = jnp.where(below > step, factor[block], 0.0)
                for tile in active:
                    line = row_splat(rows[block][tile], step) * root
                    rows[block][tile] = jnp.where(
                        below == step, line, rows[block][tile] - lower * line
                    )
                    for group in range(block + 1, groups):
                        rows[group][tile] = rows[group][tile] - factor[group] * line
        for group in range(groups):
            for tile in active:
                work_ref[top + SUBLANES * group : top + SUBLANES * (group + 1), tile * LANES : (tile + 1) * LANES] = rows[
                    group
                ][tile]
        rest = top + panel
        if rest < size:
            first, last = active[0] * LANES, (active[-1] + 1) * LANES
            lines = work_ref[top:rest, first:last]
            high, middle, low = split_pieces(work_ref[top:rest, rest // LANES * LANES : size], 3)
            above, between, below_ = split_pieces(lines, 3)
            update = lax.dot_general(
                jnp.concatenate([high, high, high, middle, middle, low], axis=0),
                jnp.concatenate([above, between, below_, above, between, above], axis=0),
                (((0,), (0,)), ((), ())),
                preferred_element_type=jnp.float32,
            )
            work_ref[rest:, first:last] -= update[rest % LANES :]


def start_factor(work_ref, inner):
    size = inner.shape[0]
    work_ref[:, :size] = inner
    row = lax.broadcasted_iota(jnp.int32, (size, size), 0)
    column = lax.broadcasted_iota(jnp.int32, (size, size), 1)
    work_ref[:, size:] = jnp.where(row == column, 1.0, 0.0)


def finish_factor(work_ref):
    size = work_ref.shape[0]
    row = lax.broadcasted_iota(jnp.int32, (size, size), 0)
    column = lax.broadcasted_iota(jnp.int32, (size, size), 1)
    return jnp.where(row >= column, work_ref[:, size:], 0.0)


def rows_dot(left, right):
    return lax.dot_general(left, right, (((1,), (1,)), ((), ())), preferred_element_type=jnp.float32)


def rows_inner(value):
    high, middle, low = split_pieces(value, 3)
    mixed = rows_dot(high, middle) + rows_dot(high, low)
    return rows_dot(high, high) + rows_dot(middle, middle) + (mixed + mixed.T)


def fold_symmetric(value, folded_ref, height):
    half = value.shape[0] // 2
    row = lax.broadcasted_iota(jnp.int32, (half, half), 0)
    column = lax.broadcasted_iota(jnp.int32, (half, half), 1)
    corner = value[half:, half:]
    both = jnp.where(row >= column, value[:half, :half], corner)
    diagonal = jnp.sum(jnp.where(row == column, corner, 0.0), axis=0, keepdims=True)
    quarter = half // 2
    for place in range(4):
        source = value[half:, :half] if place < 2 else both
        folded_ref[place, :quarter] = source[place % 2 * quarter : (place % 2 + 1) * quarter]
        folded_ref[place, quarter:] = jnp.broadcast_to(diagonal, (SUBLANES, half))


def unfold_symmetric(parts):
    quarter = parts[0].shape[0] - SUBLANES
    half = 2 * quarter
    row = lax.broadcasted_iota(jnp.int32, (half, half), 0)
    column = lax.broadcasted_iota(jnp.int32, (half, half), 1)
    left = jnp.concatenate([parts[0][:quarter], parts[1][:quarter]], axis=0)
    both = jnp.concatenate([parts[2][:quarter], parts[3][:quarter]], axis=0)
    turned = both.T
    corner = jnp.where(row == column, parts[3][quarter : quarter + 1], jnp.where(row < column, both, turned))
    upper = jnp.concatenate([jnp.where(row >= column, both, turned), left.T], axis=1)
    return jnp.concatenate([upper, jnp.concatenate([left, corner], axis=1)], axis=0)


def project_kernel(order, sources, quarter_ref, place_ref, rows_ref, *refs):
    refs, (inner_ref, *outs), (full_ref, folded_ref, held_ref, sem) = refs[:sources], refs[sources:-4], refs[-4:]
    size = full_ref.shape[0]
    copy = pltpu.make_async_copy(rows_ref, held_ref, sem)
    copy.start()
    load_all(order, place_ref, refs, full_ref)
    image = full_ref[...]
    inner_ref[...] = rows_inner(image)
    split = jnp.concatenate(split_pieces(image, PIECES), axis=0)
    copy.wait()
    sampled = rows_dot(split, held_ref[...])
    sampled = sum(sampled[piece * size : (piece + 1) * size] for piece in range(PIECES))
    high, low = split_pieces(sampled, PIECES)
    mixed = rows_dot(high, low)
    fold_symmetric(rows_dot(high, high) + (mixed + mixed.T), folded_ref, size)
    for offset, out_ref in enumerate(outs):
        out_ref[...] = folded_ref[jnp.bitwise_xor(quarter_ref[0], offset)]


def project(genotypes, quarter, place, gathered, order, size):
    samples, cap = genotypes.shape
    scalar, vmem = pl.BlockSpec(memory_space=pltpu.SMEM), pl.BlockSpec(memory_space=pltpu.VMEM)
    part = (size // 4 + SUBLANES, size // 2)
    outs = [(size, size)] + [part] * 4
    return pl.pallas_call(
        functools.partial(project_kernel, order, len(gathered)),
        in_specs=[scalar, scalar, pl.BlockSpec(memory_space=pl.ANY)] + [vmem] * len(gathered),
        out_specs=[vmem] * len(outs),
        out_shape=[jax.ShapeDtypeStruct(shape, jnp.float32) for shape in outs],
        scratch_shapes=[
            pltpu.VMEM((size, cap), jnp.float32),
            pltpu.VMEM((4,) + part, jnp.float32),
            pltpu.VMEM((samples, cap), jnp.bfloat16),
            pltpu.SemaphoreType.DMA,
        ],
        compiler_params=pltpu.CompilerParams(vmem_limit_bytes=VMEM_LIMIT),
    )(quarter, place, genotypes, *gathered)


def second_kernel(gain, first, last, *refs):
    (source_ref, *own_ref), (work_ref, *basis_ref) = refs[: len(refs) // 2], refs[len(refs) // 2 :]
    if first == 0:
        start_factor(work_ref, source_ref[...])
    else:
        work_ref[...] = source_ref[...]
    inverse_factor(work_ref, work_ref.shape[0], PANEL, first, last)
    if own_ref:
        factor = finish_factor(work_ref)
        own = jnp.dot(factor, own_ref[0][...], precision=HIGHEST, preferred_element_type=jnp.float32)
        basis_ref[0][...] = own.T * gain


def second_factor(source, first, last, own=None, gain=1.0):
    size = source.shape[0]
    vmem = pl.BlockSpec(memory_space=pltpu.VMEM)
    shapes = [(size, 2 * size)] + ([] if own is None else [own.shape[::-1]])
    outs = pl.pallas_call(
        functools.partial(second_kernel, gain, first, last),
        in_specs=[vmem] * len(shapes),
        out_specs=[vmem] * len(shapes),
        out_shape=[jax.ShapeDtypeStruct(shape, jnp.float32) for shape in shapes],
        compiler_params=pltpu.CompilerParams(vmem_limit_bytes=VMEM_LIMIT),
        cost_estimate=FACTOR_COST,
    )(source, *([] if own is None else [own]))
    return outs[0] if own is None else outs


def finish_kernel(scale, quarter_ref, factor_ref, *refs):
    parts, (out_ref, trace_ref, folded_ref) = refs[:4], refs[4:]
    for offset in range(4):
        folded_ref[jnp.bitwise_xor(quarter_ref[0], offset)] = parts[offset][...]
    cross = unfold_symmetric([folded_ref[place] for place in range(4)])
    factor = finish_factor(factor_ref)
    half = jnp.dot(factor, cross, precision=HIGHEST, preferred_element_type=jnp.float32)
    result = scale * lax.dot_general(
        half, factor, (((1,), (1,)), ((), ())), precision=HIGHEST, preferred_element_type=jnp.float32
    )
    out_ref[...] = result
    row = lax.broadcasted_iota(jnp.int32, result.shape, 0)
    column = lax.broadcasted_iota(jnp.int32, result.shape, 1)
    trace_ref[...] = jnp.broadcast_to(jnp.sum(jnp.where(row == column, result, 0.0)), trace_ref.shape)


def finish(quarter, factor, parts, scale):
    vmem = pl.BlockSpec(memory_space=pltpu.VMEM)
    return pl.pallas_call(
        functools.partial(finish_kernel, scale),
        in_specs=[pl.BlockSpec(memory_space=pltpu.SMEM)] + [vmem] * 5,
        out_specs=[vmem] * 2,
        out_shape=[
            jax.ShapeDtypeStruct((factor.shape[0],) * 2, jnp.float32),
            jax.ShapeDtypeStruct((SUBLANES, LANES), jnp.float32),
        ],
        scratch_shapes=[pltpu.VMEM((4,) + parts[0].shape, jnp.float32)],
        compiler_params=pltpu.CompilerParams(vmem_limit_bytes=VMEM_LIMIT),
    )(quarter, factor, *parts)


def to_natural(gathered, order, me):
    places = jnp.argsort(jnp.array(order, jnp.int32))
    mine = jnp.bitwise_xor(jnp.arange(len(order), dtype=jnp.int32), me)
    stacked = jnp.concatenate(gathered, axis=0)[places][mine]
    return jnp.transpose(stacked, (1, 0, 2)).reshape(stacked.shape[1], -1)


def to_relative(rows, order, me, width, parts):
    chunks = jnp.transpose(rows.reshape(rows.shape[0], -1, width), (1, 0, 2))
    return jnp.split(chunks[jnp.bitwise_xor(jnp.array(order, jnp.int32), me)], parts, axis=0)


def body(genotypes, sizes, start):
    groups = lax.axis_size("smp")
    dosages = genotypes[0]
    samples, cap = dosages.shape
    width, size = start.shape[1:]
    scale = 1.0 / (samples * groups)
    me = lax.axis_index("smp")
    place = me.reshape(1).astype(jnp.int32)
    stages = stage_bits(groups)
    order = relative_order(stages)
    packed = width == LANES and size == TILES * LANES

    def gather(message):
        gathered = gather_chunks(message, groups)
        return gathered if packed else [to_natural(gathered, order, me)]

    def apply(message, normalise):
        outs = apply_samples(dosages, sizes, place, gather(message), order, normalise, scale)
        if not packed:
            outs = to_relative(outs[0], order, me, width, len(offsets(stages[0])))
        return reduce_chunks(outs[0], outs[1:], groups, packed)

    if packed:
        message = encode(place, sizes, start[0])
    else:
        row = me * width + lax.broadcasted_iota(jnp.int32, (width, size), 0)
        message = jnp.where(row < sizes[0], start[0], 0.0).T[None]
    _, message = apply(message, False)
    own, message = apply(message, True)
    quarter = jnp.bitwise_and(place, 3)
    inner, *quarters = project(dosages, quarter, place, gather(message), order, size)
    cuts = [0, size // 4 + size // 8, size - size // 4, size]
    beside = [
        lambda _: second_factor(inner, cuts[0], cuts[1]),
        lambda work: second_factor(work, cuts[1], cuts[2]),
        lambda work: second_factor(work, cuts[2], cuts[3], own[0], math.sqrt(cap)),
    ]
    quarters, (second, basis) = sum_quarters(quarters, groups, beside)
    rayleigh, trace = finish(quarter, second, quarters, scale)
    blocks = lax.axis_size("blk")
    total = trace
    for shift in range(1, blocks):
        total = total + lax.ppermute(trace, "blk", [(block, (block + shift) % blocks) for block in range(blocks)])
    scaled = rayleigh * (genotypes.shape[0] * blocks * size / total[0, 0])
    return basis[None], scaled[None]


def solution(mesh):
    return jax.shard_map(
        body,
        mesh=mesh,
        in_specs=(P("blk", "smp", None), P("blk"), P("blk", "smp", None)),
        out_specs=(P("blk", "smp", None), P("blk", None, None)),
        check_vma=False,
    )
```

```python
import functools
import math

import jax
import jax.numpy as jnp
from jax import lax
from jax.experimental import pallas as pl
from jax.experimental.pallas import tpu as pltpu
from jax.sharding import PartitionSpec as P

LANES = 128
SUBLANES = 8
PANEL = 32
PIECES = 2
CODES = 128
STEPS = 65535.0
LEAST = 2.0**-90
VMEM_LIMIT = 32 * 1024 * 1024
VMEM_SMALL = 8 * 1024 * 1024
HIGHEST = lax.Precision.HIGHEST
FACTOR_COST = pl.CostEstimate(flops=4_000_000_000, bytes_accessed=4 << 20, transcendentals=0)


def stage_bits(groups):
    count = groups.bit_length() - 1
    return [list(range(count))[place : place + 2] for place in range(0, count, 2)]


def offsets(bits):
    found = [0]
    for bit in bits:
        found = found + [value ^ (1 << bit) for value in found]
    return found


def relative_order(stages):
    order = [0]
    for bits in reversed(stages):
        order = [high ^ low for high in offsets(bits) for low in order]
    return order


def exchange(value, groups, offset):
    return lax.ppermute(value, "smp", [(device, device ^ offset) for device in range(groups)])


def reduce_chunks(keep, sends, groups, packed):
    stages = stage_bits(groups)
    for depth, bits in enumerate(stages):
        arrived = [exchange(send, groups, span) for send, span in zip(sends, offsets(bits)[1:])]
        parts = len(offsets(stages[depth + 1])) if depth + 1 < len(stages) else 1
        if packed:
            keep, *sends = combine(keep, arrived, parts)
        else:
            keep, *sends = jnp.split(keep + sum(arrived), parts, axis=0)
    return keep, sends[0] if packed else keep


def stack_kernel(*refs):
    first = 0
    for ref in refs[:-1]:
        refs[-1][first : first + ref.shape[0]] = ref[...]
        first += ref.shape[0]


def stack(parts):
    if parts[0].dtype != jnp.int32:
        return jnp.concatenate(parts, axis=0)
    vmem = pl.BlockSpec(memory_space=pltpu.VMEM)
    shape = (len(parts) * parts[0].shape[0],) + parts[0].shape[1:]
    return pl.pallas_call(
        stack_kernel,
        in_specs=[vmem] * len(parts),
        out_specs=vmem,
        out_shape=jax.ShapeDtypeStruct(shape, parts[0].dtype),
        compiler_params=pltpu.CompilerParams(vmem_limit_bytes=VMEM_SMALL),
    )(*parts)


def gather_chunks(message, groups):
    stages = stage_bits(groups)
    for bits in reversed(stages[1:]):
        message = stack([message] + [exchange(message, groups, span) for span in offsets(bits)[1:]])
    return [message] + [exchange(message, groups, span) for span in offsets(stages[0])[1:]]


def pair_sum(parts):
    while len(parts) > 1:
        parts = [left + right for left, right in zip(parts[::2], parts[1::2])]
    return parts[0]


def sum_quarters(quarters, groups, beside):
    stages = stage_bits(groups)
    spans = offsets(stages[0])
    steps = list(beside)
    state = steps.pop(0)(None)
    arrived = [exchange(part, groups, span) for part, span in zip(quarters[1:], spans[1:])]
    arrived, state = lax.optimization_barrier((arrived, state))
    total = pair_sum([quarters[0]] + arrived)
    for bits in stages[1:]:
        if len(steps) > 1:
            state = steps.pop(0)(state)
        arrived = [exchange(total, groups, span) for span in offsets(bits)[1:]]
        arrived, state = lax.optimization_barrier((arrived, state))
        total = pair_sum([total] + arrived)
    for step in steps:
        state = step(state)
    return [total] + [exchange(total, groups, span) for span in spans[1:]], state


TILES = 2
FINE = 28
NIBBLES = 4
PACKED = TILES * LANES // 2 + SUBLANES


def row_scales(peaks):
    codes = jnp.ceil(jnp.log2(jnp.maximum(peaks, LEAST)) * CODES) + 1.0
    return codes, jnp.exp2(codes * (1.0 / CODES))


def gather_columns(columns):
    lane = lax.broadcasted_iota(jnp.int32, (LANES, LANES), 1)
    matrix = jnp.zeros((LANES, LANES), jnp.float32)
    for place, column in enumerate(columns):
        matrix = jnp.where(lane == place, column, matrix)
    return matrix


def pack_chunks(chunks):
    peaks = [jnp.max(jnp.abs(chunk), axis=1, keepdims=True) for chunk in chunks]
    codes, scales = row_scales(
        gather_columns([peak[tile * LANES : (tile + 1) * LANES] for peak in peaks for tile in range(TILES)])
    )
    factors = STEPS / scales
    lines = codes.T.astype(jnp.int32)
    sub = lax.broadcasted_iota(jnp.int32, (SUBLANES, LANES), 0)
    half = TILES * LANES // 2
    messages = []
    for place, chunk in enumerate(chunks):
        factor = jnp.concatenate(
            [factors[:, TILES * place + tile : TILES * place + tile + 1] for tile in range(TILES)], axis=0
        )
        scaled = chunk * factor
        fine = FINE * SUBLANES
        value = jnp.concatenate(
            [jnp.round(scaled[:fine]).astype(jnp.int32), 2 * jnp.round(0.5 * scaled[fine:]).astype(jnp.int32)], axis=0
        )
        high = jnp.clip(jnp.right_shift(value, 1), -32768, 32767)
        words = jnp.bitwise_or(jnp.left_shift(high[:half], 16), jnp.bitwise_and(high[half:], 0xFFFF))
        first = jnp.broadcast_to(lines[TILES * place : TILES * place + 1], (SUBLANES, LANES))
        second = jnp.broadcast_to(lines[TILES * place + 1 : TILES * place + 2], (SUBLANES, LANES))
        code = jnp.where(sub < NIBBLES, first, second)
        nibble = jnp.right_shift(code, NIBBLES * jnp.bitwise_and(sub, NIBBLES - 1))
        extra = jnp.left_shift(nibble, FINE)
        for group in range(FINE):
            bits = jnp.bitwise_and(value[group * SUBLANES : (group + 1) * SUBLANES], 1)
            extra = jnp.bitwise_or(extra, jnp.left_shift(bits, group))
        messages.append(jnp.concatenate([words, extra], axis=0))
    return messages


def unpack_chunks(messages):
    half = TILES * LANES // 2
    lines = []
    for message in messages:
        nibble = jnp.bitwise_and(jnp.right_shift(message[half:], FINE), 15)
        for tile in range(TILES):
            code = jnp.left_shift(nibble[tile * NIBBLES + NIBBLES - 1 : (tile + 1) * NIBBLES], 28)
            code = jnp.right_shift(code, 28 - NIBBLES * (NIBBLES - 1))
            for place in range(NIBBLES - 1):
                line = nibble[tile * NIBBLES + place : tile * NIBBLES + place + 1]
                code = jnp.bitwise_or(code, jnp.left_shift(line, NIBBLES * place))
            lines.append(code.astype(jnp.float32))
    lines.append(jnp.zeros((LANES - len(lines), LANES), jnp.float32))
    scales = (jnp.exp2(jnp.concatenate(lines, axis=0) * (1.0 / CODES)) * (1.0 / STEPS)).T

    def make(place, tile):
        words, extra = messages[place][:half], messages[place][half:]
        high = jnp.right_shift(words if tile == 0 else jnp.left_shift(words, 16), 16)
        low = [
            jnp.bitwise_and(jnp.right_shift(extra, group), 1) if group < FINE else jnp.zeros_like(extra)
            for group in range(tile * LANES // SUBLANES, (tile + 1) * LANES // SUBLANES)
        ]
        value = jnp.bitwise_or(jnp.left_shift(high, 1), jnp.concatenate(low, axis=0))
        column = TILES * place + tile
        return value.astype(jnp.float32) * scales[:, column : column + 1]

    return [
        [functools.partial(make, place, tile) for tile in range(TILES)] for place in range(len(messages))
    ]


def encode_kernel(place_ref, size_ref, start_ref, out_ref):
    width, size = start_ref.shape
    row = place_ref[0] * width + lax.broadcasted_iota(jnp.int32, (width, size), 0)
    value = jnp.where(row < size_ref[0], start_ref[...], 0.0)
    out_ref[0] = pack_chunks([value.T])[0]


def encode(place, sizes, start):
    width, size = start.shape
    scalar, vmem = pl.BlockSpec(memory_space=pltpu.SMEM), pl.BlockSpec(memory_space=pltpu.VMEM)
    return pl.pallas_call(
        encode_kernel,
        in_specs=[scalar, scalar, vmem],
        out_specs=vmem,
        out_shape=jax.ShapeDtypeStruct((1, PACKED, width), jnp.int32),
    )(place, sizes, start)


def combine_kernel(count, parts, keep_ref, *refs):
    arrived, own_ref, sends = refs[:count], refs[count], refs[count + 1 :]
    chunks = keep_ref.shape[0]
    tiles = unpack_chunks([part[place] for place in range(chunks) for part in arrived])
    totals = []
    for place in range(chunks):
        total = keep_ref[place]
        for source in range(count):
            total = total + jnp.concatenate([tile() for tile in tiles[place * count + source]], axis=0)
        totals.append(total)
    width = chunks // parts
    for place in range(width):
        own_ref[place] = totals[place]
    first = 0 if parts == 1 else width
    for place, message in enumerate(pack_chunks(totals[first:])):
        sends[place // width][place % width] = message


def combine(keep, arrived, parts):
    chunks, rows, lanes = keep.shape
    width = chunks // parts
    vmem = pl.BlockSpec(memory_space=pltpu.VMEM)
    outs = [jax.ShapeDtypeStruct((width, rows, lanes), jnp.float32)]
    outs += [jax.ShapeDtypeStruct((width, PACKED, lanes), jnp.int32)] * max(parts - 1, 1)
    return pl.pallas_call(
        functools.partial(combine_kernel, len(arrived), parts),
        in_specs=[vmem] * (1 + len(arrived)),
        out_specs=[vmem] * len(outs),
        out_shape=outs,
        compiler_params=pltpu.CompilerParams(vmem_limit_bytes=VMEM_SMALL),
    )(keep, *arrived)


def split_pieces(value, pieces):
    parts = []
    rest = value
    for piece in range(pieces):
        part = rest.astype(jnp.bfloat16)
        parts.append(part)
        if piece + 1 < pieces:
            rest = rest - part.astype(jnp.float32)
    return parts


def hold_kernel(after_ref, rows_ref, out_ref, sem):
    copy = pltpu.make_async_copy(rows_ref, out_ref, sem)
    copy.start()
    copy.wait()


def hold(genotypes, after):
    anywhere = pl.BlockSpec(memory_space=pl.ANY)
    return pl.pallas_call(
        hold_kernel,
        in_specs=[anywhere, anywhere],
        out_specs=pl.BlockSpec(memory_space=pltpu.VMEM),
        out_shape=jax.ShapeDtypeStruct(genotypes.shape, genotypes.dtype),
        scratch_shapes=[pltpu.SemaphoreType.DMA],
        compiler_params=pltpu.CompilerParams(vmem_limit_bytes=VMEM_SMALL),
        cost_estimate=FACTOR_COST,
    )(after, genotypes)


def load_all(order, place_ref, refs, full_ref):
    if len(refs) == 1:
        full_ref[...] = refs[0][...]
        return
    width = refs[0].shape[2]
    each = refs[0].shape[0]
    tiles = unpack_chunks([ref[place] for ref in refs for place in range(each)])
    for offset, chunk in zip(order, tiles):
        first = pl.multiple_of(jnp.bitwise_xor(place_ref[0], offset) * width, width)
        for part, tile in enumerate(chunk):
            full_ref[pl.ds(part * LANES, LANES), pl.ds(first, width)] = tile()


def apply_kernel(order, normalise, scale, sources, place_ref, size_ref, rows_ref, *refs):
    refs, outs, (full_ref, work_ref) = refs[:sources], refs[sources:-2], refs[-2:]
    size, cap = full_ref.shape
    load_all(order, place_ref, refs, full_ref)
    value = full_ref[...]
    if normalise:
        start_factor(work_ref, rows_inner(value))
        inverse_factor(work_ref, size, PANEL)
        value = jnp.dot(finish_factor(work_ref), value, precision=HIGHEST, preferred_element_type=jnp.float32)
    split = jnp.concatenate(split_pieces(value, PIECES), axis=0)
    image = rows_dot(split, rows_ref[...])
    image = sum(image[piece * size : (piece + 1) * size] for piece in range(PIECES)) * scale
    split = jnp.concatenate(split_pieces(image, PIECES), axis=0)
    back = jnp.dot(split, rows_ref[...], preferred_element_type=jnp.float32)
    back = sum(back[piece * size : (piece + 1) * size] for piece in range(PIECES))
    live = lax.broadcasted_iota(jnp.int32, (1, cap), 1) < size_ref[0]
    back = jnp.where(live, back, 0.0)
    if len(outs) == 1:
        outs[0][...] = back
        return
    full_ref[...] = back
    each, _, width = outs[0].shape
    chunks = []
    for offset in order:
        first = pl.multiple_of(jnp.bitwise_xor(place_ref[0], offset) * width, width)
        chunks.append(full_ref[:, pl.ds(first, width)])
    for place in range(each):
        outs[0][place] = chunks[place]
    for place, message in enumerate(pack_chunks(chunks[each:])):
        outs[1 + place // each][place % each] = message


def apply_samples(genotypes, sizes, place, gathered, order, normalise, scale):
    samples, cap = genotypes.shape
    if len(gathered) > 1:
        each, rows, width = gathered[0].shape
        size = TILES * LANES
        outs = [jax.ShapeDtypeStruct((each, size, width), jnp.float32)]
        outs += [jax.ShapeDtypeStruct((each, rows, width), jnp.int32)] * (len(gathered) - 1)
    else:
        size = gathered[0].shape[0]
        outs = [jax.ShapeDtypeStruct((size, cap), jnp.float32)]
    scalar, vmem = pl.BlockSpec(memory_space=pltpu.SMEM), pl.BlockSpec(memory_space=pltpu.VMEM)
    return pl.pallas_call(
        functools.partial(apply_kernel, order, normalise, scale, len(gathered)),
        in_specs=[scalar, scalar, vmem] + [vmem] * len(gathered),
        out_specs=[vmem] * len(outs),
        out_shape=outs,
        scratch_shapes=[
            pltpu.VMEM((size, cap), jnp.float32),
            pltpu.VMEM((size, 2 * size), jnp.float32),
        ],
        compiler_params=pltpu.CompilerParams(vmem_limit_bytes=VMEM_LIMIT),
    )(place, sizes, genotypes, *gathered)


def lane_splat(tile, lane):
    return jnp.broadcast_to(tile[:, lane : lane + 1], (SUBLANES, LANES))


def row_splat(tile, row):
    return jnp.broadcast_to(tile[row : row + 1, :], (SUBLANES, LANES))


def inverse_factor(work_ref, size, panel, first_top=0, last_top=None):
    tiles = 2 * size // LANES
    below = lax.broadcasted_iota(jnp.int32, (SUBLANES, LANES), 0)
    groups = panel // SUBLANES
    for top in range(first_top, size if last_top is None else last_top, panel):
        active = [
            tile
            for tile in range(tiles)
            if (top // LANES <= tile < size // LANES)
            or (size // LANES <= tile <= size // LANES + (top + panel - 1) // LANES)
        ]
        rows = [
            {
                tile: work_ref[top + SUBLANES * group : top + SUBLANES * (group + 1), tile * LANES : (tile + 1) * LANES]
                for tile in active
            }
            for group in range(groups)
        ]
        for block in range(groups):
            base = top + SUBLANES * block
            columns = {
                group: [lane_splat(rows[group][base // LANES], base % LANES + lane) for lane in range(SUBLANES)]
                for group in range(block, groups)
            }
            for step in range(SUBLANES):
                pivot = row_splat(columns[block][step], step)
                root = lax.rsqrt(pivot)
                factor = {group: columns[group][step] * root for group in range(block, groups)}
                for later in range(step + 1, SUBLANES):
                    weight = row_splat(factor[block], later)
                    for group in range(block, groups):
                        columns[group][later] = columns[group][later] - factor[group] * weight
                lower = jnp.where(below > step, factor[block], 0.0)
                for tile in active:
                    line = row_splat(rows[block][tile], step) * root
                    rows[block][tile] = jnp.where(
                        below == step, line, rows[block][tile] - lower * line
                    )
                    for group in range(block + 1, groups):
                        rows[group][tile] = rows[group][tile] - factor[group] * line
        for group in range(groups):
            for tile in active:
                work_ref[top + SUBLANES * group : top + SUBLANES * (group + 1), tile * LANES : (tile + 1) * LANES] = rows[
                    group
                ][tile]
        rest = top + panel
        if rest < size:
            first, last = active[0] * LANES, (active[-1] + 1) * LANES
            lines = work_ref[top:rest, first:last]
            high, middle, low = split_pieces(work_ref[top:rest, rest // LANES * LANES : size], 3)
            above, between, below_ = split_pieces(lines, 3)
            update = lax.dot_general(
                jnp.concatenate([high, high, high, middle, middle, low], axis=0),
                jnp.concatenate([above, between, below_, above, between, above], axis=0),
                (((0,), (0,)), ((), ())),
                preferred_element_type=jnp.float32,
            )
            work_ref[rest:, first:last] -= update[rest % LANES :]


def start_factor(work_ref, inner):
    size = inner.shape[0]
    work_ref[:, :size] = inner
    row = lax.broadcasted_iota(jnp.int32, (size, size), 0)
    column = lax.broadcasted_iota(jnp.int32, (size, size), 1)
    work_ref[:, size:] = jnp.where(row == column, 1.0, 0.0)


def finish_factor(work_ref):
    size = work_ref.shape[0]
    row = lax.broadcasted_iota(jnp.int32, (size, size), 0)
    column = lax.broadcasted_iota(jnp.int32, (size, size), 1)
    return jnp.where(row >= column, work_ref[:, size:], 0.0)


def rows_dot(left, right):
    return lax.dot_general(left, right, (((1,), (1,)), ((), ())), preferred_element_type=jnp.float32)


def rows_inner(value):
    high, middle, low = split_pieces(value, 3)
    mixed = rows_dot(high, middle) + rows_dot(high, low)
    return rows_dot(high, high) + rows_dot(middle, middle) + (mixed + mixed.T)


def fold_symmetric(value, folded_ref, height):
    half = value.shape[0] // 2
    row = lax.broadcasted_iota(jnp.int32, (half, half), 0)
    column = lax.broadcasted_iota(jnp.int32, (half, half), 1)
    corner = value[half:, half:]
    both = jnp.where(row >= column, value[:half, :half], corner)
    diagonal = jnp.sum(jnp.where(row == column, corner, 0.0), axis=0, keepdims=True)
    quarter = half // 2
    for place in range(4):
        source = value[half:, :half] if place < 2 else both
        folded_ref[place, :quarter] = source[place % 2 * quarter : (place % 2 + 1) * quarter]
        folded_ref[place, quarter:] = jnp.broadcast_to(diagonal, (SUBLANES, half))


def unfold_symmetric(parts):
    quarter = parts[0].shape[0] - SUBLANES
    half = 2 * quarter
    row = lax.broadcasted_iota(jnp.int32, (half, half), 0)
    column = lax.broadcasted_iota(jnp.int32, (half, half), 1)
    left = jnp.concatenate([parts[0][:quarter], parts[1][:quarter]], axis=0)
    both = jnp.concatenate([parts[2][:quarter], parts[3][:quarter]], axis=0)
    turned = both.T
    corner = jnp.where(row == column, parts[3][quarter : quarter + 1], jnp.where(row < column, both, turned))
    upper = jnp.concatenate([jnp.where(row >= column, both, turned), left.T], axis=1)
    return jnp.concatenate([upper, jnp.concatenate([left, corner], axis=1)], axis=0)


def project_kernel(order, sources, quarter_ref, place_ref, rows_ref, *refs):
    refs, (inner_ref, *outs), (full_ref, folded_ref) = refs[:sources], refs[sources:-2], refs[-2:]
    size = full_ref.shape[0]
    load_all(order, place_ref, refs, full_ref)
    image = full_ref[...]
    inner_ref[...] = rows_inner(image)
    split = jnp.concatenate(split_pieces(image, PIECES), axis=0)
    sampled = rows_dot(split, rows_ref[...])
    sampled = sum(sampled[piece * size : (piece + 1) * size] for piece in range(PIECES))
    high, low = split_pieces(sampled, PIECES)
    mixed = rows_dot(high, low)
    fold_symmetric(rows_dot(high, high) + (mixed + mixed.T), folded_ref, size)
    for offset, out_ref in enumerate(outs):
        out_ref[...] = folded_ref[jnp.bitwise_xor(quarter_ref[0], offset)]


def project(genotypes, quarter, place, gathered, order, size):
    samples, cap = genotypes.shape
    scalar, vmem = pl.BlockSpec(memory_space=pltpu.SMEM), pl.BlockSpec(memory_space=pltpu.VMEM)
    part = (size // 4 + SUBLANES, size // 2)
    outs = [(size, size)] + [part] * 4
    return pl.pallas_call(
        functools.partial(project_kernel, order, len(gathered)),
        in_specs=[scalar, scalar, vmem] + [vmem] * len(gathered),
        out_specs=[vmem] * len(outs),
        out_shape=[jax.ShapeDtypeStruct(shape, jnp.float32) for shape in outs],
        scratch_shapes=[
            pltpu.VMEM((size, cap), jnp.float32),
            pltpu.VMEM((4,) + part, jnp.float32),
        ],
        compiler_params=pltpu.CompilerParams(vmem_limit_bytes=VMEM_LIMIT),
    )(quarter, place, genotypes, *gathered)


def second_kernel(first, last, source_ref, work_ref):
    if first == 0:
        start_factor(work_ref, source_ref[...])
    else:
        work_ref[...] = source_ref[...]
    inverse_factor(work_ref, work_ref.shape[0], PANEL, first, last)


def second_factor(source, first, last):
    size = source.shape[0]
    vmem = pl.BlockSpec(memory_space=pltpu.VMEM)
    return pl.pallas_call(
        functools.partial(second_kernel, first, last),
        in_specs=[vmem],
        out_specs=vmem,
        out_shape=jax.ShapeDtypeStruct((size, 2 * size), jnp.float32),
        compiler_params=pltpu.CompilerParams(vmem_limit_bytes=VMEM_LIMIT),
        cost_estimate=FACTOR_COST,
    )(source)


def basis_kernel(gain, factor_ref, own_ref, out_ref):
    own = jnp.dot(finish_factor(factor_ref), own_ref[...], precision=HIGHEST, preferred_element_type=jnp.float32)
    out_ref[...] = own.T * gain


def basis_rows(factor, own, gain):
    vmem = pl.BlockSpec(memory_space=pltpu.VMEM)
    return pl.pallas_call(
        functools.partial(basis_kernel, gain),
        in_specs=[vmem] * 2,
        out_specs=vmem,
        out_shape=jax.ShapeDtypeStruct(own.shape[::-1], jnp.float32),
        compiler_params=pltpu.CompilerParams(vmem_limit_bytes=VMEM_SMALL),
        cost_estimate=pl.CostEstimate(flops=1_000_000_000, bytes_accessed=1 << 20, transcendentals=0),
    )(factor, own)


def trace_kernel(scale, quarter_ref, factor_ref, *refs):
    parts, (half_ref, trace_ref, folded_ref) = refs[:4], refs[4:]
    for offset in range(4):
        folded_ref[jnp.bitwise_xor(quarter_ref[0], offset)] = parts[offset][...]
    cross = unfold_symmetric([folded_ref[place] for place in range(4)])
    factor = finish_factor(factor_ref)
    half = scale * jnp.dot(factor, cross, precision=HIGHEST, preferred_element_type=jnp.float32)
    half_ref[...] = half
    trace_ref[...] = jnp.broadcast_to(jnp.sum(half * factor), trace_ref.shape)


def trace_half(quarter, factor, parts, scale):
    vmem = pl.BlockSpec(memory_space=pltpu.VMEM)
    return pl.pallas_call(
        functools.partial(trace_kernel, scale),
        in_specs=[pl.BlockSpec(memory_space=pltpu.SMEM)] + [vmem] * 5,
        out_specs=[vmem] * 2,
        out_shape=[
            jax.ShapeDtypeStruct((factor.shape[0],) * 2, jnp.float32),
            jax.ShapeDtypeStruct((SUBLANES, LANES), jnp.float32),
        ],
        scratch_shapes=[pltpu.VMEM((4,) + parts[0].shape, jnp.float32)],
        compiler_params=pltpu.CompilerParams(vmem_limit_bytes=VMEM_SMALL),
    )(quarter, factor, *parts)


def finish_kernel(gain, half_ref, factor_ref, *refs):
    traces, out_ref = refs[:-1], refs[-1]
    total = sum(trace[:1, :1] for trace in traces)
    whole = lax.dot_general(
        half_ref[...],
        finish_factor(factor_ref),
        (((1,), (1,)), ((), ())),
        precision=HIGHEST,
        preferred_element_type=jnp.float32,
    )
    out_ref[...] = whole * (gain / total)


def finish(half, factor, traces, gain):
    vmem = pl.BlockSpec(memory_space=pltpu.VMEM)
    return pl.pallas_call(
        functools.partial(finish_kernel, gain),
        in_specs=[vmem] * (2 + len(traces)),
        out_specs=vmem,
        out_shape=jax.ShapeDtypeStruct(half.shape, jnp.float32),
        compiler_params=pltpu.CompilerParams(vmem_limit_bytes=VMEM_SMALL),
    )(half, factor, *traces)


def to_natural(gathered, order, me):
    places = jnp.argsort(jnp.array(order, jnp.int32))
    mine = jnp.bitwise_xor(jnp.arange(len(order), dtype=jnp.int32), me)
    stacked = jnp.concatenate(gathered, axis=0)[places][mine]
    return jnp.transpose(stacked, (1, 0, 2)).reshape(stacked.shape[1], -1)


def to_relative(rows, order, me, width, parts):
    chunks = jnp.transpose(rows.reshape(rows.shape[0], -1, width), (1, 0, 2))
    return jnp.split(chunks[jnp.bitwise_xor(jnp.array(order, jnp.int32), me)], parts, axis=0)


def body(genotypes, sizes, start):
    groups = lax.axis_size("smp")
    dosages = genotypes[0]
    samples, cap = dosages.shape
    width, size = start.shape[1:]
    scale = 1.0 / (samples * groups)
    me = lax.axis_index("smp")
    place = me.reshape(1).astype(jnp.int32)
    stages = stage_bits(groups)
    order = relative_order(stages)
    packed = width == LANES and size == TILES * LANES

    def gather(message):
        gathered = gather_chunks(message, groups)
        return gathered if packed else [to_natural(gathered, order, me)]

    def apply(message, normalise):
        outs = apply_samples(dosages, sizes, place, gather(message), order, normalise, scale)
        if not packed:
            outs = to_relative(outs[0], order, me, width, len(offsets(stages[0])))
        return reduce_chunks(outs[0], outs[1:], groups, packed)

    if packed:
        message = encode(place, sizes, start[0])
    else:
        row = me * width + lax.broadcasted_iota(jnp.int32, (width, size), 0)
        message = jnp.where(row < sizes[0], start[0], 0.0).T[None]
    dosages = hold(dosages, message)
    _, message = apply(message, False)
    own, message = apply(message, True)
    quarter = jnp.bitwise_and(place, 3)
    inner, *quarters = project(dosages, quarter, place, gather(message), order, size)
    cuts = [0, size // 4 + size // 8, size - size // 4, size]
    beside = [
        lambda _: second_factor(inner, cuts[0], cuts[1]),
        lambda work: second_factor(work, cuts[1], cuts[2]),
        lambda work: second_factor(work, cuts[2], cuts[3]),
    ]
    quarters, second = sum_quarters(quarters, groups, beside)
    halfway, trace = trace_half(quarter, second, quarters, scale)
    blocks = lax.axis_size("blk")
    traces = [trace] + [
        lax.ppermute(trace, "blk", [(block, (block + shift) % blocks) for block in range(blocks)])
        for shift in range(1, blocks)
    ]
    basis = basis_rows(second, own[0], math.sqrt(cap))
    scaled = finish(halfway, second, traces, float(genotypes.shape[0] * blocks * size))
    return basis[None], scaled[None]


def solution(mesh):
    return jax.shard_map(
        body,
        mesh=mesh,
        in_specs=(P("blk", "smp", None), P("blk"), P("blk", "smp", None)),
        out_specs=(P("blk", "smp", None), P("blk", None, None)),
        check_vma=False,
    )
```

```python
import functools
import math

import jax
import jax.numpy as jnp
from jax import lax
from jax.experimental import pallas as pl
from jax.experimental.pallas import tpu as pltpu
from jax.sharding import PartitionSpec as P

LANES = 128
SUBLANES = 8
PANEL = 32
PIECES = 2
CODES = 128
STEPS = 65535.0
LEAST = 2.0**-90
FINER = 64.0
WIDE_STEPS = 524287.0
WIDE = 168
VMEM_LIMIT = 32 * 1024 * 1024
VMEM_SMALL = 8 * 1024 * 1024
HIGHEST = lax.Precision.HIGHEST
FACTOR_COST = pl.CostEstimate(flops=4_000_000_000, bytes_accessed=4 << 20, transcendentals=0)


def stage_bits(groups):
    count = groups.bit_length() - 1
    return [list(range(count))[place : place + 2] for place in range(0, count, 2)]


def offsets(bits):
    found = [0]
    for bit in bits:
        found = found + [value ^ (1 << bit) for value in found]
    return found


def relative_order(stages):
    order = [0]
    for bits in reversed(stages):
        order = [high ^ low for high in offsets(bits) for low in order]
    return order


def exchange(value, groups, offset):
    return lax.ppermute(value, "smp", [(device, device ^ offset) for device in range(groups)])


def reduce_chunks(keep, sends, groups, packed):
    stages = stage_bits(groups)
    for depth, bits in enumerate(stages):
        arrived = [exchange(send, groups, span) for send, span in zip(sends, offsets(bits)[1:])]
        parts = len(offsets(stages[depth + 1])) if depth + 1 < len(stages) else 1
        if packed:
            keep, *sends = combine(keep, arrived, parts)
        else:
            keep, *sends = jnp.split(keep + sum(arrived), parts, axis=0)
    return keep, sends[0] if packed else keep


def stack_kernel(*refs):
    first = 0
    for ref in refs[:-1]:
        refs[-1][first : first + ref.shape[0]] = ref[...]
        first += ref.shape[0]


def stack(parts):
    if parts[0].dtype != jnp.int32:
        return jnp.concatenate(parts, axis=0)
    vmem = pl.BlockSpec(memory_space=pltpu.VMEM)
    shape = (len(parts) * parts[0].shape[0],) + parts[0].shape[1:]
    return pl.pallas_call(
        stack_kernel,
        in_specs=[vmem] * len(parts),
        out_specs=vmem,
        out_shape=jax.ShapeDtypeStruct(shape, parts[0].dtype),
        compiler_params=pltpu.CompilerParams(vmem_limit_bytes=VMEM_SMALL),
    )(*parts)


def gather_chunks(message, groups):
    stages = stage_bits(groups)
    for bits in reversed(stages[1:]):
        message = stack([message] + [exchange(message, groups, span) for span in offsets(bits)[1:]])
    return [message] + [exchange(message, groups, span) for span in offsets(stages[0])[1:]]


def pair_sum(parts):
    while len(parts) > 1:
        parts = [left + right for left, right in zip(parts[::2], parts[1::2])]
    return parts[0]


def sum_quarters(quarters, groups, beside):
    stages = stage_bits(groups)
    spans = offsets(stages[0])
    steps = list(beside)
    state = steps.pop(0)(None)
    arrived = [exchange(part, groups, span) for part, span in zip(quarters[1:], spans[1:])]
    arrived, state = lax.optimization_barrier((arrived, state))
    total = pair_sum([quarters[0]] + arrived)
    for bits in stages[1:]:
        if len(steps) > 1:
            state = steps.pop(0)(state)
        arrived = [exchange(total, groups, span) for span in offsets(bits)[1:]]
        arrived, state = lax.optimization_barrier((arrived, state))
        total = pair_sum([total] + arrived)
    for step in steps:
        state = step(state)
    return [total] + [exchange(total, groups, span) for span in spans[1:]], state


TILES = 2
FINE = 28
NIBBLES = 4
PACKED = TILES * LANES // 2 + SUBLANES


def row_scales(peaks):
    codes = jnp.ceil(jnp.log2(jnp.maximum(peaks, LEAST)) * CODES) + 1.0
    return codes, jnp.exp2(codes * (1.0 / CODES))


def gather_columns(columns):
    lane = lax.broadcasted_iota(jnp.int32, (LANES, LANES), 1)
    matrix = jnp.zeros((LANES, LANES), jnp.float32)
    for place, column in enumerate(columns):
        matrix = jnp.where(lane == place, column, matrix)
    return matrix


def pack_chunks(chunks):
    peaks = [jnp.max(jnp.abs(chunk), axis=1, keepdims=True) for chunk in chunks]
    codes, scales = row_scales(
        gather_columns([peak[tile * LANES : (tile + 1) * LANES] for peak in peaks for tile in range(TILES)])
    )
    factors = STEPS / scales
    lines = codes.T.astype(jnp.int32)
    sub = lax.broadcasted_iota(jnp.int32, (SUBLANES, LANES), 0)
    half = TILES * LANES // 2
    messages = []
    for place, chunk in enumerate(chunks):
        factor = jnp.concatenate(
            [factors[:, TILES * place + tile : TILES * place + tile + 1] for tile in range(TILES)], axis=0
        )
        scaled = chunk * factor
        fine = FINE * SUBLANES
        value = jnp.concatenate(
            [jnp.round(scaled[:fine]).astype(jnp.int32), 2 * jnp.round(0.5 * scaled[fine:]).astype(jnp.int32)], axis=0
        )
        high = jnp.clip(jnp.right_shift(value, 1), -32768, 32767)
        words = jnp.bitwise_or(jnp.left_shift(high[:half], 16), jnp.bitwise_and(high[half:], 0xFFFF))
        first = jnp.broadcast_to(lines[TILES * place : TILES * place + 1], (SUBLANES, LANES))
        second = jnp.broadcast_to(lines[TILES * place + 1 : TILES * place + 2], (SUBLANES, LANES))
        code = jnp.where(sub < NIBBLES, first, second)
        nibble = jnp.right_shift(code, NIBBLES * jnp.bitwise_and(sub, NIBBLES - 1))
        extra = jnp.left_shift(nibble, FINE)
        for group in range(FINE):
            bits = jnp.bitwise_and(value[group * SUBLANES : (group + 1) * SUBLANES], 1)
            extra = jnp.bitwise_or(extra, jnp.left_shift(bits, group))
        messages.append(jnp.concatenate([words, extra], axis=0))
    return messages


def unpack_chunks(messages):
    half = TILES * LANES // 2
    lines = []
    for message in messages:
        nibble = jnp.bitwise_and(jnp.right_shift(message[half:], FINE), 15)
        for tile in range(TILES):
            code = jnp.left_shift(nibble[tile * NIBBLES + NIBBLES - 1 : (tile + 1) * NIBBLES], 28)
            code = jnp.right_shift(code, 28 - NIBBLES * (NIBBLES - 1))
            for place in range(NIBBLES - 1):
                line = nibble[tile * NIBBLES + place : tile * NIBBLES + place + 1]
                code = jnp.bitwise_or(code, jnp.left_shift(line, NIBBLES * place))
            lines.append(code.astype(jnp.float32))
    lines.append(jnp.zeros((LANES - len(lines), LANES), jnp.float32))
    scales = (jnp.exp2(jnp.concatenate(lines, axis=0) * (1.0 / CODES)) * (1.0 / STEPS)).T

    def make(place, tile):
        words, extra = messages[place][:half], messages[place][half:]
        high = jnp.right_shift(words if tile == 0 else jnp.left_shift(words, 16), 16)
        low = [
            jnp.bitwise_and(jnp.right_shift(extra, group), 1) if group < FINE else jnp.zeros_like(extra)
            for group in range(tile * LANES // SUBLANES, (tile + 1) * LANES // SUBLANES)
        ]
        value = jnp.bitwise_or(jnp.left_shift(high, 1), jnp.concatenate(low, axis=0))
        column = TILES * place + tile
        return value.astype(jnp.float32) * scales[:, column : column + 1]

    return [
        [functools.partial(make, place, tile) for tile in range(TILES)] for place in range(len(messages))
    ]


def encode_kernel(place_ref, size_ref, start_ref, out_ref):
    width, size = start_ref.shape
    row = place_ref[0] * width + lax.broadcasted_iota(jnp.int32, (width, size), 0)
    value = jnp.where(row < size_ref[0], start_ref[...], 0.0)
    out_ref[0] = pack_chunks([value.T])[0]


def encode(place, sizes, start):
    width, size = start.shape
    scalar, vmem = pl.BlockSpec(memory_space=pltpu.SMEM), pl.BlockSpec(memory_space=pltpu.VMEM)
    return pl.pallas_call(
        encode_kernel,
        in_specs=[scalar, scalar, vmem],
        out_specs=vmem,
        out_shape=jax.ShapeDtypeStruct((1, PACKED, width), jnp.int32),
    )(place, sizes, start)


def combine_kernel(count, parts, keep_ref, *refs):
    arrived, own_ref, sends = refs[:count], refs[count], refs[count + 1 :]
    chunks = keep_ref.shape[0]
    tiles = unpack_chunks([part[place] for place in range(chunks) for part in arrived])
    totals = []
    for place in range(chunks):
        total = keep_ref[place]
        for source in range(count):
            total = total + jnp.concatenate([tile() for tile in tiles[place * count + source]], axis=0)
        totals.append(total)
    width = chunks // parts
    for place in range(width):
        own_ref[place] = totals[place]
    first = 0 if parts == 1 else width
    for place, message in enumerate(pack_chunks(totals[first:])):
        sends[place // width][place % width] = message


def combine(keep, arrived, parts):
    chunks, rows, lanes = keep.shape
    width = chunks // parts
    vmem = pl.BlockSpec(memory_space=pltpu.VMEM)
    outs = [jax.ShapeDtypeStruct((width, rows, lanes), jnp.float32)]
    outs += [jax.ShapeDtypeStruct((width, PACKED, lanes), jnp.int32)] * max(parts - 1, 1)
    return pl.pallas_call(
        functools.partial(combine_kernel, len(arrived), parts),
        in_specs=[vmem] * (1 + len(arrived)),
        out_specs=[vmem] * len(outs),
        out_shape=outs,
        compiler_params=pltpu.CompilerParams(vmem_limit_bytes=VMEM_SMALL),
    )(keep, *arrived)


def split_pieces(value, pieces):
    parts = []
    rest = value
    for piece in range(pieces):
        part = rest.astype(jnp.bfloat16)
        parts.append(part)
        if piece + 1 < pieces:
            rest = rest - part.astype(jnp.float32)
    return parts


def hold_kernel(after_ref, rows_ref, out_ref, sem):
    copy = pltpu.make_async_copy(rows_ref, out_ref, sem)
    copy.start()
    copy.wait()


def hold(genotypes, after):
    anywhere = pl.BlockSpec(memory_space=pl.ANY)
    return pl.pallas_call(
        hold_kernel,
        in_specs=[anywhere, anywhere],
        out_specs=pl.BlockSpec(memory_space=pltpu.VMEM),
        out_shape=jax.ShapeDtypeStruct(genotypes.shape, genotypes.dtype),
        scratch_shapes=[pltpu.SemaphoreType.DMA],
        compiler_params=pltpu.CompilerParams(vmem_limit_bytes=VMEM_SMALL),
        cost_estimate=FACTOR_COST,
    )(after, genotypes)


def load_all(order, place_ref, refs, full_ref):
    if len(refs) == 1:
        full_ref[...] = refs[0][...]
        return
    width = refs[0].shape[2]
    each = refs[0].shape[0]
    tiles = unpack_chunks([ref[place] for ref in refs for place in range(each)])
    for offset, chunk in zip(order, tiles):
        first = pl.multiple_of(jnp.bitwise_xor(place_ref[0], offset) * width, width)
        for part, tile in enumerate(chunk):
            full_ref[pl.ds(part * LANES, LANES), pl.ds(first, width)] = tile()


def apply_kernel(order, normalise, scale, sources, place_ref, size_ref, rows_ref, *refs):
    refs, outs, (full_ref, work_ref) = refs[:sources], refs[sources:-2], refs[-2:]
    size, cap = full_ref.shape
    load_all(order, place_ref, refs, full_ref)
    value = full_ref[...]
    if normalise:
        start_factor(work_ref, rows_inner(value))
        inverse_factor(work_ref, size, PANEL)
        value = jnp.dot(finish_factor(work_ref), value, precision=HIGHEST, preferred_element_type=jnp.float32)
    split = jnp.concatenate(split_pieces(value, PIECES), axis=0)
    image = rows_dot(split, rows_ref[...])
    image = sum(image[piece * size : (piece + 1) * size] for piece in range(PIECES)) * scale
    split = jnp.concatenate(split_pieces(image, PIECES), axis=0)
    back = jnp.dot(split, rows_ref[...], preferred_element_type=jnp.float32)
    back = sum(back[piece * size : (piece + 1) * size] for piece in range(PIECES))
    live = lax.broadcasted_iota(jnp.int32, (1, cap), 1) < size_ref[0]
    back = jnp.where(live, back, 0.0)
    if len(outs) == 1:
        outs[0][...] = back
        return
    full_ref[...] = back
    each, _, width = outs[0].shape
    chunks = []
    for offset in order:
        first = pl.multiple_of(jnp.bitwise_xor(place_ref[0], offset) * width, width)
        chunks.append(full_ref[:, pl.ds(first, width)])
    for place in range(each):
        outs[0][place] = chunks[place]
    for place, message in enumerate(pack_chunks(chunks[each:])):
        outs[1 + place // each][place % each] = message


def apply_samples(genotypes, sizes, place, gathered, order, normalise, scale):
    samples, cap = genotypes.shape
    if len(gathered) > 1:
        each, rows, width = gathered[0].shape
        size = TILES * LANES
        outs = [jax.ShapeDtypeStruct((each, size, width), jnp.float32)]
        outs += [jax.ShapeDtypeStruct((each, rows, width), jnp.int32)] * (len(gathered) - 1)
    else:
        size = gathered[0].shape[0]
        outs = [jax.ShapeDtypeStruct((size, cap), jnp.float32)]
    scalar, vmem = pl.BlockSpec(memory_space=pltpu.SMEM), pl.BlockSpec(memory_space=pltpu.VMEM)
    return pl.pallas_call(
        functools.partial(apply_kernel, order, normalise, scale, len(gathered)),
        in_specs=[scalar, scalar, vmem] + [vmem] * len(gathered),
        out_specs=[vmem] * len(outs),
        out_shape=outs,
        scratch_shapes=[
            pltpu.VMEM((size, cap), jnp.float32),
            pltpu.VMEM((size, 2 * size), jnp.float32),
        ],
        compiler_params=pltpu.CompilerParams(vmem_limit_bytes=VMEM_LIMIT),
    )(place, sizes, genotypes, *gathered)


def lane_splat(tile, lane):
    return jnp.broadcast_to(tile[:, lane : lane + 1], (SUBLANES, LANES))


def row_splat(tile, row):
    return jnp.broadcast_to(tile[row : row + 1, :], (SUBLANES, LANES))


def inverse_factor(work_ref, size, panel, first_top=0, last_top=None):
    tiles = 2 * size // LANES
    below = lax.broadcasted_iota(jnp.int32, (SUBLANES, LANES), 0)
    groups = panel // SUBLANES
    for top in range(first_top, size if last_top is None else last_top, panel):
        active = [
            tile
            for tile in range(tiles)
            if (top // LANES <= tile < size // LANES)
            or (size // LANES <= tile <= size // LANES + (top + panel - 1) // LANES)
        ]
        rows = [
            {
                tile: work_ref[top + SUBLANES * group : top + SUBLANES * (group + 1), tile * LANES : (tile + 1) * LANES]
                for tile in active
            }
            for group in range(groups)
        ]
        for block in range(groups):
            base = top + SUBLANES * block
            columns = {
                group: [lane_splat(rows[group][base // LANES], base % LANES + lane) for lane in range(SUBLANES)]
                for group in range(block, groups)
            }
            for step in range(SUBLANES):
                pivot = row_splat(columns[block][step], step)
                root = lax.rsqrt(pivot)
                factor = {group: columns[group][step] * root for group in range(block, groups)}
                for later in range(step + 1, SUBLANES):
                    weight = row_splat(factor[block], later)
                    for group in range(block, groups):
                        columns[group][later] = columns[group][later] - factor[group] * weight
                lower = jnp.where(below > step, factor[block], 0.0)
                for tile in active:
                    line = row_splat(rows[block][tile], step) * root
                    rows[block][tile] = jnp.where(
                        below == step, line, rows[block][tile] - lower * line
                    )
                    for group in range(block + 1, groups):
                        rows[group][tile] = rows[group][tile] - factor[group] * line
        for group in range(groups):
            for tile in active:
                work_ref[top + SUBLANES * group : top + SUBLANES * (group + 1), tile * LANES : (tile + 1) * LANES] = rows[
                    group
                ][tile]
        rest = top + panel
        if rest < size:
            first, last = active[0] * LANES, (active[-1] + 1) * LANES
            lines = work_ref[top:rest, first:last]
            high, middle, low = split_pieces(work_ref[top:rest, rest // LANES * LANES : size], 3)
            above, between, below_ = split_pieces(lines, 3)
            update = lax.dot_general(
                jnp.concatenate([high, high, high, middle, middle, low], axis=0),
                jnp.concatenate([above, between, below_, above, between, above], axis=0),
                (((0,), (0,)), ((), ())),
                preferred_element_type=jnp.float32,
            )
            work_ref[rest:, first:last] -= update[rest % LANES :]


def start_factor(work_ref, inner):
    size = inner.shape[0]
    work_ref[:, :size] = inner
    row = lax.broadcasted_iota(jnp.int32, (size, size), 0)
    column = lax.broadcasted_iota(jnp.int32, (size, size), 1)
    work_ref[:, size:] = jnp.where(row == column, 1.0, 0.0)


def finish_factor(work_ref):
    size = work_ref.shape[0]
    row = lax.broadcasted_iota(jnp.int32, (size, size), 0)
    column = lax.broadcasted_iota(jnp.int32, (size, size), 1)
    return jnp.where(row >= column, work_ref[:, size:], 0.0)


def rows_dot(left, right):
    return lax.dot_general(left, right, (((1,), (1,)), ((), ())), preferred_element_type=jnp.float32)


def rows_inner(value):
    high, middle, low = split_pieces(value, 3)
    mixed = rows_dot(high, middle) + rows_dot(high, low)
    return rows_dot(high, high) + rows_dot(middle, middle) + (mixed + mixed.T)


def fold_symmetric(value, folded_ref, height):
    half = value.shape[0] // 2
    row = lax.broadcasted_iota(jnp.int32, (half, half), 0)
    column = lax.broadcasted_iota(jnp.int32, (half, half), 1)
    corner = value[half:, half:]
    both = jnp.where(row >= column, value[:half, :half], corner)
    diagonal = jnp.sum(jnp.where(row == column, corner, 0.0), axis=0, keepdims=True)
    quarter = half // 2
    for place in range(4):
        source = value[half:, :half] if place < 2 else both
        folded_ref[place, :quarter] = source[place % 2 * quarter : (place % 2 + 1) * quarter]
        folded_ref[place, quarter:] = jnp.broadcast_to(diagonal, (SUBLANES, half))


def unfold_symmetric(folded, diagonal):
    half = folded.shape[1]
    row = lax.broadcasted_iota(jnp.int32, (half, half), 0)
    column = lax.broadcasted_iota(jnp.int32, (half, half), 1)
    left, both = folded[:half], folded[half:]
    turned = both.T
    corner = jnp.where(row == column, diagonal, jnp.where(row < column, both, turned))
    upper = jnp.concatenate([jnp.where(row >= column, both, turned), left.T], axis=1)
    return jnp.concatenate([upper, jnp.concatenate([left, corner], axis=1)], axis=0)


def diagonal_of(value):
    row = lax.broadcasted_iota(jnp.int32, value.shape, 0)
    column = lax.broadcasted_iota(jnp.int32, value.shape, 1)
    kept = jnp.where(row == column, value, 0.0)
    return jnp.sum(kept, axis=0, keepdims=True), jnp.sum(kept, axis=1, keepdims=True)


def fold_message(folded, diagonal):
    size, half = folded.shape
    row = lax.broadcasted_iota(jnp.int32, (size, 1), 0)
    most = jnp.max(jnp.abs(diagonal), axis=1, keepdims=True)
    peaks = jnp.max(jnp.abs(folded), axis=1, keepdims=True)
    peaks = jnp.where(row == half, jnp.maximum(peaks, most), peaks)
    codes, scales = row_scales(gather_columns([peaks[:half], peaks[half:]]))
    factors = WIDE_STEPS / scales
    lines = codes.T.astype(jnp.int32)
    value = jnp.round(folded * jnp.concatenate([factors[:, :1], factors[:, 1:2]], axis=0)).astype(jnp.int32)
    high = jnp.right_shift(value, NIBBLES)
    rows = [jnp.bitwise_or(jnp.left_shift(high[:half], 16), jnp.bitwise_and(high[half:], 0xFFFF))]
    for first in range(0, size, 8 * SUBLANES):
        extra = jnp.zeros((SUBLANES, half), jnp.int32)
        for group in range(8):
            start = first + group * SUBLANES
            extra = jnp.bitwise_or(
                extra, jnp.left_shift(jnp.bitwise_and(value[start : start + SUBLANES], 15), NIBBLES * group)
            )
        rows.append(extra)
    last = jnp.round(diagonal * (factors[:1, 1:2] * FINER)).astype(jnp.int32)
    code = jnp.bitwise_or(jnp.bitwise_and(lines[0:1], 0xFFFF), jnp.left_shift(lines[1:2], 16))
    sub = lax.broadcasted_iota(jnp.int32, (SUBLANES, half), 0)
    rows.append(jnp.where(sub == 0, code, jnp.where(sub == 1, last, 0)))
    return jnp.concatenate(rows, axis=0)


def sum_folded(messages):
    half = LANES
    lines = []
    for message in messages:
        code = message[half + 32 : half + 33]
        lines += [jnp.right_shift(jnp.left_shift(code, 16), 16), jnp.right_shift(code, 16)]
    lines = [line.astype(jnp.float32) for line in lines]
    lines.append(jnp.zeros((LANES - len(lines), LANES), jnp.float32))
    scales = (jnp.exp2(jnp.concatenate(lines, axis=0) * (1.0 / CODES)) * (1.0 / WIDE_STEPS)).T
    parts, diagonals = [], []
    for place, message in enumerate(messages):
        words = message[:half]
        high = jnp.concatenate([jnp.right_shift(words, 16), jnp.right_shift(jnp.left_shift(words, 16), 16)], axis=0)
        low = []
        for tile in range(4):
            extra = message[half + tile * SUBLANES : half + (tile + 1) * SUBLANES]
            low += [jnp.bitwise_and(jnp.right_shift(extra, NIBBLES * group), 15) for group in range(8)]
        value = jnp.bitwise_or(jnp.left_shift(high, NIBBLES), jnp.concatenate(low, axis=0))
        scale = jnp.concatenate([scales[:, 2 * place : 2 * place + 1], scales[:, 2 * place + 1 : 2 * place + 2]], axis=0)
        parts.append(value.astype(jnp.float32) * scale)
        last = message[half + 33 : half + 34].astype(jnp.float32)
        diagonals.append(last * (scales[:1, 2 * place + 1 : 2 * place + 2] * (1.0 / FINER)))
    return pair_sum(parts), pair_sum(diagonals)


def add_kernel(*refs):
    refs[-1][...] = fold_message(*sum_folded([ref[...] for ref in refs[:-1]]))


def add_messages(messages):
    vmem = pl.BlockSpec(memory_space=pltpu.VMEM)
    return pl.pallas_call(
        add_kernel,
        in_specs=[vmem] * len(messages),
        out_specs=vmem,
        out_shape=jax.ShapeDtypeStruct(messages[0].shape, messages[0].dtype),
        compiler_params=pltpu.CompilerParams(vmem_limit_bytes=VMEM_SMALL),
    )(*messages)


def sum_messages(message, groups, beside):
    stages = stage_bits(groups)
    steps, state = list(beside), None
    for depth, bits in enumerate(reversed(stages)):
        if depth > 0:
            message = add_messages(messages)
        messages = [message] + [exchange(message, groups, span) for span in offsets(bits)[1:]]
        if steps:
            state = steps.pop(0)(state)
        if depth + 1 < len(stages):
            messages, state = lax.optimization_barrier((messages, state))
    for step in steps:
        state = step(state)
    return messages, state


def project_kernel(order, sources, coded, quarter_ref, place_ref, rows_ref, *refs):
    refs, (inner_ref, *outs), (full_ref, folded_ref) = refs[:sources], refs[sources:-2], refs[-2:]
    size = full_ref.shape[0]
    load_all(order, place_ref, refs, full_ref)
    image = full_ref[...]
    inner = rows_inner(image)
    inner_ref[...] = inner
    split = jnp.concatenate(split_pieces(image, PIECES), axis=0)
    sampled = rows_dot(split, rows_ref[...])
    sampled = sum(sampled[piece * size : (piece + 1) * size] for piece in range(PIECES))
    high, low = split_pieces(sampled, PIECES)
    mixed = rows_dot(high, low)
    cross = rows_dot(high, high) + (mixed + mixed.T)
    across, down = diagonal_of(inner)
    fold_symmetric(cross * (lax.rsqrt(down) * lax.rsqrt(across)), folded_ref, size)
    if coded:
        quarter = size // 4
        folded = jnp.concatenate([folded_ref[place, :quarter] for place in range(4)], axis=0)
        outs[0][...] = fold_message(folded, folded_ref[0, quarter : quarter + 1])
        return
    for offset, out_ref in enumerate(outs):
        out_ref[...] = folded_ref[jnp.bitwise_xor(quarter_ref[0], offset)]


def project(genotypes, quarter, place, gathered, order, size):
    samples, cap = genotypes.shape
    scalar, vmem = pl.BlockSpec(memory_space=pltpu.SMEM), pl.BlockSpec(memory_space=pltpu.VMEM)
    part = (size // 4 + SUBLANES, size // 2)
    coded = size == TILES * LANES
    outs = [jax.ShapeDtypeStruct((size, size), jnp.float32)]
    if coded:
        outs += [jax.ShapeDtypeStruct((WIDE, LANES), jnp.int32)]
    else:
        outs += [jax.ShapeDtypeStruct(part, jnp.float32)] * 4
    return pl.pallas_call(
        functools.partial(project_kernel, order, len(gathered), coded),
        in_specs=[scalar, scalar, vmem] + [vmem] * len(gathered),
        out_specs=[vmem] * len(outs),
        out_shape=outs,
        scratch_shapes=[
            pltpu.VMEM((size, cap), jnp.float32),
            pltpu.VMEM((4,) + part, jnp.float32),
        ],
        compiler_params=pltpu.CompilerParams(vmem_limit_bytes=VMEM_LIMIT),
    )(quarter, place, genotypes, *gathered)


def second_kernel(first, last, source_ref, work_ref):
    if first == 0:
        start_factor(work_ref, source_ref[...])
    else:
        work_ref[...] = source_ref[...]
    inverse_factor(work_ref, work_ref.shape[0], PANEL, first, last)


def second_factor(source, first, last):
    size = source.shape[0]
    vmem = pl.BlockSpec(memory_space=pltpu.VMEM)
    return pl.pallas_call(
        functools.partial(second_kernel, first, last),
        in_specs=[vmem],
        out_specs=vmem,
        out_shape=jax.ShapeDtypeStruct((size, 2 * size), jnp.float32),
        compiler_params=pltpu.CompilerParams(vmem_limit_bytes=VMEM_LIMIT),
        cost_estimate=FACTOR_COST,
    )(source)


def basis_kernel(gain, factor_ref, own_ref, out_ref):
    own = jnp.dot(finish_factor(factor_ref), own_ref[...], precision=HIGHEST, preferred_element_type=jnp.float32)
    out_ref[...] = own.T * gain


def basis_rows(factor, own, gain):
    vmem = pl.BlockSpec(memory_space=pltpu.VMEM)
    return pl.pallas_call(
        functools.partial(basis_kernel, gain),
        in_specs=[vmem] * 2,
        out_specs=vmem,
        out_shape=jax.ShapeDtypeStruct(own.shape[::-1], jnp.float32),
        compiler_params=pltpu.CompilerParams(vmem_limit_bytes=VMEM_SMALL),
        cost_estimate=pl.CostEstimate(flops=1_000_000_000, bytes_accessed=1 << 20, transcendentals=0),
    )(factor, own)


def trace_kernel(scale, quarter_ref, factor_ref, inner_ref, *refs):
    parts, (half_ref, trace_ref, folded_ref) = refs[:-3], refs[-3:]
    if parts[0].dtype == jnp.int32:
        folded, diagonal = sum_folded([part[...] for part in parts])
    else:
        for offset in range(4):
            folded_ref[jnp.bitwise_xor(quarter_ref[0], offset)] = parts[offset][...]
        quarter = folded_ref.shape[1] - SUBLANES
        folded = jnp.concatenate([folded_ref[place, :quarter] for place in range(4)], axis=0)
        diagonal = folded_ref[3, quarter : quarter + 1]
    across, down = diagonal_of(inner_ref[...])
    cross = unfold_symmetric(folded, diagonal) * ((down * lax.rsqrt(down)) * (across * lax.rsqrt(across)))
    factor = finish_factor(factor_ref)
    half = scale * jnp.dot(factor, cross, precision=HIGHEST, preferred_element_type=jnp.float32)
    half_ref[...] = half
    trace_ref[...] = jnp.broadcast_to(jnp.sum(half * factor), trace_ref.shape)


def trace_half(quarter, factor, inner, parts, scale):
    vmem = pl.BlockSpec(memory_space=pltpu.VMEM)
    return pl.pallas_call(
        functools.partial(trace_kernel, scale),
        in_specs=[pl.BlockSpec(memory_space=pltpu.SMEM)] + [vmem] * (2 + len(parts)),
        out_specs=[vmem] * 2,
        out_shape=[
            jax.ShapeDtypeStruct(inner.shape, jnp.float32),
            jax.ShapeDtypeStruct((SUBLANES, LANES), jnp.float32),
        ],
        scratch_shapes=[pltpu.VMEM((4,) + parts[0].shape, parts[0].dtype)],
        compiler_params=pltpu.CompilerParams(vmem_limit_bytes=VMEM_SMALL),
    )(quarter, factor, inner, *parts)


def finish_kernel(gain, half_ref, factor_ref, *refs):
    traces, out_ref = refs[:-1], refs[-1]
    total = sum(trace[:1, :1] for trace in traces)
    whole = lax.dot_general(
        half_ref[...],
        finish_factor(factor_ref),
        (((1,), (1,)), ((), ())),
        precision=HIGHEST,
        preferred_element_type=jnp.float32,
    )
    out_ref[...] = whole * (gain / total)


def finish(half, factor, traces, gain):
    vmem = pl.BlockSpec(memory_space=pltpu.VMEM)
    return pl.pallas_call(
        functools.partial(finish_kernel, gain),
        in_specs=[vmem] * (2 + len(traces)),
        out_specs=vmem,
        out_shape=jax.ShapeDtypeStruct(half.shape, jnp.float32),
        compiler_params=pltpu.CompilerParams(vmem_limit_bytes=VMEM_SMALL),
    )(half, factor, *traces)


def to_natural(gathered, order, me):
    places = jnp.argsort(jnp.array(order, jnp.int32))
    mine = jnp.bitwise_xor(jnp.arange(len(order), dtype=jnp.int32), me)
    stacked = jnp.concatenate(gathered, axis=0)[places][mine]
    return jnp.transpose(stacked, (1, 0, 2)).reshape(stacked.shape[1], -1)


def to_relative(rows, order, me, width, parts):
    chunks = jnp.transpose(rows.reshape(rows.shape[0], -1, width), (1, 0, 2))
    return jnp.split(chunks[jnp.bitwise_xor(jnp.array(order, jnp.int32), me)], parts, axis=0)


def body(genotypes, sizes, start):
    groups = lax.axis_size("smp")
    dosages = genotypes[0]
    samples, cap = dosages.shape
    width, size = start.shape[1:]
    scale = 1.0 / (samples * groups)
    me = lax.axis_index("smp")
    place = me.reshape(1).astype(jnp.int32)
    stages = stage_bits(groups)
    order = relative_order(stages)
    packed = width == LANES and size == TILES * LANES

    def gather(message):
        gathered = gather_chunks(message, groups)
        return gathered if packed else [to_natural(gathered, order, me)]

    def apply(message, normalise):
        outs = apply_samples(dosages, sizes, place, gather(message), order, normalise, scale)
        if not packed:
            outs = to_relative(outs[0], order, me, width, len(offsets(stages[0])))
        return reduce_chunks(outs[0], outs[1:], groups, packed)

    if packed:
        message = encode(place, sizes, start[0])
    else:
        row = me * width + lax.broadcasted_iota(jnp.int32, (width, size), 0)
        message = jnp.where(row < sizes[0], start[0], 0.0).T[None]
    dosages = hold(dosages, message)
    _, message = apply(message, False)
    own, message = apply(message, True)
    quarter = jnp.bitwise_and(place, 3)
    inner, *parts = project(dosages, quarter, place, gather(message), order, size)
    if len(parts) == 1:
        cut = size // 2 + size // 8
        beside = [lambda _: second_factor(inner, 0, cut), lambda work: second_factor(work, cut, size)]
        parts, second = sum_messages(parts[0], groups, beside)
    else:
        cuts = [0, size // 4 + size // 8, size - size // 4, size]
        beside = [
            lambda _: second_factor(inner, cuts[0], cuts[1]),
            lambda work: second_factor(work, cuts[1], cuts[2]),
            lambda work: second_factor(work, cuts[2], cuts[3]),
        ]
        parts, second = sum_quarters(parts, groups, beside)
    halfway, trace = trace_half(quarter, second, inner, parts, scale)
    blocks = lax.axis_size("blk")
    traces = [trace] + [
        lax.ppermute(trace, "blk", [(block, (block + shift) % blocks) for block in range(blocks)])
        for shift in range(1, blocks)
    ]
    basis = basis_rows(second, own[0], math.sqrt(cap))
    scaled = finish(halfway, second, traces, float(genotypes.shape[0] * blocks * size))
    return basis[None], scaled[None]


def solution(mesh):
    return jax.shard_map(
        body,
        mesh=mesh,
        in_specs=(P("blk", "smp", None), P("blk"), P("blk", "smp", None)),
        out_specs=(P("blk", "smp", None), P("blk", None, None)),
        check_vma=False,
    )
```

```python
import functools
import math

import jax
import jax.numpy as jnp
from jax import lax
from jax.experimental import pallas as pl
from jax.experimental.pallas import tpu as pltpu
from jax.sharding import PartitionSpec as P

LANES = 128
SUBLANES = 8
PANEL = 32
PIECES = 2
CODES = 128
STEPS = 65535.0
LEAST = 2.0**-90
FINER = 64.0
WIDE_STEPS = 524287.0
WIDE = 168
VMEM_LIMIT = 32 * 1024 * 1024
VMEM_SMALL = 8 * 1024 * 1024
HIGHEST = lax.Precision.HIGHEST
FACTOR_COST = pl.CostEstimate(flops=4_000_000_000, bytes_accessed=4 << 20, transcendentals=0)


def stage_bits(groups):
    count = groups.bit_length() - 1
    return [list(range(count))[place : place + 2] for place in range(0, count, 2)]


def offsets(bits):
    found = [0]
    for bit in bits:
        found = found + [value ^ (1 << bit) for value in found]
    return found


def relative_order(stages):
    order = [0]
    for bits in reversed(stages):
        order = [high ^ low for high in offsets(bits) for low in order]
    return order


def exchange(value, groups, offset):
    return lax.ppermute(value, "smp", [(device, device ^ offset) for device in range(groups)])


def reduce_chunks(keep, sends, groups, packed):
    stages = stage_bits(groups)
    for depth, bits in enumerate(stages):
        arrived = [exchange(send, groups, span) for send, span in zip(sends, offsets(bits)[1:])]
        parts = len(offsets(stages[depth + 1])) if depth + 1 < len(stages) else 1
        if packed:
            keep, *sends = combine(keep, arrived, parts)
        else:
            keep, *sends = jnp.split(keep + sum(arrived), parts, axis=0)
    return keep, sends[0] if packed else keep


def stack_kernel(*refs):
    first = 0
    for ref in refs[:-1]:
        refs[-1][first : first + ref.shape[0]] = ref[...]
        first += ref.shape[0]


def stack(parts):
    if parts[0].dtype != jnp.int32:
        return jnp.concatenate(parts, axis=0)
    vmem = pl.BlockSpec(memory_space=pltpu.VMEM)
    shape = (len(parts) * parts[0].shape[0],) + parts[0].shape[1:]
    return pl.pallas_call(
        stack_kernel,
        in_specs=[vmem] * len(parts),
        out_specs=vmem,
        out_shape=jax.ShapeDtypeStruct(shape, parts[0].dtype),
        compiler_params=pltpu.CompilerParams(vmem_limit_bytes=VMEM_SMALL),
    )(*parts)


def gather_chunks(message, groups):
    stages = stage_bits(groups)
    for bits in reversed(stages[1:]):
        message = stack([message] + [exchange(message, groups, span) for span in offsets(bits)[1:]])
    return [message] + [exchange(message, groups, span) for span in offsets(stages[0])[1:]]


def pair_sum(parts):
    while len(parts) > 1:
        parts = [left + right for left, right in zip(parts[::2], parts[1::2])]
    return parts[0]


def sum_quarters(quarters, groups, beside):
    stages = stage_bits(groups)
    spans = offsets(stages[0])
    steps = list(beside)
    state = steps.pop(0)(None)
    arrived = [exchange(part, groups, span) for part, span in zip(quarters[1:], spans[1:])]
    arrived, state = lax.optimization_barrier((arrived, state))
    total = pair_sum([quarters[0]] + arrived)
    for bits in stages[1:]:
        if len(steps) > 1:
            state = steps.pop(0)(state)
        arrived = [exchange(total, groups, span) for span in offsets(bits)[1:]]
        arrived, state = lax.optimization_barrier((arrived, state))
        total = pair_sum([total] + arrived)
    for step in steps:
        state = step(state)
    return [total] + [exchange(total, groups, span) for span in spans[1:]], state


TILES = 2
FINE = 28
NIBBLES = 4
PACKED = TILES * LANES // 2 + SUBLANES


def row_scales(peaks):
    codes = jnp.ceil(jnp.log2(jnp.maximum(peaks, LEAST)) * CODES) + 1.0
    return codes, jnp.exp2(codes * (1.0 / CODES))


def gather_columns(columns):
    lane = lax.broadcasted_iota(jnp.int32, (LANES, LANES), 1)
    matrix = jnp.zeros((LANES, LANES), jnp.float32)
    for place, column in enumerate(columns):
        matrix = jnp.where(lane == place, column, matrix)
    return matrix


def pack_chunks(chunks):
    peaks = [jnp.max(jnp.abs(chunk), axis=1, keepdims=True) for chunk in chunks]
    codes, scales = row_scales(
        gather_columns([peak[tile * LANES : (tile + 1) * LANES] for peak in peaks for tile in range(TILES)])
    )
    factors = STEPS / scales
    lines = codes.T.astype(jnp.int32)
    sub = lax.broadcasted_iota(jnp.int32, (SUBLANES, LANES), 0)
    half = TILES * LANES // 2
    messages = []
    for place, chunk in enumerate(chunks):
        factor = jnp.concatenate(
            [factors[:, TILES * place + tile : TILES * place + tile + 1] for tile in range(TILES)], axis=0
        )
        scaled = chunk * factor
        fine = FINE * SUBLANES
        value = jnp.concatenate(
            [jnp.round(scaled[:fine]).astype(jnp.int32), 2 * jnp.round(0.5 * scaled[fine:]).astype(jnp.int32)], axis=0
        )
        high = jnp.clip(jnp.right_shift(value, 1), -32768, 32767)
        words = jnp.bitwise_or(jnp.left_shift(high[:half], 16), jnp.bitwise_and(high[half:], 0xFFFF))
        first = jnp.broadcast_to(lines[TILES * place : TILES * place + 1], (SUBLANES, LANES))
        second = jnp.broadcast_to(lines[TILES * place + 1 : TILES * place + 2], (SUBLANES, LANES))
        code = jnp.where(sub < NIBBLES, first, second)
        nibble = jnp.right_shift(code, NIBBLES * jnp.bitwise_and(sub, NIBBLES - 1))
        extra = jnp.left_shift(nibble, FINE)
        for group in range(FINE):
            bits = jnp.bitwise_and(value[group * SUBLANES : (group + 1) * SUBLANES], 1)
            extra = jnp.bitwise_or(extra, jnp.left_shift(bits, group))
        messages.append(jnp.concatenate([words, extra], axis=0))
    return messages


def unpack_chunks(messages):
    half = TILES * LANES // 2
    lines = []
    for message in messages:
        nibble = jnp.bitwise_and(jnp.right_shift(message[half:], FINE), 15)
        for tile in range(TILES):
            code = jnp.left_shift(nibble[tile * NIBBLES + NIBBLES - 1 : (tile + 1) * NIBBLES], 28)
            code = jnp.right_shift(code, 28 - NIBBLES * (NIBBLES - 1))
            for place in range(NIBBLES - 1):
                line = nibble[tile * NIBBLES + place : tile * NIBBLES + place + 1]
                code = jnp.bitwise_or(code, jnp.left_shift(line, NIBBLES * place))
            lines.append(code.astype(jnp.float32))
    lines.append(jnp.zeros((LANES - len(lines), LANES), jnp.float32))
    scales = (jnp.exp2(jnp.concatenate(lines, axis=0) * (1.0 / CODES)) * (1.0 / STEPS)).T

    def make(place, tile):
        words, extra = messages[place][:half], messages[place][half:]
        high = jnp.right_shift(words if tile == 0 else jnp.left_shift(words, 16), 16)
        low = [
            jnp.bitwise_and(jnp.right_shift(extra, group), 1) if group < FINE else jnp.zeros_like(extra)
            for group in range(tile * LANES // SUBLANES, (tile + 1) * LANES // SUBLANES)
        ]
        value = jnp.bitwise_or(jnp.left_shift(high, 1), jnp.concatenate(low, axis=0))
        column = TILES * place + tile
        return value.astype(jnp.float32) * scales[:, column : column + 1]

    return [
        [functools.partial(make, place, tile) for tile in range(TILES)] for place in range(len(messages))
    ]


def encode_kernel(place_ref, size_ref, start_ref, out_ref):
    width, size = start_ref.shape
    row = place_ref[0] * width + lax.broadcasted_iota(jnp.int32, (width, size), 0)
    value = jnp.where(row < size_ref[0], start_ref[...], 0.0)
    out_ref[0] = pack_chunks([value.T])[0]


def encode(place, sizes, start):
    width, size = start.shape
    scalar, vmem = pl.BlockSpec(memory_space=pltpu.SMEM), pl.BlockSpec(memory_space=pltpu.VMEM)
    return pl.pallas_call(
        encode_kernel,
        in_specs=[scalar, scalar, vmem],
        out_specs=vmem,
        out_shape=jax.ShapeDtypeStruct((1, PACKED, width), jnp.int32),
    )(place, sizes, start)


def combine_kernel(count, parts, keep_ref, *refs):
    arrived, own_ref, sends = refs[:count], refs[count], refs[count + 1 :]
    chunks = keep_ref.shape[0]
    tiles = unpack_chunks([part[place] for place in range(chunks) for part in arrived])
    totals = []
    for place in range(chunks):
        total = keep_ref[place]
        for source in range(count):
            total = total + jnp.concatenate([tile() for tile in tiles[place * count + source]], axis=0)
        totals.append(total)
    width = chunks // parts
    for place in range(width):
        own_ref[place] = totals[place]
    first = 0 if parts == 1 else width
    for place, message in enumerate(pack_chunks(totals[first:])):
        sends[place // width][place % width] = message


def combine(keep, arrived, parts):
    chunks, rows, lanes = keep.shape
    width = chunks // parts
    vmem = pl.BlockSpec(memory_space=pltpu.VMEM)
    outs = [jax.ShapeDtypeStruct((width, rows, lanes), jnp.float32)]
    outs += [jax.ShapeDtypeStruct((width, PACKED, lanes), jnp.int32)] * max(parts - 1, 1)
    return pl.pallas_call(
        functools.partial(combine_kernel, len(arrived), parts),
        in_specs=[vmem] * (1 + len(arrived)),
        out_specs=[vmem] * len(outs),
        out_shape=outs,
        compiler_params=pltpu.CompilerParams(vmem_limit_bytes=VMEM_SMALL),
    )(keep, *arrived)


def split_pieces(value, pieces):
    parts = []
    rest = value
    for piece in range(pieces):
        part = rest.astype(jnp.bfloat16)
        parts.append(part)
        if piece + 1 < pieces:
            rest = rest - part.astype(jnp.float32)
    return parts


def hold_kernel(after_ref, rows_ref, out_ref, sem):
    copy = pltpu.make_async_copy(rows_ref, out_ref, sem)
    copy.start()
    copy.wait()


def hold(genotypes, after):
    anywhere = pl.BlockSpec(memory_space=pl.ANY)
    return pl.pallas_call(
        hold_kernel,
        in_specs=[anywhere, anywhere],
        out_specs=pl.BlockSpec(memory_space=pltpu.VMEM),
        out_shape=jax.ShapeDtypeStruct(genotypes.shape, genotypes.dtype),
        scratch_shapes=[pltpu.SemaphoreType.DMA],
        compiler_params=pltpu.CompilerParams(vmem_limit_bytes=VMEM_SMALL),
        cost_estimate=FACTOR_COST,
    )(after, genotypes)


def load_all(order, place_ref, refs, full_ref):
    if len(refs) == 1:
        full_ref[...] = refs[0][...]
        return
    width = refs[0].shape[2]
    each = refs[0].shape[0]
    tiles = unpack_chunks([ref[place] for ref in refs for place in range(each)])
    for offset, chunk in zip(order, tiles):
        first = pl.multiple_of(jnp.bitwise_xor(place_ref[0], offset) * width, width)
        for part, tile in enumerate(chunk):
            full_ref[pl.ds(part * LANES, LANES), pl.ds(first, width)] = tile()


def apply_kernel(order, normalise, scale, sources, place_ref, size_ref, rows_ref, *refs):
    refs, outs, (full_ref, work_ref) = refs[:sources], refs[sources:-2], refs[-2:]
    size, cap = full_ref.shape
    load_all(order, place_ref, refs, full_ref)
    value = full_ref[...]
    if normalise:
        start_factor(work_ref, rows_inner(value))
        inverse_factor(work_ref, size, PANEL)
        value = jnp.dot(finish_factor(work_ref), value, precision=HIGHEST, preferred_element_type=jnp.float32)
    split = jnp.concatenate(split_pieces(value, PIECES), axis=0)
    image = rows_dot(split, rows_ref[...])
    image = sum(image[piece * size : (piece + 1) * size] for piece in range(PIECES)) * scale
    split = jnp.concatenate(split_pieces(image, PIECES), axis=0)
    back = jnp.dot(split, rows_ref[...], preferred_element_type=jnp.float32)
    back = sum(back[piece * size : (piece + 1) * size] for piece in range(PIECES))
    live = lax.broadcasted_iota(jnp.int32, (1, cap), 1) < size_ref[0]
    back = jnp.where(live, back, 0.0)
    if len(outs) == 1:
        outs[0][...] = back
        return
    full_ref[...] = back
    each, _, width = outs[0].shape
    chunks = []
    for offset in order:
        first = pl.multiple_of(jnp.bitwise_xor(place_ref[0], offset) * width, width)
        chunks.append(full_ref[:, pl.ds(first, width)])
    for place in range(each):
        outs[0][place] = chunks[place]
    for place, message in enumerate(pack_chunks(chunks[each:])):
        outs[1 + place // each][place % each] = message


def apply_samples(genotypes, sizes, place, gathered, order, normalise, scale):
    samples, cap = genotypes.shape
    if len(gathered) > 1:
        each, rows, width = gathered[0].shape
        size = TILES * LANES
        outs = [jax.ShapeDtypeStruct((each, size, width), jnp.float32)]
        outs += [jax.ShapeDtypeStruct((each, rows, width), jnp.int32)] * (len(gathered) - 1)
    else:
        size = gathered[0].shape[0]
        outs = [jax.ShapeDtypeStruct((size, cap), jnp.float32)]
    scalar, vmem = pl.BlockSpec(memory_space=pltpu.SMEM), pl.BlockSpec(memory_space=pltpu.VMEM)
    return pl.pallas_call(
        functools.partial(apply_kernel, order, normalise, scale, len(gathered)),
        in_specs=[scalar, scalar, vmem] + [vmem] * len(gathered),
        out_specs=[vmem] * len(outs),
        out_shape=outs,
        scratch_shapes=[
            pltpu.VMEM((size, cap), jnp.float32),
            pltpu.VMEM((size, 2 * size), jnp.float32),
        ],
        compiler_params=pltpu.CompilerParams(vmem_limit_bytes=VMEM_LIMIT),
    )(place, sizes, genotypes, *gathered)


def lane_splat(tile, lane):
    return jnp.broadcast_to(tile[:, lane : lane + 1], (SUBLANES, LANES))


def row_splat(tile, row):
    return jnp.broadcast_to(tile[row : row + 1, :], (SUBLANES, LANES))


def inverse_factor(work_ref, size, panel, first_top=0, last_top=None):
    tiles = 2 * size // LANES
    below = lax.broadcasted_iota(jnp.int32, (SUBLANES, LANES), 0)
    groups = panel // SUBLANES
    for top in range(first_top, size if last_top is None else last_top, panel):
        active = [
            tile
            for tile in range(tiles)
            if (top // LANES <= tile < size // LANES)
            or (size // LANES <= tile <= size // LANES + (top + panel - 1) // LANES)
        ]
        rows = [
            {
                tile: work_ref[top + SUBLANES * group : top + SUBLANES * (group + 1), tile * LANES : (tile + 1) * LANES]
                for tile in active
            }
            for group in range(groups)
        ]
        for block in range(groups):
            base = top + SUBLANES * block
            columns = {
                group: [lane_splat(rows[group][base // LANES], base % LANES + lane) for lane in range(SUBLANES)]
                for group in range(block, groups)
            }
            for step in range(SUBLANES):
                pivot = row_splat(columns[block][step], step)
                root = lax.rsqrt(pivot)
                factor = {group: columns[group][step] * root for group in range(block, groups)}
                for later in range(step + 1, SUBLANES):
                    weight = row_splat(factor[block], later)
                    for group in range(block, groups):
                        columns[group][later] = columns[group][later] - factor[group] * weight
                lower = jnp.where(below > step, factor[block], 0.0)
                for tile in active:
                    line = row_splat(rows[block][tile], step) * root
                    rows[block][tile] = jnp.where(
                        below == step, line, rows[block][tile] - lower * line
                    )
                    for group in range(block + 1, groups):
                        rows[group][tile] = rows[group][tile] - factor[group] * line
        for group in range(groups):
            for tile in active:
                work_ref[top + SUBLANES * group : top + SUBLANES * (group + 1), tile * LANES : (tile + 1) * LANES] = rows[
                    group
                ][tile]
        rest = top + panel
        if rest < size:
            first, last = active[0] * LANES, (active[-1] + 1) * LANES
            lines = work_ref[top:rest, first:last]
            high, middle, low = split_pieces(work_ref[top:rest, rest // LANES * LANES : size], 3)
            above, between, below_ = split_pieces(lines, 3)
            update = lax.dot_general(
                jnp.concatenate([high, high, high, middle, middle, low], axis=0),
                jnp.concatenate([above, between, below_, above, between, above], axis=0),
                (((0,), (0,)), ((), ())),
                preferred_element_type=jnp.float32,
            )
            work_ref[rest:, first:last] -= update[rest % LANES :]


def start_factor(work_ref, inner):
    size = inner.shape[0]
    work_ref[:, :size] = inner
    row = lax.broadcasted_iota(jnp.int32, (size, size), 0)
    column = lax.broadcasted_iota(jnp.int32, (size, size), 1)
    work_ref[:, size:] = jnp.where(row == column, 1.0, 0.0)


def finish_factor(work_ref):
    size = work_ref.shape[0]
    row = lax.broadcasted_iota(jnp.int32, (size, size), 0)
    column = lax.broadcasted_iota(jnp.int32, (size, size), 1)
    return jnp.where(row >= column, work_ref[:, size:], 0.0)


def rows_dot(left, right):
    return lax.dot_general(left, right, (((1,), (1,)), ((), ())), preferred_element_type=jnp.float32)


def rows_inner(value):
    high, middle, low = split_pieces(value, 3)
    mixed = rows_dot(high, middle) + rows_dot(high, low)
    return rows_dot(high, high) + rows_dot(middle, middle) + (mixed + mixed.T)


def fold_symmetric(value, folded_ref, height):
    half = value.shape[0] // 2
    row = lax.broadcasted_iota(jnp.int32, (half, half), 0)
    column = lax.broadcasted_iota(jnp.int32, (half, half), 1)
    corner = value[half:, half:]
    both = jnp.where(row >= column, value[:half, :half], corner)
    diagonal = jnp.sum(jnp.where(row == column, corner, 0.0), axis=0, keepdims=True)
    quarter = half // 2
    for place in range(4):
        source = value[half:, :half] if place < 2 else both
        folded_ref[place, :quarter] = source[place % 2 * quarter : (place % 2 + 1) * quarter]
        folded_ref[place, quarter:] = jnp.broadcast_to(diagonal, (SUBLANES, half))


def unfold_symmetric(folded, diagonal):
    half = folded.shape[1]
    row = lax.broadcasted_iota(jnp.int32, (half, half), 0)
    column = lax.broadcasted_iota(jnp.int32, (half, half), 1)
    left, both = folded[:half], folded[half:]
    turned = both.T
    corner = jnp.where(row == column, diagonal, jnp.where(row < column, both, turned))
    upper = jnp.concatenate([jnp.where(row >= column, both, turned), left.T], axis=1)
    return jnp.concatenate([upper, jnp.concatenate([left, corner], axis=1)], axis=0)


def diagonal_of(value):
    row = lax.broadcasted_iota(jnp.int32, value.shape, 0)
    column = lax.broadcasted_iota(jnp.int32, value.shape, 1)
    kept = jnp.where(row == column, value, 0.0)
    return jnp.sum(kept, axis=0, keepdims=True), jnp.sum(kept, axis=1, keepdims=True)


def fold_message(folded, diagonal):
    size, half = folded.shape
    row = lax.broadcasted_iota(jnp.int32, (size, 1), 0)
    most = jnp.max(jnp.abs(diagonal), axis=1, keepdims=True)
    peaks = jnp.max(jnp.abs(folded), axis=1, keepdims=True)
    peaks = jnp.where(row == half, jnp.maximum(peaks, most), peaks)
    codes, scales = row_scales(gather_columns([peaks[:half], peaks[half:]]))
    factors = WIDE_STEPS / scales
    lines = codes.T.astype(jnp.int32)
    value = jnp.round(folded * jnp.concatenate([factors[:, :1], factors[:, 1:2]], axis=0)).astype(jnp.int32)
    high = jnp.right_shift(value, NIBBLES)
    rows = [jnp.bitwise_or(jnp.left_shift(high[:half], 16), jnp.bitwise_and(high[half:], 0xFFFF))]
    for first in range(0, size, 8 * SUBLANES):
        extra = jnp.zeros((SUBLANES, half), jnp.int32)
        for group in range(8):
            start = first + group * SUBLANES
            extra = jnp.bitwise_or(
                extra, jnp.left_shift(jnp.bitwise_and(value[start : start + SUBLANES], 15), NIBBLES * group)
            )
        rows.append(extra)
    last = jnp.round(diagonal * (factors[:1, 1:2] * FINER)).astype(jnp.int32)
    code = jnp.bitwise_or(jnp.bitwise_and(lines[0:1], 0xFFFF), jnp.left_shift(lines[1:2], 16))
    sub = lax.broadcasted_iota(jnp.int32, (SUBLANES, half), 0)
    rows.append(jnp.where(sub == 0, code, jnp.where(sub == 1, last, 0)))
    return jnp.concatenate(rows, axis=0)


def sum_folded(messages):
    half = LANES
    lines = []
    for message in messages:
        code = message[half + 32 : half + 33]
        lines += [jnp.right_shift(jnp.left_shift(code, 16), 16), jnp.right_shift(code, 16)]
    lines = [line.astype(jnp.float32) for line in lines]
    lines.append(jnp.zeros((LANES - len(lines), LANES), jnp.float32))
    scales = (jnp.exp2(jnp.concatenate(lines, axis=0) * (1.0 / CODES)) * (1.0 / WIDE_STEPS)).T
    parts, diagonals = [], []
    for place, message in enumerate(messages):
        words = message[:half]
        high = jnp.concatenate([jnp.right_shift(words, 16), jnp.right_shift(jnp.left_shift(words, 16), 16)], axis=0)
        low = []
        for tile in range(4):
            extra = message[half + tile * SUBLANES : half + (tile + 1) * SUBLANES]
            low += [jnp.bitwise_and(jnp.right_shift(extra, NIBBLES * group), 15) for group in range(8)]
        value = jnp.bitwise_or(jnp.left_shift(high, NIBBLES), jnp.concatenate(low, axis=0))
        scale = jnp.concatenate([scales[:, 2 * place : 2 * place + 1], scales[:, 2 * place + 1 : 2 * place + 2]], axis=0)
        parts.append(value.astype(jnp.float32) * scale)
        last = message[half + 33 : half + 34].astype(jnp.float32)
        diagonals.append(last * (scales[:1, 2 * place + 1 : 2 * place + 2] * (1.0 / FINER)))
    return pair_sum(parts), pair_sum(diagonals)


def add_kernel(*refs):
    refs[-1][...] = fold_message(*sum_folded([ref[...] for ref in refs[:-1]]))


def add_messages(messages):
    vmem = pl.BlockSpec(memory_space=pltpu.VMEM)
    return pl.pallas_call(
        add_kernel,
        in_specs=[vmem] * len(messages),
        out_specs=vmem,
        out_shape=jax.ShapeDtypeStruct(messages[0].shape, messages[0].dtype),
        compiler_params=pltpu.CompilerParams(vmem_limit_bytes=VMEM_SMALL),
    )(*messages)


def sum_messages(message, groups, beside):
    stages = stage_bits(groups)
    steps, state = list(beside), None
    for depth, bits in enumerate(reversed(stages)):
        if depth > 0:
            message = add_messages(messages)
        messages = [message] + [exchange(message, groups, span) for span in offsets(bits)[1:]]
        if steps:
            state = steps.pop(0)(state)
        if depth + 1 < len(stages):
            messages, state = lax.optimization_barrier((messages, state))
    for step in steps:
        state = step(state)
    return messages, state


def project_kernel(order, sources, coded, quarter_ref, place_ref, rows_ref, *refs):
    refs, (inner_ref, *outs), (full_ref, folded_ref) = refs[:sources], refs[sources:-2], refs[-2:]
    size = full_ref.shape[0]
    load_all(order, place_ref, refs, full_ref)
    image = full_ref[...]
    inner = rows_inner(image)
    inner_ref[...] = inner
    split = jnp.concatenate(split_pieces(image, PIECES), axis=0)
    sampled = rows_dot(split, rows_ref[...])
    sampled = sum(sampled[piece * size : (piece + 1) * size] for piece in range(PIECES))
    high, low = split_pieces(sampled, PIECES)
    mixed = rows_dot(high, low)
    cross = rows_dot(high, high) + (mixed + mixed.T)
    across, down = diagonal_of(inner)
    fold_symmetric(cross * (lax.rsqrt(down) * lax.rsqrt(across)), folded_ref, size)
    if coded:
        quarter = size // 4
        folded = jnp.concatenate([folded_ref[place, :quarter] for place in range(4)], axis=0)
        outs[0][...] = fold_message(folded, folded_ref[0, quarter : quarter + 1])
        return
    for offset, out_ref in enumerate(outs):
        out_ref[...] = folded_ref[jnp.bitwise_xor(quarter_ref[0], offset)]


def project(genotypes, quarter, place, gathered, order, size):
    samples, cap = genotypes.shape
    scalar, vmem = pl.BlockSpec(memory_space=pltpu.SMEM), pl.BlockSpec(memory_space=pltpu.VMEM)
    part = (size // 4 + SUBLANES, size // 2)
    coded = size == TILES * LANES
    outs = [jax.ShapeDtypeStruct((size, size), jnp.float32)]
    if coded:
        outs += [jax.ShapeDtypeStruct((WIDE, LANES), jnp.int32)]
    else:
        outs += [jax.ShapeDtypeStruct(part, jnp.float32)] * 4
    return pl.pallas_call(
        functools.partial(project_kernel, order, len(gathered), coded),
        in_specs=[scalar, scalar, vmem] + [vmem] * len(gathered),
        out_specs=[vmem] * len(outs),
        out_shape=outs,
        scratch_shapes=[
            pltpu.VMEM((size, cap), jnp.float32),
            pltpu.VMEM((4,) + part, jnp.float32),
        ],
        compiler_params=pltpu.CompilerParams(vmem_limit_bytes=VMEM_LIMIT),
    )(quarter, place, genotypes, *gathered)


def second_kernel(first, last, source_ref, work_ref):
    if first == 0:
        start_factor(work_ref, source_ref[...])
    else:
        work_ref[...] = source_ref[...]
    inverse_factor(work_ref, work_ref.shape[0], PANEL, first, last)


def second_factor(source, first, last):
    size = source.shape[0]
    vmem = pl.BlockSpec(memory_space=pltpu.VMEM)
    return pl.pallas_call(
        functools.partial(second_kernel, first, last),
        in_specs=[vmem],
        out_specs=vmem,
        out_shape=jax.ShapeDtypeStruct((size, 2 * size), jnp.float32),
        compiler_params=pltpu.CompilerParams(vmem_limit_bytes=VMEM_LIMIT),
        cost_estimate=FACTOR_COST,
    )(source)


def basis_kernel(gain, factor_ref, own_ref, out_ref):
    own = jnp.dot(finish_factor(factor_ref), own_ref[...], precision=HIGHEST, preferred_element_type=jnp.float32)
    out_ref[...] = own.T * gain


def basis_rows(factor, own, gain):
    vmem = pl.BlockSpec(memory_space=pltpu.VMEM)
    return pl.pallas_call(
        functools.partial(basis_kernel, gain),
        in_specs=[vmem] * 2,
        out_specs=vmem,
        out_shape=jax.ShapeDtypeStruct(own.shape[::-1], jnp.float32),
        compiler_params=pltpu.CompilerParams(vmem_limit_bytes=VMEM_SMALL),
        cost_estimate=pl.CostEstimate(flops=1_000_000_000, bytes_accessed=1 << 20, transcendentals=0),
    )(factor, own)


def trace_kernel(scale, quarter_ref, factor_ref, inner_ref, *refs):
    parts, (half_ref, trace_ref, folded_ref) = refs[:-3], refs[-3:]
    if parts[0].dtype == jnp.int32:
        folded, diagonal = sum_folded([part[...] for part in parts])
    else:
        for offset in range(4):
            folded_ref[jnp.bitwise_xor(quarter_ref[0], offset)] = parts[offset][...]
        quarter = folded_ref.shape[1] - SUBLANES
        folded = jnp.concatenate([folded_ref[place, :quarter] for place in range(4)], axis=0)
        diagonal = folded_ref[3, quarter : quarter + 1]
    across, down = diagonal_of(inner_ref[...])
    cross = unfold_symmetric(folded, diagonal) * ((down * lax.rsqrt(down)) * (across * lax.rsqrt(across)))
    factor = finish_factor(factor_ref)
    half = scale * jnp.dot(factor, cross, precision=HIGHEST, preferred_element_type=jnp.float32)
    half_ref[...] = half
    trace_ref[...] = jnp.broadcast_to(jnp.sum(half * factor), trace_ref.shape)


def trace_half(quarter, factor, inner, parts, scale):
    vmem = pl.BlockSpec(memory_space=pltpu.VMEM)
    return pl.pallas_call(
        functools.partial(trace_kernel, scale),
        in_specs=[pl.BlockSpec(memory_space=pltpu.SMEM)] + [vmem] * (2 + len(parts)),
        out_specs=[vmem] * 2,
        out_shape=[
            jax.ShapeDtypeStruct(inner.shape, jnp.float32),
            jax.ShapeDtypeStruct((SUBLANES, LANES), jnp.float32),
        ],
        scratch_shapes=[pltpu.VMEM((4,) + parts[0].shape, parts[0].dtype)],
        compiler_params=pltpu.CompilerParams(vmem_limit_bytes=VMEM_SMALL),
    )(quarter, factor, inner, *parts)


def finish_kernel(gain, half_ref, factor_ref, *refs):
    traces, out_ref = refs[:-1], refs[-1]
    total = sum(trace[:1, :1] for trace in traces)
    whole = lax.dot_general(
        half_ref[...],
        finish_factor(factor_ref),
        (((1,), (1,)), ((), ())),
        precision=HIGHEST,
        preferred_element_type=jnp.float32,
    )
    out_ref[...] = whole * (gain / total)


def finish(half, factor, traces, gain):
    vmem = pl.BlockSpec(memory_space=pltpu.VMEM)
    return pl.pallas_call(
        functools.partial(finish_kernel, gain),
        in_specs=[vmem] * (2 + len(traces)),
        out_specs=vmem,
        out_shape=jax.ShapeDtypeStruct(half.shape, jnp.float32),
        compiler_params=pltpu.CompilerParams(vmem_limit_bytes=VMEM_SMALL),
    )(half, factor, *traces)


def to_natural(gathered, order, me):
    places = jnp.argsort(jnp.array(order, jnp.int32))
    mine = jnp.bitwise_xor(jnp.arange(len(order), dtype=jnp.int32), me)
    stacked = jnp.concatenate(gathered, axis=0)[places][mine]
    return jnp.transpose(stacked, (1, 0, 2)).reshape(stacked.shape[1], -1)


def to_relative(rows, order, me, width, parts):
    chunks = jnp.transpose(rows.reshape(rows.shape[0], -1, width), (1, 0, 2))
    return jnp.split(chunks[jnp.bitwise_xor(jnp.array(order, jnp.int32), me)], parts, axis=0)


def body(genotypes, sizes, start):
    groups = lax.axis_size("smp")
    dosages = genotypes[0]
    samples, cap = dosages.shape
    width, size = start.shape[1:]
    scale = 1.0 / (samples * groups)
    me = lax.axis_index("smp")
    place = me.reshape(1).astype(jnp.int32)
    stages = stage_bits(groups)
    order = relative_order(stages)
    packed = width == LANES and size == TILES * LANES

    def gather(message):
        gathered = gather_chunks(message, groups)
        return gathered if packed else [to_natural(gathered, order, me)]

    def apply(message, normalise):
        outs = apply_samples(dosages, sizes, place, gather(message), order, normalise, scale)
        if not packed:
            outs = to_relative(outs[0], order, me, width, len(offsets(stages[0])))
        return reduce_chunks(outs[0], outs[1:], groups, packed)

    if packed:
        message = encode(place, sizes, start[0])
    else:
        row = me * width + lax.broadcasted_iota(jnp.int32, (width, size), 0)
        message = jnp.where(row < sizes[0], start[0], 0.0).T[None]
    dosages = hold(dosages, message)
    _, message = apply(message, False)
    own, message = apply(message, True)
    quarter = jnp.bitwise_and(place, 3)
    inner, *parts = project(dosages, quarter, place, gather(message), order, size)
    if len(parts) == 1:
        cut = size // 2
        beside = [lambda _: second_factor(inner, 0, cut), lambda work: second_factor(work, cut, size)]
        parts, second = sum_messages(parts[0], groups, beside)
    else:
        cuts = [0, size // 4 + size // 8, size - size // 4, size]
        beside = [
            lambda _: second_factor(inner, cuts[0], cuts[1]),
            lambda work: second_factor(work, cuts[1], cuts[2]),
            lambda work: second_factor(work, cuts[2], cuts[3]),
        ]
        parts, second = sum_quarters(parts, groups, beside)
    halfway, trace = trace_half(quarter, second, inner, parts, scale)
    blocks = lax.axis_size("blk")
    traces = [trace] + [
        lax.ppermute(trace, "blk", [(block, (block + shift) % blocks) for block in range(blocks)])
        for shift in range(1, blocks)
    ]
    basis = basis_rows(second, own[0], math.sqrt(cap))
    scaled = finish(halfway, second, traces, float(genotypes.shape[0] * blocks * size))
    return basis[None], scaled[None]


def solution(mesh):
    return jax.shard_map(
        body,
        mesh=mesh,
        in_specs=(P("blk", "smp", None), P("blk"), P("blk", "smp", None)),
        out_specs=(P("blk", "smp", None), P("blk", None, None)),
        check_vma=False,
    )
```

```python
import functools
import math

import jax
import jax.numpy as jnp
from jax import lax
from jax.experimental import pallas as pl
from jax.experimental.pallas import tpu as pltpu
from jax.sharding import PartitionSpec as P

LANES = 128
SUBLANES = 8
PANEL = 32
PIECES = 2
CODES = 128
STEPS = 65535.0
LEAST = 2.0**-90
FINER = 64.0
WIDE_STEPS = 524287.0
WIDE = 168
VMEM_LIMIT = 32 * 1024 * 1024
VMEM_SMALL = 8 * 1024 * 1024
HIGHEST = lax.Precision.HIGHEST
FACTOR_COST = pl.CostEstimate(flops=4_000_000_000, bytes_accessed=4 << 20, transcendentals=0)


def stage_bits(groups):
    count = groups.bit_length() - 1
    return [list(range(count))[place : place + 2] for place in range(0, count, 2)]


def offsets(bits):
    found = [0]
    for bit in bits:
        found = found + [value ^ (1 << bit) for value in found]
    return found


def relative_order(stages):
    order = [0]
    for bits in reversed(stages):
        order = [high ^ low for high in offsets(bits) for low in order]
    return order


def exchange(value, groups, offset):
    return lax.ppermute(value, "smp", [(device, device ^ offset) for device in range(groups)])


def reduce_chunks(keep, sends, groups, packed):
    stages = stage_bits(groups)
    for depth, bits in enumerate(stages):
        arrived = [exchange(send, groups, span) for send, span in zip(sends, offsets(bits)[1:])]
        parts = len(offsets(stages[depth + 1])) if depth + 1 < len(stages) else 1
        if packed:
            keep, *sends = combine(keep, arrived, parts)
        else:
            keep, *sends = jnp.split(keep + sum(arrived), parts, axis=0)
    return keep, sends[0] if packed else keep


def stack_kernel(*refs):
    first = 0
    for ref in refs[:-1]:
        refs[-1][first : first + ref.shape[0]] = ref[...]
        first += ref.shape[0]


def stack(parts):
    if parts[0].dtype != jnp.int32:
        return jnp.concatenate(parts, axis=0)
    vmem = pl.BlockSpec(memory_space=pltpu.VMEM)
    shape = (len(parts) * parts[0].shape[0],) + parts[0].shape[1:]
    return pl.pallas_call(
        stack_kernel,
        in_specs=[vmem] * len(parts),
        out_specs=vmem,
        out_shape=jax.ShapeDtypeStruct(shape, parts[0].dtype),
        compiler_params=pltpu.CompilerParams(vmem_limit_bytes=VMEM_SMALL),
    )(*parts)


def gather_chunks(message, groups):
    stages = stage_bits(groups)
    for bits in reversed(stages[1:]):
        message = stack([message] + [exchange(message, groups, span) for span in offsets(bits)[1:]])
    return [message] + [exchange(message, groups, span) for span in offsets(stages[0])[1:]]


def pair_sum(parts):
    while len(parts) > 1:
        parts = [left + right for left, right in zip(parts[::2], parts[1::2])]
    return parts[0]


def sum_quarters(quarters, groups, beside):
    stages = stage_bits(groups)
    spans = offsets(stages[0])
    steps = list(beside)
    state = steps.pop(0)(None)
    arrived = [exchange(part, groups, span) for part, span in zip(quarters[1:], spans[1:])]
    arrived, state = lax.optimization_barrier((arrived, state))
    total = pair_sum([quarters[0]] + arrived)
    for bits in stages[1:]:
        if len(steps) > 1:
            state = steps.pop(0)(state)
        arrived = [exchange(total, groups, span) for span in offsets(bits)[1:]]
        arrived, state = lax.optimization_barrier((arrived, state))
        total = pair_sum([total] + arrived)
    for step in steps:
        state = step(state)
    return [total] + [exchange(total, groups, span) for span in spans[1:]], state


TILES = 2
FINE = 28
NIBBLES = 4
PACKED = TILES * LANES // 2 + SUBLANES


def row_scales(peaks):
    codes = jnp.ceil(jnp.log2(jnp.maximum(peaks, LEAST)) * CODES) + 1.0
    return codes, jnp.exp2(codes * (1.0 / CODES))


def gather_columns(columns):
    lane = lax.broadcasted_iota(jnp.int32, (LANES, LANES), 1)
    matrix = jnp.zeros((LANES, LANES), jnp.float32)
    for place, column in enumerate(columns):
        matrix = jnp.where(lane == place, column, matrix)
    return matrix


def pack_chunks(chunks):
    peaks = [jnp.max(jnp.abs(chunk), axis=1, keepdims=True) for chunk in chunks]
    codes, scales = row_scales(
        gather_columns([peak[tile * LANES : (tile + 1) * LANES] for peak in peaks for tile in range(TILES)])
    )
    factors = STEPS / scales
    lines = codes.T.astype(jnp.int32)
    sub = lax.broadcasted_iota(jnp.int32, (SUBLANES, LANES), 0)
    half = TILES * LANES // 2
    messages = []
    for place, chunk in enumerate(chunks):
        factor = jnp.concatenate(
            [factors[:, TILES * place + tile : TILES * place + tile + 1] for tile in range(TILES)], axis=0
        )
        scaled = chunk * factor
        fine = FINE * SUBLANES
        value = jnp.concatenate(
            [jnp.round(scaled[:fine]).astype(jnp.int32), 2 * jnp.round(0.5 * scaled[fine:]).astype(jnp.int32)], axis=0
        )
        high = jnp.clip(jnp.right_shift(value, 1), -32768, 32767)
        words = jnp.bitwise_or(jnp.left_shift(high[:half], 16), jnp.bitwise_and(high[half:], 0xFFFF))
        first = jnp.broadcast_to(lines[TILES * place : TILES * place + 1], (SUBLANES, LANES))
        second = jnp.broadcast_to(lines[TILES * place + 1 : TILES * place + 2], (SUBLANES, LANES))
        code = jnp.where(sub < NIBBLES, first, second)
        nibble = jnp.right_shift(code, NIBBLES * jnp.bitwise_and(sub, NIBBLES - 1))
        extra = jnp.left_shift(nibble, FINE)
        for group in range(FINE):
            bits = jnp.bitwise_and(value[group * SUBLANES : (group + 1) * SUBLANES], 1)
            extra = jnp.bitwise_or(extra, jnp.left_shift(bits, group))
        messages.append(jnp.concatenate([words, extra], axis=0))
    return messages


def unpack_chunks(messages):
    half = TILES * LANES // 2
    lines = []
    for message in messages:
        nibble = jnp.bitwise_and(jnp.right_shift(message[half:], FINE), 15)
        for tile in range(TILES):
            code = jnp.left_shift(nibble[tile * NIBBLES + NIBBLES - 1 : (tile + 1) * NIBBLES], 28)
            code = jnp.right_shift(code, 28 - NIBBLES * (NIBBLES - 1))
            for place in range(NIBBLES - 1):
                line = nibble[tile * NIBBLES + place : tile * NIBBLES + place + 1]
                code = jnp.bitwise_or(code, jnp.left_shift(line, NIBBLES * place))
            lines.append(code.astype(jnp.float32))
    lines.append(jnp.zeros((LANES - len(lines), LANES), jnp.float32))
    scales = (jnp.exp2(jnp.concatenate(lines, axis=0) * (1.0 / CODES)) * (1.0 / STEPS)).T

    def make(place, tile):
        words, extra = messages[place][:half], messages[place][half:]
        high = jnp.right_shift(words if tile == 0 else jnp.left_shift(words, 16), 16)
        low = [
            jnp.bitwise_and(jnp.right_shift(extra, group), 1) if group < FINE else jnp.zeros_like(extra)
            for group in range(tile * LANES // SUBLANES, (tile + 1) * LANES // SUBLANES)
        ]
        value = jnp.bitwise_or(jnp.left_shift(high, 1), jnp.concatenate(low, axis=0))
        column = TILES * place + tile
        return value.astype(jnp.float32) * scales[:, column : column + 1]

    return [
        [functools.partial(make, place, tile) for tile in range(TILES)] for place in range(len(messages))
    ]


def encode_kernel(place_ref, size_ref, start_ref, out_ref):
    width, size = start_ref.shape
    row = place_ref[0] * width + lax.broadcasted_iota(jnp.int32, (width, size), 0)
    value = jnp.where(row < size_ref[0], start_ref[...], 0.0)
    out_ref[0] = pack_chunks([value.T])[0]


def encode(place, sizes, start):
    width, size = start.shape
    scalar, vmem = pl.BlockSpec(memory_space=pltpu.SMEM), pl.BlockSpec(memory_space=pltpu.VMEM)
    return pl.pallas_call(
        encode_kernel,
        in_specs=[scalar, scalar, vmem],
        out_specs=vmem,
        out_shape=jax.ShapeDtypeStruct((1, PACKED, width), jnp.int32),
    )(place, sizes, start)


def combine_kernel(count, parts, keep_ref, *refs):
    arrived, own_ref, sends = refs[:count], refs[count], refs[count + 1 :]
    chunks = keep_ref.shape[0]
    tiles = unpack_chunks([part[place] for place in range(chunks) for part in arrived])
    totals = []
    for place in range(chunks):
        total = keep_ref[place]
        for source in range(count):
            total = total + jnp.concatenate([tile() for tile in tiles[place * count + source]], axis=0)
        totals.append(total)
    width = chunks // parts
    for place in range(width):
        own_ref[place] = totals[place]
    first = 0 if parts == 1 else width
    for place, message in enumerate(pack_chunks(totals[first:])):
        sends[place // width][place % width] = message


def combine(keep, arrived, parts):
    chunks, rows, lanes = keep.shape
    width = chunks // parts
    vmem = pl.BlockSpec(memory_space=pltpu.VMEM)
    outs = [jax.ShapeDtypeStruct((width, rows, lanes), jnp.float32)]
    outs += [jax.ShapeDtypeStruct((width, PACKED, lanes), jnp.int32)] * max(parts - 1, 1)
    return pl.pallas_call(
        functools.partial(combine_kernel, len(arrived), parts),
        in_specs=[vmem] * (1 + len(arrived)),
        out_specs=[vmem] * len(outs),
        out_shape=outs,
        compiler_params=pltpu.CompilerParams(vmem_limit_bytes=VMEM_SMALL),
    )(keep, *arrived)


def split_pieces(value, pieces):
    parts = []
    rest = value
    for piece in range(pieces):
        part = rest.astype(jnp.bfloat16)
        parts.append(part)
        if piece + 1 < pieces:
            rest = rest - part.astype(jnp.float32)
    return parts


def hold_kernel(after_ref, rows_ref, out_ref, sem):
    copy = pltpu.make_async_copy(rows_ref, out_ref, sem)
    copy.start()
    copy.wait()


def hold(genotypes, after):
    anywhere = pl.BlockSpec(memory_space=pl.ANY)
    return pl.pallas_call(
        hold_kernel,
        in_specs=[anywhere, anywhere],
        out_specs=pl.BlockSpec(memory_space=pltpu.VMEM),
        out_shape=jax.ShapeDtypeStruct(genotypes.shape, genotypes.dtype),
        scratch_shapes=[pltpu.SemaphoreType.DMA],
        compiler_params=pltpu.CompilerParams(vmem_limit_bytes=VMEM_SMALL),
        cost_estimate=FACTOR_COST,
    )(after, genotypes)


def load_all(order, place_ref, refs, full_ref):
    if len(refs) == 1:
        full_ref[...] = refs[0][...]
        return
    width = refs[0].shape[2]
    each = refs[0].shape[0]
    tiles = unpack_chunks([ref[place] for ref in refs for place in range(each)])
    for offset, chunk in zip(order, tiles):
        first = pl.multiple_of(jnp.bitwise_xor(place_ref[0], offset) * width, width)
        for part, tile in enumerate(chunk):
            full_ref[pl.ds(part * LANES, LANES), pl.ds(first, width)] = tile()


def apply_kernel(order, normalise, scale, sources, place_ref, size_ref, rows_ref, *refs):
    refs, outs, (full_ref, work_ref) = refs[:sources], refs[sources:-2], refs[-2:]
    size, cap = full_ref.shape
    load_all(order, place_ref, refs, full_ref)
    value = full_ref[...]
    if normalise:
        start_factor(work_ref, rows_inner(value))
        inverse_factor(work_ref, size, PANEL)
        value = wide_dot(finish_factor(work_ref), value)
    split = jnp.concatenate(split_pieces(value, PIECES), axis=0)
    image = rows_dot(split, rows_ref[...])
    image = sum(image[piece * size : (piece + 1) * size] for piece in range(PIECES)) * scale
    split = jnp.concatenate(split_pieces(image, PIECES), axis=0)
    back = jnp.dot(split, rows_ref[...], preferred_element_type=jnp.float32)
    back = sum(back[piece * size : (piece + 1) * size] for piece in range(PIECES))
    live = lax.broadcasted_iota(jnp.int32, (1, cap), 1) < size_ref[0]
    back = jnp.where(live, back, 0.0)
    if len(outs) == 1:
        outs[0][...] = back
        return
    full_ref[...] = back
    each, _, width = outs[0].shape
    chunks = []
    for offset in order:
        first = pl.multiple_of(jnp.bitwise_xor(place_ref[0], offset) * width, width)
        chunks.append(full_ref[:, pl.ds(first, width)])
    for place in range(each):
        outs[0][place] = chunks[place]
    for place, message in enumerate(pack_chunks(chunks[each:])):
        outs[1 + place // each][place % each] = message


def apply_samples(genotypes, sizes, place, gathered, order, normalise, scale):
    samples, cap = genotypes.shape
    if len(gathered) > 1:
        each, rows, width = gathered[0].shape
        size = TILES * LANES
        outs = [jax.ShapeDtypeStruct((each, size, width), jnp.float32)]
        outs += [jax.ShapeDtypeStruct((each, rows, width), jnp.int32)] * (len(gathered) - 1)
    else:
        size = gathered[0].shape[0]
        outs = [jax.ShapeDtypeStruct((size, cap), jnp.float32)]
    scalar, vmem = pl.BlockSpec(memory_space=pltpu.SMEM), pl.BlockSpec(memory_space=pltpu.VMEM)
    return pl.pallas_call(
        functools.partial(apply_kernel, order, normalise, scale, len(gathered)),
        in_specs=[scalar, scalar, vmem] + [vmem] * len(gathered),
        out_specs=[vmem] * len(outs),
        out_shape=outs,
        scratch_shapes=[
            pltpu.VMEM((size, cap), jnp.float32),
            pltpu.VMEM((size, 2 * size), jnp.float32),
        ],
        compiler_params=pltpu.CompilerParams(vmem_limit_bytes=VMEM_LIMIT),
    )(place, sizes, genotypes, *gathered)


def lane_splat(tile, lane):
    return jnp.broadcast_to(tile[:, lane : lane + 1], (SUBLANES, LANES))


def row_splat(tile, row):
    return jnp.broadcast_to(tile[row : row + 1, :], (SUBLANES, LANES))


def inverse_factor(work_ref, size, panel, first_top=0, last_top=None):
    tiles = 2 * size // LANES
    below = lax.broadcasted_iota(jnp.int32, (SUBLANES, LANES), 0)
    groups = panel // SUBLANES
    for top in range(first_top, size if last_top is None else last_top, panel):
        active = [
            tile
            for tile in range(tiles)
            if (top // LANES <= tile < size // LANES)
            or (size // LANES <= tile <= size // LANES + (top + panel - 1) // LANES)
        ]
        rows = [
            {
                tile: work_ref[top + SUBLANES * group : top + SUBLANES * (group + 1), tile * LANES : (tile + 1) * LANES]
                for tile in active
            }
            for group in range(groups)
        ]
        for block in range(groups):
            base = top + SUBLANES * block
            columns = {
                group: [lane_splat(rows[group][base // LANES], base % LANES + lane) for lane in range(SUBLANES)]
                for group in range(block, groups)
            }
            for step in range(SUBLANES):
                pivot = row_splat(columns[block][step], step)
                root = lax.rsqrt(pivot)
                factor = {group: columns[group][step] * root for group in range(block, groups)}
                for later in range(step + 1, SUBLANES):
                    weight = row_splat(factor[block], later)
                    for group in range(block, groups):
                        columns[group][later] = columns[group][later] - factor[group] * weight
                lower = jnp.where(below > step, factor[block], 0.0)
                for tile in active:
                    line = row_splat(rows[block][tile], step) * root
                    rows[block][tile] = jnp.where(
                        below == step, line, rows[block][tile] - lower * line
                    )
                    for group in range(block + 1, groups):
                        rows[group][tile] = rows[group][tile] - factor[group] * line
        for group in range(groups):
            for tile in active:
                work_ref[top + SUBLANES * group : top + SUBLANES * (group + 1), tile * LANES : (tile + 1) * LANES] = rows[
                    group
                ][tile]
        rest = top + panel
        if rest < size:
            first, last = active[0] * LANES, (active[-1] + 1) * LANES
            lines = work_ref[top:rest, first:last]
            high, middle, low = split_pieces(work_ref[top:rest, rest // LANES * LANES : size], 3)
            above, between, below_ = split_pieces(lines, 3)
            update = lax.dot_general(
                jnp.concatenate([high, high, high, middle, middle, low], axis=0),
                jnp.concatenate([above, between, below_, above, between, above], axis=0),
                (((0,), (0,)), ((), ())),
                preferred_element_type=jnp.float32,
            )
            work_ref[rest:, first:last] -= update[rest % LANES :]


def start_factor(work_ref, inner):
    size = inner.shape[0]
    work_ref[:, :size] = inner
    row = lax.broadcasted_iota(jnp.int32, (size, size), 0)
    column = lax.broadcasted_iota(jnp.int32, (size, size), 1)
    work_ref[:, size:] = jnp.where(row == column, 1.0, 0.0)


def finish_factor(work_ref):
    size = work_ref.shape[0]
    row = lax.broadcasted_iota(jnp.int32, (size, size), 0)
    column = lax.broadcasted_iota(jnp.int32, (size, size), 1)
    return jnp.where(row >= column, work_ref[:, size:], 0.0)


def rows_dot(left, right):
    return lax.dot_general(left, right, (((1,), (1,)), ((), ())), preferred_element_type=jnp.float32)


def wide_dot(left, right, across=False):
    rows = left.shape[0]
    pieces = split_pieces(left, 3)
    total = None
    for place, part in enumerate(split_pieces(right, 3)):
        used = jnp.concatenate(pieces[: 3 - place], axis=0)
        product = rows_dot(used, part) if across else jnp.dot(used, part, preferred_element_type=jnp.float32)
        for piece in reversed(range(3 - place)):
            term = product[piece * rows : (piece + 1) * rows]
            total = term if total is None else total + term
    return total


def rows_inner(value):
    high, middle, low = split_pieces(value, 3)
    mixed = rows_dot(high, middle) + rows_dot(high, low)
    return rows_dot(high, high) + rows_dot(middle, middle) + (mixed + mixed.T)


def fold_symmetric(value, folded_ref, height):
    half = value.shape[0] // 2
    row = lax.broadcasted_iota(jnp.int32, (half, half), 0)
    column = lax.broadcasted_iota(jnp.int32, (half, half), 1)
    corner = value[half:, half:]
    both = jnp.where(row >= column, value[:half, :half], corner)
    diagonal = jnp.sum(jnp.where(row == column, corner, 0.0), axis=0, keepdims=True)
    quarter = half // 2
    for place in range(4):
        source = value[half:, :half] if place < 2 else both
        folded_ref[place, :quarter] = source[place % 2 * quarter : (place % 2 + 1) * quarter]
        folded_ref[place, quarter:] = jnp.broadcast_to(diagonal, (SUBLANES, half))


def unfold_symmetric(folded, diagonal):
    half = folded.shape[1]
    row = lax.broadcasted_iota(jnp.int32, (half, half), 0)
    column = lax.broadcasted_iota(jnp.int32, (half, half), 1)
    left, both = folded[:half], folded[half:]
    turned = both.T
    corner = jnp.where(row == column, diagonal, jnp.where(row < column, both, turned))
    upper = jnp.concatenate([jnp.where(row >= column, both, turned), left.T], axis=1)
    return jnp.concatenate([upper, jnp.concatenate([left, corner], axis=1)], axis=0)


def diagonal_of(value):
    row = lax.broadcasted_iota(jnp.int32, value.shape, 0)
    column = lax.broadcasted_iota(jnp.int32, value.shape, 1)
    kept = jnp.where(row == column, value, 0.0)
    return jnp.sum(kept, axis=0, keepdims=True), jnp.sum(kept, axis=1, keepdims=True)


def fold_message(folded, diagonal):
    size, half = folded.shape
    row = lax.broadcasted_iota(jnp.int32, (size, 1), 0)
    most = jnp.max(jnp.abs(diagonal), axis=1, keepdims=True)
    peaks = jnp.max(jnp.abs(folded), axis=1, keepdims=True)
    peaks = jnp.where(row == half, jnp.maximum(peaks, most), peaks)
    codes, scales = row_scales(gather_columns([peaks[:half], peaks[half:]]))
    factors = WIDE_STEPS / scales
    lines = codes.T.astype(jnp.int32)
    value = jnp.round(folded * jnp.concatenate([factors[:, :1], factors[:, 1:2]], axis=0)).astype(jnp.int32)
    high = jnp.right_shift(value, NIBBLES)
    rows = [jnp.bitwise_or(jnp.left_shift(high[:half], 16), jnp.bitwise_and(high[half:], 0xFFFF))]
    for first in range(0, size, 8 * SUBLANES):
        extra = jnp.zeros((SUBLANES, half), jnp.int32)
        for group in range(8):
            start = first + group * SUBLANES
            extra = jnp.bitwise_or(
                extra, jnp.left_shift(jnp.bitwise_and(value[start : start + SUBLANES], 15), NIBBLES * group)
            )
        rows.append(extra)
    last = jnp.round(diagonal * (factors[:1, 1:2] * FINER)).astype(jnp.int32)
    code = jnp.bitwise_or(jnp.bitwise_and(lines[0:1], 0xFFFF), jnp.left_shift(lines[1:2], 16))
    sub = lax.broadcasted_iota(jnp.int32, (SUBLANES, half), 0)
    rows.append(jnp.where(sub == 0, code, jnp.where(sub == 1, last, 0)))
    return jnp.concatenate(rows, axis=0)


def sum_folded(messages):
    half = LANES
    lines = []
    for message in messages:
        code = message[half + 32 : half + 33]
        lines += [jnp.right_shift(jnp.left_shift(code, 16), 16), jnp.right_shift(code, 16)]
    lines = [line.astype(jnp.float32) for line in lines]
    lines.append(jnp.zeros((LANES - len(lines), LANES), jnp.float32))
    scales = (jnp.exp2(jnp.concatenate(lines, axis=0) * (1.0 / CODES)) * (1.0 / WIDE_STEPS)).T
    parts, diagonals = [], []
    for place, message in enumerate(messages):
        words = message[:half]
        high = jnp.concatenate([jnp.right_shift(words, 16), jnp.right_shift(jnp.left_shift(words, 16), 16)], axis=0)
        low = []
        for tile in range(4):
            extra = message[half + tile * SUBLANES : half + (tile + 1) * SUBLANES]
            low += [jnp.bitwise_and(jnp.right_shift(extra, NIBBLES * group), 15) for group in range(8)]
        value = jnp.bitwise_or(jnp.left_shift(high, NIBBLES), jnp.concatenate(low, axis=0))
        scale = jnp.concatenate([scales[:, 2 * place : 2 * place + 1], scales[:, 2 * place + 1 : 2 * place + 2]], axis=0)
        parts.append(value.astype(jnp.float32) * scale)
        last = message[half + 33 : half + 34].astype(jnp.float32)
        diagonals.append(last * (scales[:1, 2 * place + 1 : 2 * place + 2] * (1.0 / FINER)))
    return pair_sum(parts), pair_sum(diagonals)


def add_kernel(*refs):
    refs[-1][...] = fold_message(*sum_folded([ref[...] for ref in refs[:-1]]))


def add_messages(messages):
    vmem = pl.BlockSpec(memory_space=pltpu.VMEM)
    return pl.pallas_call(
        add_kernel,
        in_specs=[vmem] * len(messages),
        out_specs=vmem,
        out_shape=jax.ShapeDtypeStruct(messages[0].shape, messages[0].dtype),
        compiler_params=pltpu.CompilerParams(vmem_limit_bytes=VMEM_SMALL),
    )(*messages)


def sum_messages(message, groups, beside):
    stages = stage_bits(groups)
    steps, state = list(beside), None
    for depth, bits in enumerate(reversed(stages)):
        if depth > 0:
            message = add_messages(messages)
        messages = [message] + [exchange(message, groups, span) for span in offsets(bits)[1:]]
        if steps:
            state = steps.pop(0)(state)
        if depth + 1 < len(stages):
            messages, state = lax.optimization_barrier((messages, state))
    for step in steps:
        state = step(state)
    return messages, state


def project_kernel(order, sources, coded, quarter_ref, place_ref, rows_ref, *refs):
    refs, (inner_ref, *outs), (full_ref, folded_ref) = refs[:sources], refs[sources:-2], refs[-2:]
    size = full_ref.shape[0]
    load_all(order, place_ref, refs, full_ref)
    image = full_ref[...]
    inner = rows_inner(image)
    inner_ref[...] = inner
    split = jnp.concatenate(split_pieces(image, PIECES), axis=0)
    sampled = rows_dot(split, rows_ref[...])
    sampled = sum(sampled[piece * size : (piece + 1) * size] for piece in range(PIECES))
    high, low = split_pieces(sampled, PIECES)
    mixed = rows_dot(high, low)
    cross = rows_dot(high, high) + (mixed + mixed.T)
    across, down = diagonal_of(inner)
    fold_symmetric(cross * (lax.rsqrt(down) * lax.rsqrt(across)), folded_ref, size)
    if coded:
        quarter = size // 4
        folded = jnp.concatenate([folded_ref[place, :quarter] for place in range(4)], axis=0)
        outs[0][...] = fold_message(folded, folded_ref[0, quarter : quarter + 1])
        return
    for offset, out_ref in enumerate(outs):
        out_ref[...] = folded_ref[jnp.bitwise_xor(quarter_ref[0], offset)]


def project(genotypes, quarter, place, gathered, order, size):
    samples, cap = genotypes.shape
    scalar, vmem = pl.BlockSpec(memory_space=pltpu.SMEM), pl.BlockSpec(memory_space=pltpu.VMEM)
    part = (size // 4 + SUBLANES, size // 2)
    coded = size == TILES * LANES
    outs = [jax.ShapeDtypeStruct((size, size), jnp.float32)]
    if coded:
        outs += [jax.ShapeDtypeStruct((WIDE, LANES), jnp.int32)]
    else:
        outs += [jax.ShapeDtypeStruct(part, jnp.float32)] * 4
    return pl.pallas_call(
        functools.partial(project_kernel, order, len(gathered), coded),
        in_specs=[scalar, scalar, vmem] + [vmem] * len(gathered),
        out_specs=[vmem] * len(outs),
        out_shape=outs,
        scratch_shapes=[
            pltpu.VMEM((size, cap), jnp.float32),
            pltpu.VMEM((4,) + part, jnp.float32),
        ],
        compiler_params=pltpu.CompilerParams(vmem_limit_bytes=VMEM_LIMIT),
    )(quarter, place, genotypes, *gathered)


def second_kernel(first, last, source_ref, work_ref):
    if first == 0:
        start_factor(work_ref, source_ref[...])
    else:
        work_ref[...] = source_ref[...]
    inverse_factor(work_ref, work_ref.shape[0], PANEL, first, last)


def second_factor(source, first, last):
    size = source.shape[0]
    vmem = pl.BlockSpec(memory_space=pltpu.VMEM)
    return pl.pallas_call(
        functools.partial(second_kernel, first, last),
        in_specs=[vmem],
        out_specs=vmem,
        out_shape=jax.ShapeDtypeStruct((size, 2 * size), jnp.float32),
        compiler_params=pltpu.CompilerParams(vmem_limit_bytes=VMEM_LIMIT),
        cost_estimate=FACTOR_COST,
    )(source)


def basis_kernel(gain, factor_ref, own_ref, out_ref):
    own = wide_dot(finish_factor(factor_ref), own_ref[...])
    out_ref[...] = own.T * gain


def basis_rows(factor, own, gain):
    vmem = pl.BlockSpec(memory_space=pltpu.VMEM)
    return pl.pallas_call(
        functools.partial(basis_kernel, gain),
        in_specs=[vmem] * 2,
        out_specs=vmem,
        out_shape=jax.ShapeDtypeStruct(own.shape[::-1], jnp.float32),
        compiler_params=pltpu.CompilerParams(vmem_limit_bytes=VMEM_SMALL),
        cost_estimate=pl.CostEstimate(flops=1_000_000_000, bytes_accessed=1 << 20, transcendentals=0),
    )(factor, own)


def trace_kernel(scale, quarter_ref, factor_ref, inner_ref, *refs):
    parts, (half_ref, trace_ref, folded_ref) = refs[:-3], refs[-3:]
    if parts[0].dtype == jnp.int32:
        folded, diagonal = sum_folded([part[...] for part in parts])
    else:
        for offset in range(4):
            folded_ref[jnp.bitwise_xor(quarter_ref[0], offset)] = parts[offset][...]
        quarter = folded_ref.shape[1] - SUBLANES
        folded = jnp.concatenate([folded_ref[place, :quarter] for place in range(4)], axis=0)
        diagonal = folded_ref[3, quarter : quarter + 1]
    across, down = diagonal_of(inner_ref[...])
    cross = unfold_symmetric(folded, diagonal) * ((down * lax.rsqrt(down)) * (across * lax.rsqrt(across)))
    factor = finish_factor(factor_ref)
    half = scale * wide_dot(factor, cross)
    half_ref[...] = half
    trace_ref[...] = jnp.broadcast_to(jnp.sum(half * factor), trace_ref.shape)


def trace_half(quarter, factor, inner, parts, scale):
    vmem = pl.BlockSpec(memory_space=pltpu.VMEM)
    return pl.pallas_call(
        functools.partial(trace_kernel, scale),
        in_specs=[pl.BlockSpec(memory_space=pltpu.SMEM)] + [vmem] * (2 + len(parts)),
        out_specs=[vmem] * 2,
        out_shape=[
            jax.ShapeDtypeStruct(inner.shape, jnp.float32),
            jax.ShapeDtypeStruct((SUBLANES, LANES), jnp.float32),
        ],
        scratch_shapes=[pltpu.VMEM((4,) + parts[0].shape, parts[0].dtype)],
        compiler_params=pltpu.CompilerParams(vmem_limit_bytes=VMEM_SMALL),
    )(quarter, factor, inner, *parts)


def finish_kernel(gain, half_ref, factor_ref, *refs):
    traces, out_ref = refs[:-1], refs[-1]
    total = sum(trace[:1, :1] for trace in traces)
    whole = wide_dot(half_ref[...], finish_factor(factor_ref), across=True)
    out_ref[...] = whole * (gain / total)


def finish(half, factor, traces, gain):
    vmem = pl.BlockSpec(memory_space=pltpu.VMEM)
    return pl.pallas_call(
        functools.partial(finish_kernel, gain),
        in_specs=[vmem] * (2 + len(traces)),
        out_specs=vmem,
        out_shape=jax.ShapeDtypeStruct(half.shape, jnp.float32),
        compiler_params=pltpu.CompilerParams(vmem_limit_bytes=VMEM_SMALL),
    )(half, factor, *traces)


def to_natural(gathered, order, me):
    places = jnp.argsort(jnp.array(order, jnp.int32))
    mine = jnp.bitwise_xor(jnp.arange(len(order), dtype=jnp.int32), me)
    stacked = jnp.concatenate(gathered, axis=0)[places][mine]
    return jnp.transpose(stacked, (1, 0, 2)).reshape(stacked.shape[1], -1)


def to_relative(rows, order, me, width, parts):
    chunks = jnp.transpose(rows.reshape(rows.shape[0], -1, width), (1, 0, 2))
    return jnp.split(chunks[jnp.bitwise_xor(jnp.array(order, jnp.int32), me)], parts, axis=0)


def body(genotypes, sizes, start):
    groups = lax.axis_size("smp")
    dosages = genotypes[0]
    samples, cap = dosages.shape
    width, size = start.shape[1:]
    scale = 1.0 / (samples * groups)
    me = lax.axis_index("smp")
    place = me.reshape(1).astype(jnp.int32)
    stages = stage_bits(groups)
    order = relative_order(stages)
    packed = width == LANES and size == TILES * LANES

    def gather(message):
        gathered = gather_chunks(message, groups)
        return gathered if packed else [to_natural(gathered, order, me)]

    def apply(message, normalise):
        outs = apply_samples(dosages, sizes, place, gather(message), order, normalise, scale)
        if not packed:
            outs = to_relative(outs[0], order, me, width, len(offsets(stages[0])))
        return reduce_chunks(outs[0], outs[1:], groups, packed)

    if packed:
        message = encode(place, sizes, start[0])
    else:
        row = me * width + lax.broadcasted_iota(jnp.int32, (width, size), 0)
        message = jnp.where(row < sizes[0], start[0], 0.0).T[None]
    dosages = hold(dosages, message)
    _, message = apply(message, False)
    own, message = apply(message, True)
    quarter = jnp.bitwise_and(place, 3)
    inner, *parts = project(dosages, quarter, place, gather(message), order, size)
    if len(parts) == 1:
        cut = size // 2
        beside = [lambda _: second_factor(inner, 0, cut), lambda work: second_factor(work, cut, size)]
        parts, second = sum_messages(parts[0], groups, beside)
    else:
        cuts = [0, size // 4 + size // 8, size - size // 4, size]
        beside = [
            lambda _: second_factor(inner, cuts[0], cuts[1]),
            lambda work: second_factor(work, cuts[1], cuts[2]),
            lambda work: second_factor(work, cuts[2], cuts[3]),
        ]
        parts, second = sum_quarters(parts, groups, beside)
    halfway, trace = trace_half(quarter, second, inner, parts, scale)
    blocks = lax.axis_size("blk")
    traces = [trace] + [
        lax.ppermute(trace, "blk", [(block, (block + shift) % blocks) for block in range(blocks)])
        for shift in range(1, blocks)
    ]
    basis = basis_rows(second, own[0], math.sqrt(cap))
    scaled = finish(halfway, second, traces, float(genotypes.shape[0] * blocks * size))
    return basis[None], scaled[None]


def solution(mesh):
    return jax.shard_map(
        body,
        mesh=mesh,
        in_specs=(P("blk", "smp", None), P("blk"), P("blk", "smp", None)),
        out_specs=(P("blk", "smp", None), P("blk", None, None)),
        check_vma=False,
    )
```
